128 devices in a mesh: seq: 16 (over z, x), vis: 8 (over y, core).
Axes of the slice: x: 4, y: 4, z: 4, core: 2. Of those that a mesh axis runs over, the one named last changes fastest.
Arguments:
- query: bfloat16 [5120, 4096], P('seq', 'vis'), may hold values from -15 to 15
- key: bfloat16 [5120, 4096], P('seq', 'vis'), may hold values from -15 to 15
- value: bfloat16 [5120, 4096], P('seq', 'vis'), may hold values from -6 to 6
- doc_ids: int32 [5120], P('seq'), may hold values from 0 to 3, never falling along the last dimension, each value on 1 to 2560 neighbouring positions
- cross_query: bfloat16 [5120, 4096], P('seq', 'vis'), may hold values from -15 to 15
- latent_key: bfloat16 [8, 64, 4096], P('vis'), may hold values from -15 to 15
- latent_value: bfloat16 [8, 64, 4096], P('vis'), may hold values from -6 to 6
- token_slot: int32 [5120], P('seq'), may hold values from 0 to 4, as said below
- slot_image: int32 [64], P('seq'), may hold values from 0 to 7, as said below
- cross_gate: float32 [4096], P('vis'), may hold values from -1.5 to 1.5
- out_grad: bfloat16 [5120, 4096], P('seq', 'vis'), may hold values from -6 to 6
Outputs:
- mixed: bfloat16 [5120, 4096], P('seq', 'vis')
- query_grad: float32 [5120, 4096], P('seq', 'vis')
- key_grad: float32 [5120, 4096], P('seq', 'vis')
- value_grad: float32 [5120, 4096], P('seq', 'vis')
- cross_query_grad: float32 [5120, 4096], P('seq', 'vis')
- latent_key_grad: float32 [8, 64, 4096], P('vis', None, 'seq')
- latent_value_grad: float32 [8, 64, 4096], P('vis', None, 'seq')
The draws below stay inside these ranges and needn't reach their ends.
Inputs may be any that keep to these rules, and one draw needn't show every extreme that they name: `token_slot`: within each text shard of 320 tokens the values after the leading 4s never fall; 4 marks the tokens before the shard's first image, which see no image. `slot_image`: the images of one shard's slots need not differ; image m is held by index m of vis.
All inputs are finite; a program needn't handle non-finite values.
Results may differ from the reference program's by a relative error of at most 0.03.
Values may be sent and summed in bfloat16 or wider, within the bound.
A program may use at most 192 MiB of HBM per device.

```python
import math
import jax
import jax.numpy as jnp
import numpy as np
from jax import lax

HEADS = 32
HEAD_DIM = 128
LATENTS = 64
SLOTS = 4
DOCS = 4
TOK_DEV = 320
TOKENS = 5120
IMAGES = 8
WIDTH = 4096


def draw_query(key, part):
    own_key = jax.random.fold_in(key, 1)
    base_draw = jnp.clip(jax.random.normal(own_key, (TOKENS, WIDTH), jnp.float32), -4.0, 4.0)
    return base_draw.astype(jnp.bfloat16)


def draw_key(key, part):
    own_key = jax.random.fold_in(key, 2)
    base_draw = jnp.clip(jax.random.normal(own_key, (TOKENS, WIDTH), jnp.float32), -4.0, 4.0)
    return base_draw.astype(jnp.bfloat16)


def draw_cross_query(key, part):
    own_key = jax.random.fold_in(key, 3)
    base_draw = jnp.clip(jax.random.normal(own_key, (TOKENS, WIDTH), jnp.float32), -4.0, 4.0)
    return base_draw.astype(jnp.bfloat16)


def draw_latent_key(key, part):
    own_key = jax.random.fold_in(key, 4)
    base_draw = jnp.clip(jax.random.normal(own_key, (IMAGES, LATENTS, WIDTH), jnp.float32), -4.0, 4.0)
    return base_draw.astype(jnp.bfloat16)


def draw_token_slot(key, part):
    own_key = jax.random.fold_in(key, 5)
    shard_count = TOKENS // TOK_DEV
    span = TOK_DEV // SLOTS
    jitter = jax.random.randint(own_key, (shard_count, SLOTS), 1, span // 2 + 1)
    starts = jnp.arange(SLOTS, dtype=jnp.int32)[None, :] * span + jitter
    local_rows = jnp.arange(TOK_DEV, dtype=jnp.int32)
    counted = jnp.sum((local_rows[None, :, None] >= starts[:, None, :]).astype(jnp.int32), axis=2)
    slot_value = jnp.where(counted == 0, SLOTS, counted - 1)
    return slot_value.reshape(TOKENS).astype(jnp.int32)


def draw_slot_image(key, part):
    own_key = jax.random.fold_in(key, 6)
    shard_count = TOKENS // TOK_DEV
    base_image = jnp.arange(shard_count, dtype=jnp.int32) * IMAGES // shard_count
    jitter = jax.random.randint(own_key, (shard_count, SLOTS), 0, 2)
    images = (base_image[:, None] + jnp.arange(SLOTS, dtype=jnp.int32)[None, :] + jitter) % IMAGES
    return images.reshape(shard_count * SLOTS).astype(jnp.int32)


def block_scale(key, dims, pieces, least, high):
    factor_of, own = 1.0, jax.random.fold_in(key, 6)
    for position, parts in pieces:
        heights = jnp.exp(jax.random.uniform(jax.random.fold_in(own, position), (parts,), jnp.float32, least / len(pieces), high / len(pieces)))
        factor_of = factor_of * jnp.repeat(heights, dims[position] // parts).reshape([-1 if axis == position else 1 for axis in range(len(dims))])
    return factor_of


def profile(count, total, limit, skew):
    loads = [(1 << 20) // math.isqrt(rank ** skew) + 1 for rank in range(2, count + 1)]
    rest, counts = total - limit - (count - 1), [1] * (count - 1)
    while rest > 0:
        free = [i for i in range(count - 1) if counts[i] < limit]
        pool, remaining = sum([loads[i] for i in free]), rest
        for i in free:
            extra = min(limit - counts[i], max(1, remaining * loads[i] // pool), rest)
            counts[i] = counts[i] + extra
            rest = rest - extra
    return np.array([limit] + counts)


def uneven_parts(key, number_of, total, bound, slope):
    if number_of == 2:
        one = jax.random.randint(key, (), max(1, total - bound), min(bound, total - 1) + 1)
        return jnp.stack([one, total - one])
    tallies = jnp.asarray(profile(number_of, total, bound, slope), jnp.int32)
    pairs = (number_of - 1) // 2
    giver, sink = tallies[1:1 + 2 * pairs:2], tallies[2:2 + 2 * pairs:2]
    slack = jnp.minimum(giver - 1, bound - sink)
    passed = jax.random.randint(jax.random.fold_in(key, 1), (pairs,), 0, 1 << 20) % (slack + 1)
    tallies = tallies.at[1:1 + 2 * pairs:2].set(giver - passed).at[2:2 + 2 * pairs:2].set(sink + passed)
    return tallies[jax.random.permutation(jax.random.fold_in(key, 2), number_of)]


def noise(rng, dims, deviation, most, cuts=(), held_as=jnp.bfloat16):
    drawn = deviation * jax.random.normal(rng, dims, jnp.float32)
    if cuts:
        drawn = drawn * block_scale(rng, dims, cuts, -0.22, 0.18)
    return jnp.clip(drawn, -most, most).astype(held_as)


def setup_inputs(seed: int = 0) -> dict:
    streams_of = jax.random.split(jax.random.key(seed), 12)
    query = draw_query(jax.random.fold_in(streams_of[11], 71), 0)
    key = draw_key(jax.random.fold_in(streams_of[11], 71), 0)
    value = noise(streams_of[2], (TOKENS, WIDTH), 1.0, 6.0, ((0, 16), (1, 8)))
    doc_ids = jnp.searchsorted(jnp.cumsum(uneven_parts(streams_of[3], DOCS, TOKENS, TOKENS // 2, 0)), jnp.arange(TOKENS), side="right").astype(jnp.int32)
    cross_query = draw_cross_query(jax.random.fold_in(streams_of[11], 71), 0)
    latent_key = draw_latent_key(jax.random.fold_in(streams_of[11], 71), 0)
    latent_value = noise(streams_of[6], (IMAGES, LATENTS, WIDTH), 1.0, 6.0, ((0, 8),))
    token_slot = draw_token_slot(jax.random.fold_in(streams_of[11], 71), 0)
    slot_image = draw_slot_image(jax.random.fold_in(streams_of[11], 71), 0)
    cross_gate = jnp.clip(jax.random.uniform(streams_of[9], (WIDTH,), jnp.float32, -1.5, 1.5) * block_scale(streams_of[9], (WIDTH,), ((0, 8),), -0.4, 0.0), -1.5, 1.5)
    out_grad = noise(streams_of[10], (TOKENS, WIDTH), 1.0, 6.0, ((0, 16), (1, 8)))
    return dict(query=query, key=key, value=value, doc_ids=doc_ids, cross_query=cross_query, latent_key=latent_key, latent_value=latent_value, token_slot=token_slot, slot_image=slot_image, cross_gate=cross_gate, out_grad=out_grad)


big_negative = -1e+30

def softmax_rows(scores, allowed):
    masked = jnp.where(allowed, scores, big_negative)
    row_max = lax.optimization_barrier(jnp.max(masked, axis=-1, keepdims=True))
    weights = jnp.where(allowed, jnp.exp(masked - row_max), 0.0)
    return (weights, lax.optimization_barrier(jnp.sum(weights, axis=-1, keepdims=True)))

def reference(query, key, value, doc_ids, cross_query, latent_key, latent_value, token_slot, slot_image, cross_gate, out_grad):
    score_scale = 1.0 / math.sqrt(HEAD_DIM)
    positions = jnp.arange(TOKENS, dtype=jnp.int32)
    allowed = (positions[None, :] <= positions[:, None]) & (doc_ids[None, :] == doc_ids[:, None])

    def by_heads(matrix):
        return matrix.reshape(TOKENS, HEADS, HEAD_DIM).transpose(1, 0, 2)

    def merged(stacked):
        return stacked.transpose(1, 0, 2).reshape(TOKENS, HEADS * HEAD_DIM)

    def self_head(operands):
        query_head, key_head, value_head, grad_head = operands
        scores = jnp.dot(query_head, key_head.T, preferred_element_type=jnp.float32) * score_scale
        weights, row_sum = softmax_rows(scores, allowed)
        probs = weights / row_sum
        probs_low = probs.astype(jnp.bfloat16)
        self_out = jnp.dot(probs_low, value_head, preferred_element_type=jnp.float32)
        row_dot = lax.optimization_barrier(jnp.sum(grad_head.astype(jnp.float32) * self_out, axis=1, keepdims=True))
        grad_probs = jnp.dot(grad_head, value_head.T, preferred_element_type=jnp.float32)
        grad_scores = (probs * (grad_probs - row_dot) * score_scale).astype(jnp.bfloat16)
        head_query_grad = jnp.dot(grad_scores, key_head, preferred_element_type=jnp.float32)
        head_key_grad = jnp.dot(grad_scores.T, query_head, preferred_element_type=jnp.float32)
        head_value_grad = jnp.dot(probs_low.T, grad_head, preferred_element_type=jnp.float32)
        return (self_out, head_query_grad, head_key_grad, head_value_grad)
    results = lax.map(self_head, (by_heads(query), by_heads(key), by_heads(value), by_heads(out_grad)))
    self_out, query_grad, key_grad, value_grad = [merged(stacked) for stacked in results]
    shard_count = TOKENS // TOK_DEV
    width = HEADS * HEAD_DIM
    gate_tanh = jnp.tanh(cross_gate)
    column_slot = jnp.arange(SLOTS * LATENTS, dtype=jnp.int32) // LATENTS

    def cross_shard(operands):
        cross_rows, grad_rows, slot_rows, images, self_rows = operands
        slot_keys = jnp.take(latent_key, images, axis=0).reshape(SLOTS * LATENTS, HEADS, HEAD_DIM).astype(jnp.float32)
        slot_values = jnp.take(latent_value, images, axis=0).reshape(SLOTS * LATENTS, HEADS, HEAD_DIM).astype(jnp.float32)
        queries = cross_rows.reshape(TOK_DEV, HEADS, HEAD_DIM).astype(jnp.float32)
        scores = jnp.einsum('ihd,jhd->hij', queries, slot_keys) * score_scale
        allowed_cross = (column_slot[None, :] == slot_rows[:, None])[None]
        has_image = (slot_rows < SLOTS)[None, :, None]
        weights, row_sum = softmax_rows(scores, allowed_cross)
        probs = weights / jnp.where(has_image, row_sum, 1.0)
        probs_low = lax.optimization_barrier(probs.astype(jnp.bfloat16)).astype(jnp.float32)
        cross_out = jnp.einsum('hij,jhd->ihd', probs_low, slot_values).reshape(TOK_DEV, width)
        mixed_rows = (self_rows + gate_tanh[None, :] * cross_out).astype(jnp.bfloat16)
        cross_back = lax.optimization_barrier((gate_tanh[None, :] * grad_rows.astype(jnp.float32)).astype(jnp.bfloat16)).astype(jnp.float32)
        back_heads = cross_back.reshape(TOK_DEV, HEADS, HEAD_DIM)
        cross_dot = lax.optimization_barrier(jnp.sum((cross_back * cross_out).reshape(TOK_DEV, HEADS, HEAD_DIM), axis=2)).T[:, :, None]
        grad_probs = jnp.einsum('ihd,jhd->hij', back_heads, slot_values)
        grad_scores = lax.optimization_barrier((probs * (grad_probs - cross_dot) * score_scale).astype(jnp.bfloat16)).astype(jnp.float32)
        cross_grad = jnp.einsum('hij,jhd->ihd', grad_scores, slot_keys).reshape(TOK_DEV, width)
        key_slots = jnp.einsum('hij,ihd->jhd', grad_scores, queries).reshape(SLOTS, LATENTS, width).astype(jnp.bfloat16)
        value_slots = jnp.einsum('hij,ihd->jhd', probs_low, back_heads).reshape(SLOTS, LATENTS, width).astype(jnp.bfloat16)
        return (mixed_rows, cross_grad, key_slots, value_slots)
    mixed, cross_query_grad, key_slots, value_slots = lax.map(cross_shard, (cross_query.reshape(shard_count, TOK_DEV, width), out_grad.reshape(shard_count, TOK_DEV, width), token_slot.reshape(shard_count, TOK_DEV), slot_image.reshape(shard_count, SLOTS), self_out.reshape(shard_count, TOK_DEV, width)))
    mixed = mixed.reshape(TOKENS, width)
    cross_query_grad = cross_query_grad.reshape(TOKENS, width)
    latent_key_grad = jax.ops.segment_sum(key_slots.reshape(shard_count * SLOTS, LATENTS, width).astype(jnp.float32), slot_image, num_segments=IMAGES)
    latent_value_grad = jax.ops.segment_sum(value_slots.reshape(shard_count * SLOTS, LATENTS, width).astype(jnp.float32), slot_image, num_segments=IMAGES)
    return (mixed, query_grad, key_grad, value_grad, cross_query_grad, latent_key_grad, latent_value_grad)
```

```python
import functools
import math

import jax
import jax.numpy as jnp
from jax import lax
from jax.experimental import pallas as pl
from jax.experimental.pallas import tpu as pltpu
from jax.sharding import PartitionSpec as P

HD = 128
TD = 320
NX = 4
CH = TD * NX
NC = 3
TILE = 256
NQ = CH // TILE
NK = 2 * NQ + 1
LAT = 64
SLOTS = 4
IMAGES = 8
WD = 512
SCALE = 1.0 / math.sqrt(HD)
BIG = -1e30
MESH = pl.DeviceIdType.MESH
F32, BF16, I32 = jnp.float32, jnp.bfloat16, jnp.int32

NT = (((1,), (1,)), ((), ()))
NN = (((1,), (0,)), ((), ()))


def dot(a, b, dims=NN):
    return lax.dot_general(a, b, dims, preferred_element_type=F32)


def fold(a, op):
    return op(a.reshape(a.shape[0] // 8, 8, a.shape[1]), axis=0)


def kernel(
    docs_ref, tok_ref, img_ref, gate_ref, q_ref, k_ref, v_ref, cq_ref, do_ref, lk_ref, lv_ref,
    mixed_ref, qg_ref, kg_ref, vg_ref, cqg_ref, lkg_ref, lvg_ref,
    kbuf, vbuf, qbuf, dobuf, dol, kt, vt, sbuf, pbuf, maxes, dvec, starts, dqt,
    cown, cx, crow, cz,
    latk, latv, lks, lvs, gk, gv, cross, latsend, latrecv,
    obuf, dqb, part_k, part_v, own_k, own_v, got_k, got_v, sum_k, sum_v,
    o_in, dq_in, dk_in, dv_in,
    a_send, a_recv, z_send, z_recv, c_send, c_recv, l_send, l_recv, g_send, g_recv,
    p_send, p_recv, b_send, b_recv,
):
    s = lax.axis_index("seq")
    v = lax.axis_index("vis")
    x = lax.rem(s, NX)
    z = lax.div(s, NX)

    def xpeer(d):
        return lax.rem(x + d, NX)

    def remote(src, dst, ssem, rsem, seq, vis):
        return pltpu.make_async_remote_copy(
            src_ref=src, dst_ref=dst, send_sem=ssem, recv_sem=rsem,
            device_id=(seq, vis), device_id_type=MESH,
        )

    def rows(i, n=TD):
        return pl.ds(pl.multiple_of(i * n, n), n)

    def cols(i, n=HD):
        return pl.ds(pl.multiple_of(i * n, n), n)

    barrier = pltpu.get_barrier_semaphore()

    def greet(seq, vis):
        pl.semaphore_signal(barrier, inc=1, device_id=(seq, vis), device_id_type=MESH)

    for d in range(1, NX):
        greet(z * NX + xpeer(d), v)
        greet(lax.rem(z + d, NX) * NX + x, v)
    for d in range(1, IMAGES):
        greet(s, lax.rem(v + d, IMAGES))
    half = lax.rem(s, 2)
    head_group = lax.div(s, 2)
    own_piece = head_group == v
    for i in range(16):
        @pl.when(jnp.logical_not(jnp.logical_and(s == i, own_piece)))
        def _():
            greet(jnp.int32(i), head_group)
    pl.semaphore_wait(barrier, 13 + 16 - jnp.where(own_piece, 1, 0))

    docs = docs_ref[...]
    row_id = lax.broadcasted_iota(I32, (8, HD), 0)
    counts = jnp.zeros((8, HD), F32)
    for d in range(1, 4):
        c = jnp.sum(jnp.where(docs < d, 1.0, 0.0), axis=1, keepdims=True)
        counts = jnp.where(row_id == d, c, counts)
    cown[...] = counts

    ins = (k_ref, v_ref, q_ref, do_ref)
    bufs = (kbuf, vbuf, qbuf, dobuf)
    base = (2 * CH, 2 * CH, 0, 0)

    def a_copy(arr, d):
        p = xpeer(d)
        return remote(
            ins[arr].at[:, cols(p)],
            bufs[arr].at[pl.ds(pl.multiple_of(base[arr] + x * TD, TD), TD), :],
            a_send.at[arr, d - 1], a_recv.at[arr, d - 1], z * NX + p, v,
        )

    def a_wait(arr, d):
        p = lax.rem(x + NX - d, NX)
        here = bufs[arr].at[pl.ds(pl.multiple_of(base[arr] + p * TD, TD), TD), :]
        remote(here, here, a_send.at[arr, d - 1], a_recv.at[arr, d - 1], s, v).wait_recv()

    def c_copy(stage, d):
        if stage == 0:
            return remote(cown, cx.at[d - 1], c_send.at[0, d - 1], c_recv.at[0, d - 1],
                          z * NX + xpeer(d), v)
        return remote(crow, cz.at[d - 1], c_send.at[1, d - 1], c_recv.at[1, d - 1],
                      lax.rem(z + d, NX) * NX + x, v)

    def z_copy(arr, dz, d):
        p = lax.rem(x + NX - d, NX)
        src = bufs[arr].at[pl.ds(pl.multiple_of(2 * CH + p * TD, TD), TD), :]
        dst = bufs[arr].at[pl.ds(pl.multiple_of((2 - dz) * CH + p * TD, TD), TD), :]
        return remote(src, dst, z_send.at[arr, dz - 1, d], z_recv.at[arr, dz - 1, d], s + dz * NX, v)

    def z_start(arr, d):
        for dz in (1, 2):
            @pl.when(z + dz < NX)
            def _():
                z_copy(arr, dz, d).start()

    def z_wait(arr, dz):
        for d in range(NX):
            p = lax.rem(x + NX - d, NX)
            here = bufs[arr].at[pl.ds(pl.multiple_of((2 - dz) * CH + p * TD, TD), TD), :]
            remote(here, here, z_send.at[arr, dz - 1, d], z_recv.at[arr, dz - 1, d], s, v).wait_recv()

    for arr in (0, 1):
        for d in (1, 3, 2):
            a_copy(arr, d).start()
    for d in (1, 3, 2):
        c_copy(0, d).start()
    for arr in range(4):
        bufs[arr][pl.ds(pl.multiple_of(base[arr] + x * TD, TD), TD), :] = ins[arr][:, cols(x)]
    for arr in (0, 1):
        z_start(arr, 0)
    for arr in (2, 3):
        for d in (1, 3, 2):
            a_copy(arr, d).start()

    lins, lbufs = (lk_ref, lv_ref), (latk, latv)

    def l_copy(arr, d):
        p = lax.rem(v + d, IMAGES)
        return remote(lins[arr].at[0, :, cols(p, WD)], lbufs[arr].at[v],
                      l_send.at[arr, d - 1], l_recv.at[arr, d - 1], s, p)

    for arr in (0, 1):
        for d in range(1, IMAGES):
            l_copy(arr, d).start()
        lbufs[arr][v] = lins[arr][0, :, cols(v, WD)]

    for arr in (0, 1):
        for d in (1, 3, 2):
            a_wait(arr, d)
            z_start(arr, d)

    for d in range(1, NX):
        here = cx.at[d - 1]
        remote(here, here, c_send.at[0, d - 1], c_recv.at[0, d - 1], s, v).wait_recv()
    crow[...] = cown[...] + cx[0] + cx[1] + cx[2]
    for d in range(1, NX):
        c_copy(1, d).start()
    for d in (1, 3, 2):
        a_wait(2, d)
    for d in range(1, NX):
        here = cz.at[d - 1]
        remote(here, here, c_send.at[1, d - 1], c_recv.at[1, d - 1], s, v).wait_recv()
    before = crow[...] + cz[0] + cz[1] + cz[2]
    pos = lax.broadcasted_iota(I32, (8, CH), 1)
    start = jnp.zeros((8, CH), I32)
    for d in range(1, 4):
        b = before[d:d + 1, 0:1].astype(I32)
        start = jnp.where(b <= pos + z * CH, b, start)
    starts[...] = start - (z - 2) * CH

    maxes[...] = jnp.full_like(maxes, BIG)
    key_iota = lax.broadcasted_iota(I32, (TILE, TILE), 0)
    query_iota = lax.broadcasted_iota(I32, (TILE, TILE), 1)

    def tile(i):
        return pl.ds(pl.multiple_of(i * TILE, TILE), TILE)

    def score_chunk(slot):
        def per_query(t, _):
            first = starts[0:1, tile(t)]
            qt = qbuf[tile(t), :]

            def per_key(c, _):
                raw = dot(kbuf[tile(c), :], qt, NT)
                kpos = key_iota + c * TILE
                kept = (kpos >= first) & (kpos <= query_iota + (2 * CH + t * TILE))
                raw = jnp.where(kept, raw, BIG)
                sbuf[t, tile(c - t), :] = raw
                maxes[:, tile(t)] = jnp.maximum(maxes[:, tile(t)], fold(raw, jnp.max))
                return 0

            lo = jnp.maximum(t, slot * NQ)
            hi = jnp.minimum(t + NK, (slot + 1) * NQ)
            return lax.fori_loop(lo, hi, per_key, 0)

        lax.fori_loop(0, NQ, per_query, 0)

    def flip(src, dst, slot):
        def step(c, _):
            dst[:, tile(c)] = src[tile(c), :].astype(F32).T.astype(BF16)
            return 0

        lax.fori_loop(slot * NQ, (slot + 1) * NQ, step, 0)

    score_chunk(2)
    flip(kbuf, kt, 2)
    flip(vbuf, vt, 2)

    for arr in (0, 1):
        for d in range(1, IMAGES):
            here = lbufs[arr].at[lax.rem(v + IMAGES - d, IMAGES)]
            remote(here, here, l_send.at[arr, d - 1], l_recv.at[arr, d - 1], s, v).wait_recv()
    for i in range(SLOTS):
        lks[i * LAT:(i + 1) * LAT, :] = latk[img_ref[i]]
        lvs[i * LAT:(i + 1) * LAT, :] = latv[img_ref[i]]
    slot_of = lax.broadcasted_iota(I32, (SLOTS * LAT, TD), 0) // LAT
    seen = slot_of == tok_ref[...]
    any_image = tok_ref[...] < SLOTS
    gate = jnp.tanh(gate_ref[...])
    for h in range(NX):
        sl = slice(h * HD, (h + 1) * HD)
        lkh, lvh, cqh = lks[:, sl], lvs[:, sl], cq_ref[:, sl]
        raw = dot(lkh, cqh, NT)
        raw = jnp.where(seen, raw * SCALE, BIG)
        w = jnp.where(seen, jnp.exp(raw - jnp.max(raw, axis=0, keepdims=True)), 0.0)
        total = jnp.where(any_image, jnp.sum(w, axis=0, keepdims=True), 1.0)
        probs = w / total
        low = probs.astype(BF16)
        out = dot(lvh.astype(F32).T.astype(BF16), low).T
        cross[:, sl] = gate[:, sl] * out
        back = (gate[:, sl] * do_ref[:, sl].astype(F32)).astype(BF16)
        gp = dot(lvh, back, NT)
        cdot = jnp.sum(probs * gp, axis=0, keepdims=True)
        ds = (probs * (gp - cdot) * SCALE).astype(BF16)
        cqg_ref[:, sl] = dot(lkh.astype(F32).T.astype(BF16), ds).T
        gk[:, sl] = dot(ds, cqh).astype(BF16).astype(F32)
        gv[:, sl] = dot(low, back).astype(BF16).astype(F32)

    for m in range(IMAGES):
        for n, g in enumerate((gk, gv)):
            acc = jnp.zeros((LAT, WD), F32)
            for i in range(SLOTS):
                acc = acc + jnp.where(img_ref[i] == m, 1.0, 0.0) * g[i * LAT:(i + 1) * LAT, :]
            acc = acc.astype(BF16)
            latsend[m, 0, n] = acc[:, 0:256]
            latsend[m, 1, n] = acc[:, 256:512]

    def g_copy(m, h):
        return remote(latsend.at[m, h], latrecv.at[s], g_send.at[m, h], g_recv.at[s], 2 * v + h,
                      jnp.int32(m))

    def g_mine(m, h):
        return jnp.logical_and(s == 2 * v + h, v == m)

    for m in range(IMAGES):
        for h in range(2):
            @pl.when(jnp.logical_not(g_mine(m, h)))
            def _():
                g_copy(m, h).start()

    @pl.when(own_piece)
    def _():
        latrecv[s] = latsend[v, half]

    @pl.when(z >= 1)
    def _():
        z_wait(0, 1)
        score_chunk(1)
        flip(kbuf, kt, 1)

    @pl.when(z >= 2)
    def _():
        z_wait(0, 2)
        score_chunk(0)
        flip(kbuf, kt, 0)

    @pl.when(z >= 1)
    def _():
        z_wait(1, 1)
        flip(vbuf, vt, 1)

    @pl.when(z >= 2)
    def _():
        z_wait(1, 2)
        flip(vbuf, vt, 0)

    for d in (1, 3, 2):
        a_wait(3, d)

    low_tile = (2 - jnp.minimum(z, 2)) * NQ

    def forward(t, _):
        top = jnp.max(maxes[:, tile(t)], axis=0, keepdims=True)

        def per_key(c, carry):
            total, out = carry
            p = jnp.exp((sbuf[t, tile(c - t), :] - top) * SCALE)
            pb = p.astype(BF16)
            pbuf[t, tile(c - t), :] = pb
            return total + fold(p, jnp.sum), out + dot(vt[:, tile(c)], pb)

        total, out = lax.fori_loop(
            jnp.maximum(t, low_tile), t + NK, per_key,
            (jnp.zeros((8, TILE), F32), jnp.zeros((HD, TILE), F32)),
        )
        inv = 1.0 / jnp.sum(total, axis=0, keepdims=True)
        out = out * inv
        obuf[tile(t), :] = out.T.astype(BF16)
        dot_ = dobuf[tile(t), :].astype(F32).T
        dvec[:, tile(t)] = jnp.broadcast_to(jnp.sum(dot_ * out, axis=0, keepdims=True) * inv, (8, TILE))
        dol[tile(t), :] = (dot_ * inv).T.astype(BF16)
        dqt[t] = jnp.zeros((HD, TILE), F32)
        return 0

    lax.fori_loop(0, NQ, forward, 0)

    outs = (obuf, dqb, sum_k, sum_v)
    backs = (o_in, dq_in, dk_in, dv_in)

    def b_copy(arr, d):
        p = xpeer(d)
        return remote(outs[arr].at[rows(p), :], backs[arr].at[:, cols(x)],
                      b_send.at[arr, d - 1], b_recv.at[arr, d - 1], z * NX + p, v)

    def b_wait(arr, d):
        p = lax.rem(x + NX - d, NX)
        here = backs[arr].at[:, cols(p)]
        remote(here, here, b_send.at[arr, d - 1], b_recv.at[arr, d - 1], s, v).wait_recv()

    def b_own(arr):
        backs[arr][:, cols(x)] = outs[arr][rows(x), :]

    for d in (1, 3, 2):
        b_copy(0, d).start()
    b_own(0)

    def backward(slot):
        def per_key(c, _):
            kc, vc, ktc = kbuf[tile(c), :], vbuf[tile(c), :], kt[:, tile(c)]

            def per_query(t, carry):
                dk, dv = carry
                pb = pbuf[t, tile(c - t), :]
                dolt = dol[tile(t), :]
                dp = dot(vc, dolt, NT)
                ds = (pb.astype(F32) * (dp - dvec[0:1, tile(t)])).astype(BF16)
                dqt[t] += dot(ktc, ds)
                return dk + dot(ds, qbuf[tile(t), :]), dv + dot(pb, dolt)

            zero = jnp.zeros((TILE, HD), F32)
            dk, dv = lax.fori_loop(
                jnp.maximum(0, c - 2 * NQ), jnp.minimum(NQ - 1, c) + 1, per_query, (zero, zero))
            dk = dk * SCALE
            if slot == 2:
                own_k[tile(c - 2 * NQ), :] = dk
                own_v[tile(c - 2 * NQ), :] = dv
            else:
                part_k[tile(c), :] = dk.astype(BF16)
                part_v[tile(c), :] = dv.astype(BF16)
            return 0

        lax.fori_loop(slot * NQ, (slot + 1) * NQ, per_key, 0)

    parts, gots = (part_k, part_v), (got_k, got_v)

    def p_copy(arr, dz, p):
        return remote(parts[arr].at[pl.ds((2 - dz) * CH + p * TD, TD), :],
                      gots[arr].at[pl.ds((dz - 1) * CH + p * TD, TD), :],
                      p_send.at[arr, dz - 1, p], p_recv.at[arr, dz - 1, p], s - dz * NX, v)

    for dz in (2, 1):
        @pl.when(z >= dz)
        def _():
            backward(2 - dz)
            for p in range(NX):
                for arr in (0, 1):
                    p_copy(arr, dz, p).start()

    backward(2)
    for t in range(NQ):
        dqb[t * TILE:(t + 1) * TILE, :] = (dqt[t] * SCALE).T.astype(BF16)
    for d in (1, 3, 2):
        b_copy(1, d).start()
    b_own(1)

    for d in (1, 3, 2):
        b_wait(0, d)
    mixed_ref[...] = (o_in[...].astype(F32) + cross[...]).astype(BF16)
    for i in range(16):
        @pl.when(jnp.logical_not(jnp.logical_and(s == i, own_piece)))
        def _():
            here = latrecv.at[i]
            remote(here, here, g_send.at[0, 0], g_recv.at[i], s, v).wait_recv()
    for n, g in enumerate((lkg_ref, lvg_ref)):
        acc = latrecv[0, n].astype(F32)
        for i in range(1, 16):
            acc = acc + latrecv[i, n].astype(F32)
        g[0] = acc

    for p in range(NX):
        sl = slice(p * TD, (p + 1) * TD)
        for arr, (own, out) in enumerate(((own_k, sum_k), (own_v, sum_v))):
            for dz in (1, 2):
                @pl.when(z + dz < NX)
                def _():
                    here = gots[arr].at[pl.ds((dz - 1) * CH + p * TD, TD), :]
                    remote(here, here, p_send.at[arr, dz - 1, p], p_recv.at[arr, dz - 1, p], s, v).wait_recv()
                    own[sl, :] += here[...].astype(F32)
            out[sl, :] = own[sl, :].astype(BF16)
    for arr in (2, 3):
        for d in (1, 3, 2):
            b_copy(arr, d).start()
        b_own(arr)
    for arr, out in ((1, qg_ref), (2, kg_ref), (3, vg_ref)):
        for d in (1, 3, 2):
            b_wait(arr, d)
        out[...] = backs[arr][...].astype(F32)

    for d in range(1, NX):
        for arr in range(4):
            a_copy(arr, d).wait_send()
            b_copy(arr, d).wait_send()
        for stage in range(2):
            c_copy(stage, d).wait_send()
    for arr in (0, 1):
        for d in range(1, IMAGES):
            l_copy(arr, d).wait_send()
        for dz in (1, 2):
            @pl.when(z + dz < NX)
            def _():
                for d in range(NX):
                    z_copy(arr, dz, d).wait_send()

            @pl.when(z >= dz)
            def _():
                for p in range(NX):
                    p_copy(arr, dz, p).wait_send()
    for m in range(IMAGES):
        for h in range(2):
            @pl.when(jnp.logical_not(g_mine(m, h)))
            def _():
                g_copy(m, h).wait_send()


def shards(query, key, value, doc_ids, cross_query, latent_key, latent_value, token_slot,
           slot_image, cross_gate, out_grad):
    vm = pl.BlockSpec(memory_space=pltpu.VMEM)
    sm = pl.BlockSpec(memory_space=pltpu.SMEM)
    dma = pltpu.SemaphoreType.DMA
    scratch = [
        pltpu.VMEM((NC * CH, HD), BF16), pltpu.VMEM((NC * CH, HD), BF16),
        pltpu.VMEM((CH, HD), BF16), pltpu.VMEM((CH, HD), BF16), pltpu.VMEM((CH, HD), BF16),
        pltpu.VMEM((HD, NC * CH), BF16), pltpu.VMEM((HD, NC * CH), BF16),
        pltpu.VMEM((NQ, NK * TILE, TILE), F32), pltpu.VMEM((NQ, NK * TILE, TILE), BF16),
        pltpu.VMEM((8, CH), F32), pltpu.VMEM((8, CH), F32), pltpu.VMEM((8, CH), I32),
        pltpu.VMEM((NQ, HD, TILE), F32),
        pltpu.VMEM((8, HD), F32), pltpu.VMEM((3, 8, HD), F32),
        pltpu.VMEM((8, HD), F32), pltpu.VMEM((3, 8, HD), F32),
        pltpu.VMEM((IMAGES, LAT, WD), BF16), pltpu.VMEM((IMAGES, LAT, WD), BF16),
        pltpu.VMEM((SLOTS * LAT, WD), BF16), pltpu.VMEM((SLOTS * LAT, WD), BF16),
        pltpu.VMEM((SLOTS * LAT, WD), F32), pltpu.VMEM((SLOTS * LAT, WD), F32),
        pltpu.VMEM((TD, WD), F32),
        pltpu.VMEM((IMAGES, 2, 2, LAT, 256), BF16), pltpu.VMEM((16, 2, LAT, 256), BF16),
        pltpu.VMEM((CH, HD), BF16), pltpu.VMEM((CH, HD), BF16),
        pltpu.VMEM((2 * CH, HD), BF16), pltpu.VMEM((2 * CH, HD), BF16),
        pltpu.VMEM((CH, HD), F32), pltpu.VMEM((CH, HD), F32),
        pltpu.VMEM((2 * CH, HD), BF16), pltpu.VMEM((2 * CH, HD), BF16),
        pltpu.VMEM((CH, HD), BF16), pltpu.VMEM((CH, HD), BF16),
        pltpu.VMEM((TD, WD), BF16), pltpu.VMEM((TD, WD), BF16),
        pltpu.VMEM((TD, WD), BF16), pltpu.VMEM((TD, WD), BF16),
        dma((4, 3)), dma((4, 3)),
        dma((2, 2, 4)), dma((2, 2, 4)),
        dma((2, 3)), dma((2, 3)),
        dma((2, 7)), dma((2, 7)),
        dma((8, 2)), dma((16,)),
        dma((2, 2, 4)), dma((2, 2, 4)),
        dma((4, 3)), dma((4, 3)),
    ]
    full = jax.ShapeDtypeStruct((TD, WD), F32)
    lat = jax.ShapeDtypeStruct((1, LAT, 256), F32)
    return pl.pallas_call(
        kernel,
        out_shape=(jax.ShapeDtypeStruct((TD, WD), BF16), full, full, full, full, lat, lat),
        in_specs=[vm, vm, sm] + [vm] * 8,
        out_specs=(vm,) * 7,
        scratch_shapes=scratch,
        cost_estimate=pl.CostEstimate(flops=6_500_000_000, bytes_accessed=8_000_000, transcendentals=4_000_000),
        compiler_params=pltpu.CompilerParams(
            collective_id=0, has_side_effects=True, vmem_limit_bytes=58 * 1024 * 1024),
    )(
        doc_ids.reshape(1, TD), token_slot.reshape(1, TD), slot_image, cross_gate.reshape(1, WD),
        query, key, value, cross_query, out_grad, latent_key, latent_value,
    )


def solution(mesh):
    own = P("seq", "vis")
    lat_in = P("vis", None, None)
    lat_out = P("vis", None, "seq")
    return jax.shard_map(
        shards,
        mesh=mesh,
        in_specs=(own, own, own, P("seq"), own, lat_in, lat_in, P("seq"), P("seq"), P("vis"), own),
        out_specs=(own, own, own, own, own, lat_out, lat_out),
        check_vma=False,
    )
```

```python
import functools
import math

import jax
import jax.numpy as jnp
from jax import lax
from jax.experimental import pallas as pl
from jax.experimental.pallas import tpu as pltpu
from jax.sharding import PartitionSpec as P

HD = 128
TD = 320
NX = 4
CH = TD * NX
NC = 3
TILE = 256
NQ = CH // TILE
LAT = 64
SLOTS = 4
IMAGES = 8
WD = 512
SCALE = 1.0 / math.sqrt(HD)
BIG = -1e30
MESH = pl.DeviceIdType.MESH
F32, BF16, I32 = jnp.float32, jnp.bfloat16, jnp.int32

NT = (((1,), (1,)), ((), ()))
NN = (((1,), (0,)), ((), ()))


def dot(a, b, dims=NN):
    return lax.dot_general(a, b, dims, preferred_element_type=F32)


def fold(a, op):
    return op(a.reshape(a.shape[0] // 8, 8, a.shape[1]), axis=0)

LOG2E = 1.4426950408889634

FWD_TILES = (
    tuple((c * TILE, TILE, 0, (c + 1) * TILE) for c in range(NQ)),
    tuple((c * TILE, TILE, 0, CH) for c in range(NQ)),
    tuple((c * TILE, TILE, c * TILE, CH - c * TILE) for c in range(NQ)),
)
BWD_TILES = (FWD_TILES[0], ((0, CH // 2, 0, CH), (CH // 2, CH // 2, 0, CH)), FWD_TILES[2])
ORDER = (0, 1, 3, 2)


def kernel(
    docs_ref, tok_ref, img_ref, gate_ref, q_ref, k_ref, v_ref, cq_ref, do_ref, lk_ref, lv_ref,
    mixed_ref, qg_ref, kg_ref, vg_ref, cqg_ref, lkg_ref, lvg_ref,
    kbuf, vbuf, qbuf, dobuf, dol, kt, vt, sbuf, pbuf, opart, maxes, sums, starts, dot_t, dqt,
    cown, cx, crow, cz, cqv, dov, stage,
    latk, latv, lks, lvs, gk, gv, cross, latsend, latx, latz, latzin, latp, latin,
    obuf, dqb, part_k, part_v, own_k, own_v, got_k, got_v, sum_k, sum_v,
    o_in, dq_in, dk_in, dv_in,
    a_send, a_recv, z_send, z_recv, c_send, c_recv, l_send, l_recv, gx_send, gx_recv, gz_send, gz_recv,
    gp_send, gp_recv, p_send, p_recv, b_send, b_recv, f_send, f_recv, own_sem,
):
    s = lax.axis_index("seq")
    v = lax.axis_index("vis")
    x = lax.rem(s, NX)
    z = lax.div(s, NX)

    def xpeer(d):
        return lax.rem(x + d, NX)

    def zpeer(d):
        return lax.rem(z + d, NX)

    def remote(src, dst, ssem, rsem, seq, vis):
        return pltpu.make_async_remote_copy(
            src_ref=src, dst_ref=dst, send_sem=ssem, recv_sem=rsem,
            device_id=(seq, vis), device_id_type=MESH,
        )

    def landed(here, rsem):
        remote(here, here, rsem, rsem, s, v).wait_recv()

    def rows(i, n=TD):
        return pl.ds(pl.multiple_of(i * n, n), n)

    def cols(i, n=HD):
        return pl.ds(pl.multiple_of(i * n, n), n)

    def piece(slot, p):
        return pl.ds(pl.multiple_of(slot * CH + p * TD, TD), TD)

    barrier = pltpu.get_barrier_semaphore()

    def greet(seq, vis):
        pl.semaphore_signal(barrier, inc=1, device_id=(seq, vis), device_id_type=MESH)

    to_seq = 2 * v + lax.rem(z, 2)
    to_vis = 2 * x + lax.div(z, 2)
    from_seq = (2 * lax.rem(v, 2) + lax.rem(s, 2)) * NX + lax.div(v, 2)
    from_vis = lax.div(s, 2)
    stays = jnp.logical_and(to_seq == s, to_vis == v)
    moves = jnp.logical_not(stays)

    for d in range(1, NX):
        greet(z * NX + xpeer(d), v)
        greet(zpeer(d) * NX + x, v)
    for d in range(1, IMAGES):
        greet(s, lax.rem(v + d, IMAGES))

    @pl.when(moves)
    def _():
        greet(from_seq, from_vis)

    def own_copy(i):
        src, dst = (
            (k_ref.at[:, cols(x)], kbuf.at[piece(2, x), :]),
            (v_ref.at[:, cols(x)], vbuf.at[piece(2, x), :]),
            (q_ref.at[:, cols(x)], qbuf.at[piece(0, x), :]),
            (do_ref.at[:, cols(x)], dobuf.at[piece(0, x), :]),
            (lk_ref.at[0, :, cols(v, WD)], latk.at[v]),
            (lv_ref.at[0, :, cols(v, WD)], latv.at[v]),
            (cq_ref, cqv),
            (do_ref, dov),
        )[i]
        return pltpu.make_async_copy(src, dst, own_sem.at[i])

    for i in range(8):
        own_copy(i).start()

    docs = docs_ref[...]
    row_id = lax.broadcasted_iota(I32, (8, HD), 0)
    counts = jnp.zeros((8, HD), F32)
    for d in range(1, 4):
        c = jnp.sum(jnp.where(docs < d, 1.0, 0.0), axis=1, keepdims=True)
        counts = jnp.where(row_id == d, c, counts)
    cown[...] = counts
    pl.semaphore_wait(barrier, 13 + jnp.where(stays, 0, 1))

    ins = (k_ref, v_ref, q_ref, do_ref)
    bufs = (kbuf, vbuf, qbuf, dobuf)
    base = (2, 2, 0, 0)

    def a_copy(arr, d):
        p = xpeer(d)
        return remote(ins[arr].at[:, cols(p)], bufs[arr].at[piece(base[arr], x), :],
                      a_send.at[arr, d - 1], a_recv.at[arr, d - 1], z * NX + p, v)

    def a_wait(arr, d):
        landed(bufs[arr].at[piece(base[arr], xpeer(NX - d)), :], a_recv.at[arr, d - 1])

    def c_copy(step, d):
        if step == 0:
            return remote(cown, cx.at[d - 1], c_send.at[0, d - 1], c_recv.at[0, d - 1],
                          z * NX + xpeer(d), v)
        return remote(crow, cz.at[d - 1], c_send.at[1, d - 1], c_recv.at[1, d - 1],
                      zpeer(d) * NX + x, v)

    def z_copy(arr, dz, i):
        p = xpeer(NX - ORDER[i])
        src = ins[arr].at[:, cols(x)] if i == 0 else bufs[arr].at[piece(2, p), :]
        return remote(src, bufs[arr].at[piece(2 - dz, p), :],
                      z_send.at[arr, dz - 1, i], z_recv.at[arr, dz - 1, i], s + dz * NX, v)

    def f_copy(arr, i):
        p = xpeer(NX - ORDER[i])
        src = ins[arr].at[:, cols(x)] if i == 0 else bufs[arr].at[piece(2, p), :]
        return remote(src, stage.at[arr, i], z_send.at[arr, 1, i], f_recv.at[arr, i], s + 3 * NX, v)

    def f_on(arr, i):
        p = xpeer(NX - ORDER[i])
        return remote(stage.at[arr, i], bufs[arr].at[piece(0, p), :],
                      f_send.at[arr, i], z_recv.at[arr, 1, i], s - NX, v)

    def z_start(arr, i):
        if i < 2:
            @pl.when(z == 0)
            def _():
                f_copy(arr, i).start()

            @pl.when(z == 1)
            def _():
                z_copy(arr, 2, i).start()
        else:
            @pl.when(z <= 1)
            def _():
                z_copy(arr, 2, i).start()

        @pl.when(z <= 2)
        def _():
            z_copy(arr, 1, i).start()

    def f_relay(arr):
        @pl.when(z == 3)
        def _():
            for i in range(2):
                landed(stage.at[arr, i], f_recv.at[arr, i])
                f_on(arr, i).start()

    def z_wait(arr, dz):
        for i in range(NX):
            landed(bufs[arr].at[piece(2 - dz, xpeer(NX - ORDER[i])), :], z_recv.at[arr, dz - 1, i])

    for arr in (0, 1):
        z_start(arr, 0)
        for d in ORDER[1:]:
            a_copy(arr, d).start()
    for d in ORDER[1:]:
        c_copy(0, d).start()
    for arr in (2, 3):
        for d in ORDER[1:]:
            a_copy(arr, d).start()

    lins, lbufs = (lk_ref, lv_ref), (latk, latv)

    def l_copy(arr, d):
        p = lax.rem(v + d, IMAGES)
        return remote(lins[arr].at[0, :, cols(p, WD)], lbufs[arr].at[v],
                      l_send.at[arr, d - 1], l_recv.at[arr, d - 1], s, p)

    for arr in (0, 1):
        for d in range(1, IMAGES):
            l_copy(arr, d).start()

    for arr in (0, 1):
        for i in range(1, NX):
            a_wait(arr, ORDER[i])
            z_start(arr, i)
    f_relay(0)

    for d in ORDER[1:]:
        landed(cx.at[d - 1], c_recv.at[0, d - 1])
    crow[...] = cown[...] + cx[0] + cx[1] + cx[2]
    for d in range(1, NX):
        c_copy(1, d).start()
    for i in range(8):
        own_copy(i).wait()
    for d in ORDER[1:]:
        a_wait(2, d)
    f_relay(1)
    for d in range(1, NX):
        landed(cz.at[d - 1], c_recv.at[1, d - 1])
    before = crow[...] + cz[0] + cz[1] + cz[2]
    pos = lax.broadcasted_iota(I32, (8, CH), 1)
    start = jnp.zeros((8, CH), I32)
    for d in range(1, 4):
        b = before[d:d + 1, 0:1].astype(I32)
        start = jnp.where(b <= pos + z * CH, b, start)
    starts[...] = start - (z - 2) * CH

    for slot in range(NC):
        maxes[slot] = jnp.full((8, CH), BIG, F32)
        sums[slot] = jnp.zeros((8, CH), F32)
        opart[slot] = jnp.zeros((HD, CH), F32)

    def forward(slot):
        at = slot * CH
        kt[:, at:at + CH] = kbuf[at:at + CH, :].T
        vt[:, at:at + CH] = vbuf[at:at + CH, :].T
        for k0, kn, q0, qn in FWD_TILES[slot]:
            across = slice(q0, q0 + qn)
            raw = dot(kbuf[at + k0:at + k0 + kn, :], qbuf[across, :], NT)
            kpos = lax.broadcasted_iota(I32, (kn, qn), 0) + (at + k0)
            kept = kpos >= starts[0:1, across]
            if slot == 2:
                kept = kept & (kpos <= lax.broadcasted_iota(I32, (kn, qn), 1) + (at + q0))
            raw = jnp.where(kept, raw, BIG)
            sbuf[k0:k0 + kn, across] = raw
            maxes[slot, :, across] = jnp.maximum(maxes[slot, :, across], fold(raw, jnp.max))
        top = jnp.max(maxes[slot], axis=0, keepdims=True)
        maxes[slot] = jnp.broadcast_to(top, (8, CH))
        for k0, kn, q0, qn in FWD_TILES[slot]:
            across = slice(q0, q0 + qn)
            p = jnp.exp2((sbuf[k0:k0 + kn, across] - top[:, across]) * (SCALE * LOG2E))
            pb = p.astype(BF16)
            pbuf[at + k0:at + k0 + kn, across] = pb
            sums[slot, :, across] += fold(p, jnp.sum)
            opart[slot, :, across] += dot(vt[:, at + k0:at + k0 + kn], pb)

    forward(2)

    for arr in (0, 1):
        for d in range(1, IMAGES):
            landed(lbufs[arr].at[lax.rem(v + IMAGES - d, IMAGES)], l_recv.at[arr, d - 1])
    for i in range(SLOTS):
        lks[i * LAT:(i + 1) * LAT, :] = latk[img_ref[i]]
        lvs[i * LAT:(i + 1) * LAT, :] = latv[img_ref[i]]
    slot_of = lax.broadcasted_iota(I32, (SLOTS * LAT, TD), 0) // LAT
    seen = slot_of == tok_ref[...]
    any_image = tok_ref[...] < SLOTS
    gate = jnp.tanh(gate_ref[...])
    for h in range(NX):
        sl = slice(h * HD, (h + 1) * HD)
        lkh, lvh, cqh = lks[:, sl], lvs[:, sl], cqv[:, sl]
        raw = dot(lkh, cqh, NT)
        raw = jnp.where(seen, raw * SCALE, BIG)
        w = jnp.where(seen, jnp.exp(raw - jnp.max(raw, axis=0, keepdims=True)), 0.0)
        total = jnp.where(any_image, jnp.sum(w, axis=0, keepdims=True), 1.0)
        probs = w / total
        low = probs.astype(BF16)
        cross[:, sl] = gate[:, sl] * dot(lvh.T, low).T
        back = (gate[:, sl] * dov[:, sl].astype(F32)).astype(BF16)
        gp = dot(lvh, back, NT)
        cdot = jnp.sum(probs * gp, axis=0, keepdims=True)
        ds = (probs * (gp - cdot) * SCALE).astype(BF16)
        cqg_ref[:, sl] = dot(lkh.T, ds).T.astype(cqg_ref.dtype)
        gk[:, sl] = dot(ds, cqh).astype(BF16).astype(F32)
        gv[:, sl] = dot(low, back).astype(BF16).astype(F32)

    for m in range(IMAGES):
        for n, g in enumerate((gk, gv)):
            acc = jnp.zeros((LAT, WD), F32)
            for i in range(SLOTS):
                acc = acc + jnp.where(img_ref[i] == m, 1.0, 0.0) * g[i * LAT:(i + 1) * LAT, :]
            acc = acc.astype(BF16)
            for h in range(2):
                latsend[m // 2, (m % 2) * 2 + h, n] = acc[:, h * 256:(h + 1) * 256]

    def gx_copy(d):
        p = xpeer(d)
        return remote(latsend.at[p], latx.at[d - 1], gx_send.at[d - 1], gx_recv.at[d - 1],
                      z * NX + p, v)

    def gz_copy(d):
        p = zpeer(d)
        return remote(latz.at[p], latzin.at[d - 1], gz_send.at[d - 1], gz_recv.at[d - 1],
                      p * NX + x, v)

    def gp_copy():
        return remote(latp, latin, gp_send.at[0], gp_recv.at[0], to_seq, to_vis)

    for d in ORDER[1:]:
        gx_copy(d).start()

    @pl.when(z >= 1)
    def _():
        z_wait(0, 1)
        z_wait(1, 1)
        forward(1)

    for d in ORDER[1:]:
        landed(latx.at[d - 1], gx_recv.at[d - 1])
    for i in range(NX):
        for n in range(2):
            acc = latsend[x, i, n].astype(F32)
            for d in range(3):
                acc = acc + latx[d, i, n].astype(F32)
            latz[i, n] = acc.astype(BF16)
    for d in ORDER[1:]:
        gz_copy(d).start()

    @pl.when(z >= 2)
    def _():
        z_wait(0, 2)
        z_wait(1, 2)
        forward(0)

    for d in ORDER[1:]:
        a_wait(3, d)

    top = jnp.maximum(jnp.maximum(maxes[0], maxes[1]), maxes[2])
    total = jnp.zeros((1, CH), F32)
    out = jnp.zeros((HD, CH), F32)
    for slot in range(NC):
        factor = jnp.exp2((maxes[slot] - top) * (SCALE * LOG2E))
        maxes[slot] = factor
        total = total + jnp.sum(sums[slot], axis=0, keepdims=True) * factor[0:1]
        out = out + opart[slot] * factor[0:1]
    inv = 1.0 / total
    out = out * inv
    obuf[...] = out.T.astype(BF16)
    dot_t[...] = dobuf[...].astype(F32).T
    row_dot = jnp.sum(dot_t[...] * out, axis=0, keepdims=True)
    for slot in range(NC):
        factor = maxes[slot] * inv
        maxes[slot] = factor
        sums[slot] = factor * row_dot
        dol[slot] = (dot_t[...] * factor[0:1]).T.astype(BF16)
    dqt[...] = jnp.zeros_like(dqt)

    outs = (obuf, dqb, sum_k, sum_v)
    backs = (o_in, dq_in, dk_in, dv_in)

    def b_copy(arr, d):
        p = xpeer(d)
        return remote(outs[arr].at[rows(p), :], backs[arr].at[:, cols(x)],
                      b_send.at[arr, d - 1], b_recv.at[arr, d - 1], z * NX + p, v)

    def b_wait(arr, d):
        landed(backs[arr].at[:, cols(xpeer(NX - d))], b_recv.at[arr, d - 1])

    def b_own(arr):
        backs[arr][:, cols(x)] = outs[arr][rows(x), :]

    for d in ORDER[1:]:
        b_copy(0, d).start()
    b_own(0)

    parts, gots = (part_k, part_v), (got_k, got_v)

    def p_copy(arr, dz, p):
        return remote(parts[arr].at[pl.ds((2 - dz) * CH + p * TD, TD), :],
                      gots[arr].at[pl.ds((dz - 1) * CH + p * TD, TD), :],
                      p_send.at[arr, dz - 1, p], p_recv.at[arr, dz - 1, p], s - dz * NX, v)

    def r_copy(arr, p):
        return remote(parts[arr].at[pl.ds(p * TD, TD), :], stage.at[arr, p],
                      p_send.at[arr, 1, p], f_recv.at[arr, p], s - 3 * NX, v)

    def r_on(arr, p):
        return remote(stage.at[arr, p], gots[arr].at[pl.ds(CH + p * TD, TD), :],
                      f_send.at[arr, p], p_recv.at[arr, 1, p], s + NX, v)

    def p_start(dz, p):
        for arr in (0, 1):
            if dz == 2 and p < 2:
                @pl.when(z == 3)
                def _():
                    r_copy(arr, p).start()

                @pl.when(z == 2)
                def _():
                    p_copy(arr, dz, p).start()
            else:
                p_copy(arr, dz, p).start()

    def backward(slot):
        at = slot * CH
        sent = 0
        for k0, kn, q0, qn in BWD_TILES[slot]:
            down, across = slice(at + k0, at + k0 + kn), slice(q0, q0 + qn)
            pb = pbuf[down, across]
            grad = dol[slot, across, :]
            dp = dot(vbuf[down, :], grad, NT)
            ds = (pb.astype(F32) * (dp - sums[slot, 0:1, across])).astype(BF16)
            dk = dot(ds, qbuf[across, :]) * SCALE
            dv = dot(pb, grad)
            dqt[:, across] += dot(kt[:, down], ds)
            if slot == 2:
                own_k[k0:k0 + kn, :] = dk
                own_v[k0:k0 + kn, :] = dv
            else:
                part_k[down, :] = dk.astype(BF16)
                part_v[down, :] = dv.astype(BF16)
                while (sent + 1) * TD <= k0 + kn:
                    p_start(2 - slot, sent)
                    sent += 1

    @pl.when(z >= 2)
    def _():
        backward(0)

    @pl.when(z >= 1)
    def _():
        backward(1)

    backward(2)
    dqb[...] = (dqt[...] * SCALE).T.astype(BF16)
    for d in ORDER[1:]:
        b_copy(1, d).start()
    b_own(1)

    @pl.when(z == 0)
    def _():
        for p in range(2):
            for arr in (0, 1):
                landed(stage.at[arr, p], f_recv.at[arr, p])
                r_on(arr, p).start()

    for d in ORDER[1:]:
        landed(latzin.at[d - 1], gz_recv.at[d - 1])
    for n in range(2):
        acc = latz[z, n].astype(F32)
        for d in range(3):
            acc = acc + latzin[d, n].astype(F32)
        latp[n] = acc.astype(BF16)

    @pl.when(moves)
    def _():
        gp_copy().start()

    @pl.when(stays)
    def _():
        latin[...] = latp[...]

    for d in ORDER[1:]:
        b_wait(0, d)
    mixed_ref[...] = (o_in[...].astype(F32) + cross[...]).astype(BF16)

    def p_wait(arr, dz, p):
        here = gots[arr].at[pl.ds((dz - 1) * CH + p * TD, TD), :]
        landed(here, p_recv.at[arr, dz - 1, p])
        return here

    for p in range(NX):
        sl = slice(p * TD, (p + 1) * TD)
        for arr, (own, out_) in enumerate(((own_k, sum_k), (own_v, sum_v))):
            for dz in (2, 1):
                @pl.when(z + dz < NX)
                def _():
                    here = p_wait(arr, dz, p)
                    own[sl, :] += here[...].astype(F32)
            out_[sl, :] = own[sl, :].astype(BF16)
        for arr in (2, 3):
            for d in range(1, NX):
                @pl.when(xpeer(d) == p)
                def _():
                    b_copy(arr, d).start()

    @pl.when(moves)
    def _():
        landed(latin, gp_recv.at[0])

    lkg_ref[0] = latin[0].astype(F32)
    lvg_ref[0] = latin[1].astype(F32)
    for d in ORDER[1:]:
        b_wait(1, d)
    qg_ref[...] = dq_in[...]
    for arr, out_ in ((2, kg_ref), (3, vg_ref)):
        b_own(arr)
        for d in ORDER[1:]:
            b_wait(arr, d)
        out_[...] = backs[arr][...]

    for d in range(1, NX):
        for arr in range(4):
            a_copy(arr, d).wait_send()
            b_copy(arr, d).wait_send()
        for step in range(2):
            c_copy(step, d).wait_send()
        gx_copy(d).wait_send()
        gz_copy(d).wait_send()

    @pl.when(moves)
    def _():
        gp_copy().wait_send()

    for arr in (0, 1):
        for d in range(1, IMAGES):
            l_copy(arr, d).wait_send()
        for dz in (1, 2):
            @pl.when(z + dz < NX)
            def _():
                for i in range(NX):
                    z_copy(arr, dz, i).wait_send()

            @pl.when(z >= dz)
            def _():
                for p in range(NX):
                    p_copy(arr, dz, p).wait_send()

        @pl.when(z == 3)
        def _():
            for i in range(2):
                f_on(arr, i).wait_send()

        @pl.when(z == 0)
        def _():
            for p in range(2):
                r_on(arr, p).wait_send()


def widen(mixed_ref, *refs):
    half = len(refs) // 2
    refs[half][...] = mixed_ref[...]
    for src, dst in zip(refs[:half], refs[half + 1:]):
        dst[...] = src[...].astype(F32)


def shards(query, key, value, doc_ids, cross_query, latent_key, latent_value, token_slot,
           slot_image, cross_gate, out_grad):
    vm = pl.BlockSpec(memory_space=pltpu.VMEM)
    sm = pl.BlockSpec(memory_space=pltpu.SMEM)
    hbm = pl.BlockSpec(memory_space=pl.ANY)
    dma = pltpu.SemaphoreType.DMA

    def low(*shape):
        return pltpu.VMEM(shape, BF16)

    def wide(*shape):
        return pltpu.VMEM(shape, F32)

    scratch = [
        low(NC * CH, HD), low(NC * CH, HD), low(CH, HD), low(CH, HD),
        low(NC, CH, HD), low(HD, NC * CH), low(HD, NC * CH),
        wide(CH, CH), low(NC * CH, CH), wide(NC, HD, CH),
        wide(NC, 8, CH), wide(NC, 8, CH), pltpu.VMEM((8, CH), I32),
        wide(HD, CH), wide(HD, CH),
        wide(8, HD), wide(3, 8, HD), wide(8, HD), wide(3, 8, HD),
        low(TD, WD), low(TD, WD), low(2, 2, TD, HD),
        low(IMAGES, LAT, WD), low(IMAGES, LAT, WD),
        low(SLOTS * LAT, WD), low(SLOTS * LAT, WD),
        wide(SLOTS * LAT, WD), wide(SLOTS * LAT, WD), wide(TD, WD),
        low(NX, NX, 2, LAT, 256), low(3, NX, 2, LAT, 256),
        low(NX, 2, LAT, 256), low(3, 2, LAT, 256), low(2, LAT, 256), low(2, LAT, 256),
        low(CH, HD), low(CH, HD), low(2 * CH, HD), low(2 * CH, HD),
        wide(CH, HD), wide(CH, HD), low(2 * CH, HD), low(2 * CH, HD),
        low(CH, HD), low(CH, HD),
        low(TD, WD), low(TD, WD), low(TD, WD), low(TD, WD),
        dma((4, 3)), dma((4, 3)),
        dma((2, 2, 4)), dma((2, 2, 4)),
        dma((2, 3)), dma((2, 3)),
        dma((2, 7)), dma((2, 7)),
        dma((3,)), dma((3,)), dma((3,)), dma((3,)), dma((1,)), dma((1,)),
        dma((2, 2, 4)), dma((2, 2, 4)),
        dma((4, 3)), dma((4, 3)),
        dma((2, 2)), dma((2, 2)), dma((8,)),
    ]
    full = jax.ShapeDtypeStruct((TD, WD), F32)
    half = jax.ShapeDtypeStruct((TD, WD), BF16)
    lat = jax.ShapeDtypeStruct((1, LAT, 256), F32)
    results = pl.pallas_call(
        kernel,
        out_shape=(half,) * 5 + (lat, lat),
        in_specs=[vm, vm, sm, vm] + [hbm] * 7,
        out_specs=(vm,) * 7,
        scratch_shapes=scratch,
        cost_estimate=pl.CostEstimate(flops=6_500_000_000, bytes_accessed=8_000_000, transcendentals=4_000_000),
        compiler_params=pltpu.CompilerParams(
            collective_id=0, has_side_effects=True, vmem_limit_bytes=58 * 1024 * 1024),
    )(
        doc_ids.reshape(1, TD), token_slot.reshape(1, TD), slot_image, cross_gate.reshape(1, WD),
        query, key, value, cross_query, out_grad, latent_key, latent_value,
    )
    return pl.pallas_call(
        widen,
        out_shape=(half,) + (full,) * 4 + (lat, lat),
        in_specs=[vm] * 7,
        out_specs=(vm,) * 7,
        cost_estimate=pl.CostEstimate(flops=1_000_000, bytes_accessed=5_000_000, transcendentals=0),
    )(*results)


def solution(mesh):
    own = P("seq", "vis")
    lat_in = P("vis", None, None)
    lat_out = P("vis", None, "seq")
    return jax.shard_map(
        shards,
        mesh=mesh,
        in_specs=(own, own, own, P("seq"), own, lat_in, lat_in, P("seq"), P("seq"), P("vis"), own),
        out_specs=(own, own, own, own, own, lat_out, lat_out),
        check_vma=False,
    )
```

```python
import math

import jax
import jax.numpy as jnp
from jax import lax
from jax.experimental import pallas as pl
from jax.experimental.pallas import tpu as pltpu
from jax.sharding import PartitionSpec as P

HD = 128
TD = 320
NX = 4
CH = TD * NX
NC = 3
TILE = 256
NQ = CH // TILE
LAT = 64
SLOTS = 4
IMAGES = 8
WD = 512
SCALE = 1.0 / math.sqrt(HD)
BIG = -1e30
MESH = pl.DeviceIdType.MESH
F32, BF16, I32 = jnp.float32, jnp.bfloat16, jnp.int32

NT = (((1,), (1,)), ((), ()))
NN = (((1,), (0,)), ((), ()))


def dot(a, b, dims=NN):
    return lax.dot_general(a, b, dims, preferred_element_type=F32)


def fold(a, op):
    return op(a.reshape(a.shape[0] // 8, 8, a.shape[1]), axis=0)


LOG2E = 1.4426950408889634

FWD_TILES = (
    tuple((c * TILE, TILE, 0, (c + 1) * TILE) for c in range(NQ)),
    tuple((c * TILE, TILE, 0, CH) for c in range(NQ)),
    tuple((c * TILE, TILE, c * TILE, CH - c * TILE) for c in range(NQ)),
)
BWD_TILES = (FWD_TILES[0], ((0, CH // 2, 0, CH), (CH // 2, CH // 2, 0, CH)), FWD_TILES[2])
ORDER = (0, 1, 3, 2)


def kernel(
    docs_ref, tok_ref, img_ref, gate_ref, q_ref, k_ref, v_ref, cq_ref, do_ref, lk_ref, lv_ref,
    mixed_ref, qg_ref, kg_ref, vg_ref, cqg_ref, lkg_ref, lvg_ref,
    kbuf, vbuf, qbuf, dobuf, dol, kt, vt, sbuf, pbuf, opart, maxes, sums, dsum, starts, dot_t, dqt,
    cown, cx, crow, cz, cqv, dov, stage,
    latk, latv, lks, lvs, gk, gv, cross, latsend, latx, latz, latzin, latp, latin,
    obuf, dqb, part_k, part_v, sum_k, sum_v, lands,
    o_in, dq_in, dk_in, dv_in,
    a_send, a_recv, z_send, z_recv, c_send, c_recv, l_send, l_recv, gx_send, gx_recv, gz_send, gz_recv,
    gp_send, gp_recv, p_send, p_recv, b_send, b_recv, f_send, f_recv, own_sem,
):
    s = lax.axis_index("seq")
    v = lax.axis_index("vis")
    x = lax.rem(s, NX)
    z = lax.div(s, NX)

    def xpeer(d):
        return lax.rem(x + d, NX)

    def zpeer(d):
        return lax.rem(z + d, NX)

    def remote(src, dst, ssem, rsem, seq, vis):
        return pltpu.make_async_remote_copy(
            src_ref=src, dst_ref=dst, send_sem=ssem, recv_sem=rsem,
            device_id=(seq, vis), device_id_type=MESH,
        )

    def landed(here, rsem):
        remote(here, here, rsem, rsem, s, v).wait_recv()

    def rows(i, n=TD):
        return pl.ds(pl.multiple_of(i * n, n), n)

    def cols(i, n=HD):
        return pl.ds(pl.multiple_of(i * n, n), n)

    def piece(slot, p):
        return pl.ds(pl.multiple_of(slot * CH + p * TD, TD), TD)

    barrier = pltpu.get_barrier_semaphore()

    def greet(seq, vis):
        pl.semaphore_signal(barrier, inc=1, device_id=(seq, vis), device_id_type=MESH)

    to_seq = 2 * v + lax.rem(z, 2)
    to_vis = 2 * x + lax.div(z, 2)
    from_seq = (2 * lax.rem(v, 2) + lax.rem(s, 2)) * NX + lax.div(v, 2)
    from_vis = lax.div(s, 2)
    stays = jnp.logical_and(to_seq == s, to_vis == v)
    moves = jnp.logical_not(stays)

    for dz in range(NX):
        for d in range(NX):
            if dz or d:
                greet(zpeer(dz) * NX + xpeer(d), v)
    for d in range(1, IMAGES):
        greet(s, lax.rem(v + d, IMAGES))

    @pl.when(moves)
    def _():
        greet(from_seq, from_vis)

    def own_copy(i):
        src, dst = (
            (k_ref.at[:, cols(x)], kbuf.at[piece(2, x), :]),
            (v_ref.at[:, cols(x)], vbuf.at[piece(2, x), :]),
            (q_ref.at[:, cols(x)], qbuf.at[piece(0, x), :]),
            (do_ref.at[:, cols(x)], dobuf.at[piece(0, x), :]),
            (lk_ref.at[0, :, cols(v, WD)], latk.at[v]),
            (lv_ref.at[0, :, cols(v, WD)], latv.at[v]),
            (cq_ref, cqv),
            (do_ref, dov),
        )[i]
        return pltpu.make_async_copy(src, dst, own_sem.at[i])

    for i in range(8):
        own_copy(i).start()

    docs = docs_ref[...].reshape(1, TD)
    row_id = lax.broadcasted_iota(I32, (8, HD), 0)
    counts = jnp.zeros((8, HD), F32)
    for d in range(1, 4):
        c = jnp.sum(jnp.where(docs < d, 1.0, 0.0), axis=1, keepdims=True)
        counts = jnp.where(row_id == d, c, counts)
    cown[...] = counts
    pl.semaphore_wait(barrier, 22 + jnp.where(stays, 0, 1))

    ins = (k_ref, v_ref, q_ref, do_ref)
    bufs = (kbuf, vbuf, qbuf, dobuf)
    base = (2, 2, 0, 0)

    def a_copy(arr, d):
        p = xpeer(d)
        return remote(ins[arr].at[:, cols(p)], bufs[arr].at[piece(base[arr], x), :],
                      a_send.at[arr, d - 1], a_recv.at[arr, d - 1], z * NX + p, v)

    def a_wait(arr, d):
        landed(bufs[arr].at[piece(base[arr], xpeer(NX - d)), :], a_recv.at[arr, d - 1])

    def c_copy(step, d):
        if step == 0:
            return remote(cown, cx.at[d - 1], c_send.at[0, d - 1], c_recv.at[0, d - 1],
                          z * NX + xpeer(d), v)
        return remote(crow, cz.at[d - 1], c_send.at[1, d - 1], c_recv.at[1, d - 1],
                      zpeer(d) * NX + x, v)

    def z_copy(arr, dz, i):
        p = xpeer(NX - ORDER[i])
        src = ins[arr].at[:, cols(x)] if i == 0 else bufs[arr].at[piece(2, p), :]
        return remote(src, bufs[arr].at[piece(2 - dz, p), :],
                      z_send.at[arr, dz - 1, i], z_recv.at[arr, dz - 1, i], s + dz * NX, v)

    def f_copy(arr, i):
        p = xpeer(NX - ORDER[i])
        src = ins[arr].at[:, cols(x)] if i == 0 else bufs[arr].at[piece(2, p), :]
        return remote(src, stage.at[arr, i], z_send.at[arr, 1, i], f_recv.at[arr, i], s + 3 * NX, v)

    def f_on(arr, i):
        p = xpeer(NX - ORDER[i])
        return remote(stage.at[arr, i], bufs[arr].at[piece(0, p), :],
                      f_send.at[arr, i], z_recv.at[arr, 1, i], s - NX, v)

    def z_start(arr, i):
        if i < 2:
            @pl.when(z == 0)
            def _():
                f_copy(arr, i).start()

            @pl.when(z == 1)
            def _():
                z_copy(arr, 2, i).start()
        else:
            @pl.when(z <= 1)
            def _():
                z_copy(arr, 2, i).start()

        @pl.when(z <= 2)
        def _():
            z_copy(arr, 1, i).start()

    def f_relay(arr):
        @pl.when(z == 3)
        def _():
            for i in range(2):
                landed(stage.at[arr, i], f_recv.at[arr, i])
                f_on(arr, i).start()

    def z_wait(arr, dz):
        for i in range(NX):
            landed(bufs[arr].at[piece(2 - dz, xpeer(NX - ORDER[i])), :], z_recv.at[arr, dz - 1, i])

    for arr in (0, 1):
        z_start(arr, 0)
        for d in ORDER[1:]:
            a_copy(arr, d).start()
    for d in ORDER[1:]:
        c_copy(0, d).start()
    for arr in (2, 3):
        for d in ORDER[1:]:
            a_copy(arr, d).start()

    lins, lbufs = (lk_ref, lv_ref), (latk, latv)

    def l_copy(arr, d):
        p = lax.rem(v + d, IMAGES)
        return remote(lins[arr].at[0, :, cols(p, WD)], lbufs[arr].at[v],
                      l_send.at[arr, d - 1], l_recv.at[arr, d - 1], s, p)

    for arr in (0, 1):
        for d in range(1, IMAGES):
            l_copy(arr, d).start()

    for arr in (0, 1):
        for i in range(1, NX):
            a_wait(arr, ORDER[i])
            z_start(arr, i)
    f_relay(0)

    for d in ORDER[1:]:
        landed(cx.at[d - 1], c_recv.at[0, d - 1])
    crow[...] = cown[...] + cx[0] + cx[1] + cx[2]
    for d in range(1, NX):
        c_copy(1, d).start()
    for i in range(8):
        own_copy(i).wait()
    for d in ORDER[1:]:
        a_wait(2, d)
    f_relay(1)
    for d in range(1, NX):
        landed(cz.at[d - 1], c_recv.at[1, d - 1])
    before = crow[...] + cz[0] + cz[1] + cz[2]
    pos = lax.broadcasted_iota(I32, (8, CH), 1)
    start = jnp.zeros((8, CH), I32)
    for d in range(1, 4):
        b = before[d:d + 1, 0:1].astype(I32)
        start = jnp.where(b <= pos + z * CH, b, start)
    starts[...] = start - (z - 2) * CH

    for slot in range(NC):
        maxes[slot] = jnp.full((8, CH), BIG, F32)
        sums[slot] = jnp.zeros((8, CH), F32)
        opart[slot] = jnp.zeros((HD, CH), F32)

    def forward(slot):
        at = slot * CH
        kt[:, at:at + CH] = kbuf[at:at + CH, :].T
        vt[:, at:at + CH] = vbuf[at:at + CH, :].T
        for k0, kn, q0, qn in FWD_TILES[slot]:
            across = slice(q0, q0 + qn)
            raw = dot(kbuf[at + k0:at + k0 + kn, :], qbuf[across, :], NT)
            kpos = lax.broadcasted_iota(I32, (kn, qn), 0) + (at + k0)
            kept = kpos >= starts[0:1, across]
            if slot == 2:
                kept = kept & (kpos <= lax.broadcasted_iota(I32, (kn, qn), 1) + (at + q0))
            raw = jnp.where(kept, raw, BIG)
            sbuf[k0:k0 + kn, across] = raw
            maxes[slot, :, across] = jnp.maximum(maxes[slot, :, across], fold(raw, jnp.max))
        top = jnp.max(maxes[slot], axis=0, keepdims=True)
        maxes[slot] = jnp.broadcast_to(top, (8, CH))
        for k0, kn, q0, qn in FWD_TILES[slot]:
            across = slice(q0, q0 + qn)
            p = jnp.exp2((sbuf[k0:k0 + kn, across] - top[:, across]) * (SCALE * LOG2E))
            pb = p.astype(BF16)
            pbuf[at + k0:at + k0 + kn, across] = pb
            sums[slot, :, across] += fold(p, jnp.sum)
            opart[slot, :, across] += dot(vt[:, at + k0:at + k0 + kn], pb)

    def row_sum(slot):
        dsum[slot] = jnp.broadcast_to(jnp.sum(dot_t[...] * opart[slot], axis=0, keepdims=True), (8, CH))

    dsum[0] = jnp.zeros((8, CH), F32)
    dsum[1] = jnp.zeros((8, CH), F32)
    forward(2)
    for d in ORDER[1:]:
        a_wait(3, d)
    dot_t[...] = dobuf[...].astype(F32).T
    row_sum(2)

    for arr in (0, 1):
        for d in range(1, IMAGES):
            landed(lbufs[arr].at[lax.rem(v + IMAGES - d, IMAGES)], l_recv.at[arr, d - 1])
    for i in range(SLOTS):
        lks[i * LAT:(i + 1) * LAT, :] = latk[img_ref[i]]
        lvs[i * LAT:(i + 1) * LAT, :] = latv[img_ref[i]]
    slot_of = lax.broadcasted_iota(I32, (SLOTS * LAT, TD), 0) // LAT
    toks = tok_ref[...].reshape(1, TD)
    seen = slot_of == toks
    any_image = toks < SLOTS
    gate = jnp.tanh(gate_ref[...].reshape(1, WD))
    for h in range(NX):
        sl = slice(h * HD, (h + 1) * HD)
        lkh, lvh, cqh = lks[:, sl], lvs[:, sl], cqv[:, sl]
        raw = dot(lkh, cqh, NT)
        raw = jnp.where(seen, raw * SCALE, BIG)
        w = jnp.where(seen, jnp.exp(raw - jnp.max(raw, axis=0, keepdims=True)), 0.0)
        total = jnp.where(any_image, jnp.sum(w, axis=0, keepdims=True), 1.0)
        probs = w / total
        low = probs.astype(BF16)
        cross[:, sl] = gate[:, sl] * dot(lvh.T, low).T
        back = (gate[:, sl] * dov[:, sl].astype(F32)).astype(BF16)
        gp = dot(lvh, back, NT)
        cdot = jnp.sum(probs * gp, axis=0, keepdims=True)
        ds = (probs * (gp - cdot) * SCALE).astype(BF16)
        cqg_ref[:, sl] = dot(lkh.T, ds).T.astype(cqg_ref.dtype)
        gk[:, sl] = dot(ds, cqh).astype(BF16).astype(F32)
        gv[:, sl] = dot(low, back).astype(BF16).astype(F32)

    for m in range(IMAGES):
        for n, g in enumerate((gk, gv)):
            acc = jnp.zeros((LAT, WD), F32)
            for i in range(SLOTS):
                acc = acc + jnp.where(img_ref[i] == m, 1.0, 0.0) * g[i * LAT:(i + 1) * LAT, :]
            acc = acc.astype(BF16)
            for h in range(2):
                latsend[m // 2, (m % 2) * 2 + h, n] = acc[:, h * 256:(h + 1) * 256]

    def gx_copy(d):
        p = xpeer(d)
        return remote(latsend.at[p], latx.at[d - 1], gx_send.at[d - 1], gx_recv.at[d - 1],
                      z * NX + p, v)

    def gz_copy(d):
        p = zpeer(d)
        return remote(latz.at[p], latzin.at[d - 1], gz_send.at[d - 1], gz_recv.at[d - 1],
                      p * NX + x, v)

    def gp_copy():
        return remote(latp, latin, gp_send.at[0], gp_recv.at[0], to_seq, to_vis)

    for d in ORDER[1:]:
        gx_copy(d).start()

    @pl.when(z >= 1)
    def _():
        z_wait(0, 1)
        z_wait(1, 1)
        forward(1)
        row_sum(1)

    for d in ORDER[1:]:
        landed(latx.at[d - 1], gx_recv.at[d - 1])
    for i in range(NX):
        for n in range(2):
            acc = latsend[x, i, n].astype(F32)
            for d in range(3):
                acc = acc + latx[d, i, n].astype(F32)
            latz[i, n] = acc.astype(BF16)
    for d in ORDER[1:]:
        gz_copy(d).start()

    @pl.when(z >= 2)
    def _():
        z_wait(0, 2)
        z_wait(1, 2)
        forward(0)
        row_sum(0)

    top = jnp.maximum(jnp.maximum(maxes[0], maxes[1]), maxes[2])
    total = jnp.zeros((1, CH), F32)
    row_dot = jnp.zeros((8, CH), F32)
    for slot in range(NC):
        factor = jnp.exp2((maxes[slot] - top) * (SCALE * LOG2E))
        maxes[slot] = factor
        total = total + jnp.sum(sums[slot], axis=0, keepdims=True) * factor[0:1]
        row_dot = row_dot + dsum[slot] * factor
    inv = 1.0 / total
    row_dot = row_dot * inv
    for slot in range(NC):
        factor = maxes[slot] * inv
        maxes[slot] = factor
        sums[slot] = factor * row_dot
    dqt[...] = jnp.zeros_like(dqt)

    for d in ORDER[1:]:
        landed(latzin.at[d - 1], gz_recv.at[d - 1])
    for n in range(2):
        acc = latz[z, n].astype(F32)
        for d in range(3):
            acc = acc + latzin[d, n].astype(F32)
        latp[n] = acc.astype(BF16)

    @pl.when(moves)
    def _():
        gp_copy().start()

    @pl.when(stays)
    def _():
        latin[...] = latp[...]

    outs = (obuf, dqb, sum_k, sum_v)
    backs = (o_in, dq_in, dk_in, dv_in)

    def b_copy(arr, d):
        p = xpeer(d)
        return remote(outs[arr].at[rows(p), :], backs[arr].at[:, cols(x)],
                      b_send.at[arr, d - 1], b_recv.at[arr, d - 1], z * NX + p, v)

    def b_wait(arr, d):
        landed(backs[arr].at[:, cols(xpeer(NX - d))], b_recv.at[arr, d - 1])

    def b_own(arr):
        backs[arr][:, cols(x)] = outs[arr][rows(x), :]

    parts = (part_k, part_v)

    def p_copy(arr, dz, p):
        return remote(parts[arr].at[piece(2 - dz, p), :], lands.at[dz - 1, arr, :, cols(x)],
                      p_send.at[arr, dz - 1, p], p_recv.at[arr, dz - 1, x], (z - dz) * NX + p, v)

    def r_copy(arr, p, d):
        return remote(parts[arr].at[piece(0, p), :], stage.at[arr, d],
                      p_send.at[arr, 1, p], f_recv.at[arr, d], x, v)

    def r_on(arr, d):
        return remote(stage.at[arr, d], lands.at[1, arr, :, cols(x)],
                      f_send.at[arr, d], p_recv.at[arr, 1, x], NX + xpeer(d), v)

    def p_start(dz, p):
        d = lax.rem(p - x + NX, NX)
        for arr in (0, 1):
            if dz == 2:
                around = jnp.logical_and(z == 3, d < 2)

                @pl.when(around)
                def _():
                    r_copy(arr, p, d).start()

                @pl.when(jnp.logical_not(around))
                def _():
                    p_copy(arr, dz, p).start()
            else:
                p_copy(arr, dz, p).start()

    def backward(slot):
        at = slot * CH
        sent = 0
        dol[slot] = (dot_t[...] * maxes[slot, 0:1, :]).T.astype(BF16)
        for k0, kn, q0, qn in BWD_TILES[slot]:
            down, across = slice(at + k0, at + k0 + kn), slice(q0, q0 + qn)
            pb = pbuf[down, across]
            grad = dol[slot, across, :]
            dp = dot(vbuf[down, :], grad, NT)
            ds = (pb.astype(F32) * (dp - sums[slot, 0:1, across])).astype(BF16)
            dk = dot(ds, qbuf[across, :]) * SCALE
            dv = dot(pb, grad)
            dqt[:, across] += dot(kt[:, down], ds)
            if slot == 2:
                sum_k[k0:k0 + kn, :] = dk.astype(BF16)
                sum_v[k0:k0 + kn, :] = dv.astype(BF16)
            else:
                part_k[down, :] = dk.astype(BF16)
                part_v[down, :] = dv.astype(BF16)
                while (sent + 1) * TD <= k0 + kn:
                    p_start(2 - slot, sent)
                    sent += 1

    @pl.when(z >= 2)
    def _():
        backward(0)

    @pl.when(z >= 1)
    def _():
        backward(1)

    out = opart[0] * maxes[0, 0:1, :] + opart[1] * maxes[1, 0:1, :] + opart[2] * maxes[2, 0:1, :]
    obuf[...] = out.T.astype(BF16)
    for d in ORDER[1:]:
        b_copy(0, d).start()
    b_own(0)
    backward(2)
    for arr in (2, 3):
        for d in ORDER[1:]:
            b_copy(arr, d).start()
        b_own(arr)
    dqb[...] = (dqt[...] * SCALE).T.astype(BF16)
    for d in ORDER[1:]:
        b_copy(1, d).start()
    b_own(1)

    @pl.when(z == 0)
    def _():
        for d in range(2):
            for arr in (0, 1):
                landed(stage.at[arr, d], f_recv.at[arr, d])
                r_on(arr, d).start()

    for d in ORDER[1:]:
        b_wait(0, d)
    mixed_ref[...] = (o_in[...].astype(F32) + cross[...]).astype(BF16)

    @pl.when(moves)
    def _():
        landed(latin, gp_recv.at[0])

    lkg_ref[0] = latin[0].astype(F32)
    lvg_ref[0] = latin[1].astype(F32)
    for d in ORDER[1:]:
        b_wait(1, d)
    qg_ref[...] = dq_in[...]

    def p_wait(arr, dz):
        for p in range(NX):
            landed(lands.at[dz - 1, arr, :, pl.ds(p * HD, HD)], p_recv.at[arr, dz - 1, p])

    for arr, out_ in ((0, kg_ref), (1, vg_ref)):
        for d in ORDER[1:]:
            b_wait(arr + 2, d)

        @pl.when(z == 3)
        def _():
            out_[...] = backs[arr + 2][...]

        @pl.when(z == 2)
        def _():
            p_wait(arr, 1)
            out_[...] = (backs[arr + 2][...].astype(F32) + lands[0, arr].astype(F32)).astype(BF16)

        @pl.when(z < 2)
        def _():
            p_wait(arr, 1)
            p_wait(arr, 2)
            out_[...] = (backs[arr + 2][...].astype(F32) + lands[0, arr].astype(F32)
                         + lands[1, arr].astype(F32)).astype(BF16)

    for d in range(1, NX):
        for arr in range(4):
            a_copy(arr, d).wait_send()
            b_copy(arr, d).wait_send()
        for step in range(2):
            c_copy(step, d).wait_send()
        gx_copy(d).wait_send()
        gz_copy(d).wait_send()

    @pl.when(moves)
    def _():
        gp_copy().wait_send()

    for arr in (0, 1):
        for d in range(1, IMAGES):
            l_copy(arr, d).wait_send()
        for dz in (1, 2):
            @pl.when(z + dz < NX)
            def _():
                for i in range(NX):
                    z_copy(arr, dz, i).wait_send()

            @pl.when(z >= dz)
            def _():
                for p in range(NX):
                    p_copy(arr, dz, p).wait_send()

        @pl.when(z == 3)
        def _():
            for i in range(2):
                f_on(arr, i).wait_send()

        @pl.when(z == 0)
        def _():
            for p in range(2):
                r_on(arr, p).wait_send()


def widen(mixed_ref, *refs):
    half = len(refs) // 2
    refs[half][...] = mixed_ref[...]
    for src, dst in zip(refs[:half], refs[half + 1:]):
        dst[...] = src[...].astype(F32)


def shards(query, key, value, doc_ids, cross_query, latent_key, latent_value, token_slot,
           slot_image, cross_gate, out_grad):
    vm = pl.BlockSpec(memory_space=pltpu.VMEM)
    sm = pl.BlockSpec(memory_space=pltpu.SMEM)
    hbm = pl.BlockSpec(memory_space=pl.ANY)
    dma = pltpu.SemaphoreType.DMA

    def low(*shape):
        return pltpu.VMEM(shape, BF16)

    def wide(*shape):
        return pltpu.VMEM(shape, F32)

    scratch = [
        low(NC * CH, HD), low(NC * CH, HD), low(CH, HD), low(CH, HD),
        low(NC, CH, HD), low(HD, NC * CH), low(HD, NC * CH),
        wide(CH, CH), low(NC * CH, CH), wide(NC, HD, CH),
        wide(NC, 8, CH), wide(NC, 8, CH), wide(NC, 8, CH), pltpu.VMEM((8, CH), I32),
        wide(HD, CH), wide(HD, CH),
        wide(8, HD), wide(3, 8, HD), wide(8, HD), wide(3, 8, HD),
        low(TD, WD), low(TD, WD), low(2, 2, TD, HD),
        low(IMAGES, LAT, WD), low(IMAGES, LAT, WD),
        low(SLOTS * LAT, WD), low(SLOTS * LAT, WD),
        wide(SLOTS * LAT, WD), wide(SLOTS * LAT, WD), wide(TD, WD),
        low(NX, NX, 2, LAT, 256), low(3, NX, 2, LAT, 256),
        low(NX, 2, LAT, 256), low(3, 2, LAT, 256), low(2, LAT, 256), low(2, LAT, 256),
        low(CH, HD), low(CH, HD), low(2 * CH, HD), low(2 * CH, HD),
        low(CH, HD), low(CH, HD), low(2, 2, TD, WD),
        low(TD, WD), low(TD, WD), low(TD, WD), low(TD, WD),
        dma((4, 3)), dma((4, 3)),
        dma((2, 2, 4)), dma((2, 2, 4)),
        dma((2, 3)), dma((2, 3)),
        dma((2, 7)), dma((2, 7)),
        dma((3,)), dma((3,)), dma((3,)), dma((3,)), dma((1,)), dma((1,)),
        dma((2, 2, 4)), dma((2, 2, 4)),
        dma((4, 3)), dma((4, 3)),
        dma((2, 2)), dma((2, 2)), dma((8,)),
    ]
    full = jax.ShapeDtypeStruct((TD, WD), F32)
    half = jax.ShapeDtypeStruct((TD, WD), BF16)
    lat = jax.ShapeDtypeStruct((1, LAT, 256), F32)
    results = pl.pallas_call(
        kernel,
        out_shape=(half,) * 5 + (lat, lat),
        in_specs=[vm, vm, sm, vm] + [hbm] * 7,
        out_specs=(vm,) * 7,
        scratch_shapes=scratch,
        cost_estimate=pl.CostEstimate(flops=6_500_000_000, bytes_accessed=8_000_000, transcendentals=4_000_000),
        compiler_params=pltpu.CompilerParams(
            collective_id=0, has_side_effects=True, vmem_limit_bytes=52 * 1024 * 1024),
    )(
        doc_ids, token_slot, slot_image, cross_gate,
        query, key, value, cross_query, out_grad, latent_key, latent_value,
    )
    return pl.pallas_call(
        widen,
        out_shape=(half,) + (full,) * 4 + (lat, lat),
        in_specs=[vm] * 7,
        out_specs=(vm,) * 7,
        cost_estimate=pl.CostEstimate(flops=1_000_000, bytes_accessed=5_000_000, transcendentals=0),
    )(*results)


def solution(mesh):
    own = P("seq", "vis")
    lat_in = P("vis", None, None)
    lat_out = P("vis", None, "seq")
    return jax.shard_map(
        shards,
        mesh=mesh,
        in_specs=(own, own, own, P("seq"), own, lat_in, lat_in, P("seq"), P("seq"), P("vis"), own),
        out_specs=(own, own, own, own, own, lat_out, lat_out),
        check_vma=False,
    )
```

```python
import math

import jax
import jax.numpy as jnp
from jax import lax
from jax.experimental import pallas as pl
from jax.experimental.pallas import tpu as pltpu
from jax.sharding import PartitionSpec as P

HD = 128
TD = 320
NX = 4
CH = TD * NX
NC = 3
TILE = 256
NQ = CH // TILE
LAT = 64
SLOTS = 4
IMAGES = 8
WD = 512
SCALE = 1.0 / math.sqrt(HD)
BIG = -1e30
MESH = pl.DeviceIdType.MESH
F32, BF16, I32 = jnp.float32, jnp.bfloat16, jnp.int32

NT = (((1,), (1,)), ((), ()))
NN = (((1,), (0,)), ((), ()))


def dot(a, b, dims=NN):
    return lax.dot_general(a, b, dims, preferred_element_type=F32)


def fold(a, op):
    return op(a.reshape(a.shape[0] // 8, 8, a.shape[1]), axis=0)


LOG2E = 1.4426950408889634

FWD_TILES = (
    tuple((c * TILE, TILE, 0, (c + 1) * TILE) for c in range(NQ)),
    tuple((c * TILE, TILE, 0, CH) for c in range(NQ)),
    tuple((c * TILE, TILE, c * TILE, CH - c * TILE) for c in range(NQ)),
)
BWD_TILES = (FWD_TILES[0], ((0, CH // 2, 0, CH), (CH // 2, CH // 2, 0, CH)), FWD_TILES[2])
ORDER = (0, 1, 3, 2)


def kernel(
    docs_ref, tok_ref, img_ref, gate_ref, q_ref, k_ref, v_ref, cq_ref, do_ref, lk_ref, lv_ref,
    mixed_ref, qg_ref, kg_ref, vg_ref, cqg_ref, lkg_ref, lvg_ref,
    kbuf, vbuf, qbuf, dobuf, dol, kt, vt, sbuf, pbuf, opart, maxes, sums, dsum, starts, dot_t, dqt,
    cown, cx, crow, cz, cqv, dov, stage,
    latk, latv, lks, lvs, gk, gv, cross, latsend, latx, latz, latin,
    obuf, dqb, part_k, part_v, own_k, own_v, got_k, got_v, sum_k, sum_v,
    o_in, dq_in, dk_in, dv_in,
    a_send, a_recv, z_send, z_recv, c_send, c_recv, l_send, l_recv, gx_send, gx_recv, gz_send, gz_recv,
    p_send, p_recv, b_send, b_recv, f_send, f_recv, own_sem,
):
    s = lax.axis_index("seq")
    v = lax.axis_index("vis")
    x = lax.rem(s, NX)
    z = lax.div(s, NX)
    core = lax.rem(v, 2)

    def xpeer(d):
        return lax.rem(x + d, NX)

    def zpeer(d):
        return lax.rem(z + d, NX)

    def remote(src, dst, ssem, rsem, seq, vis):
        return pltpu.make_async_remote_copy(
            src_ref=src, dst_ref=dst, send_sem=ssem, recv_sem=rsem,
            device_id=(seq, vis), device_id_type=MESH,
        )

    def landed(here, rsem):
        remote(here, here, rsem, rsem, s, v).wait_recv()

    def rows(i, n=TD):
        return pl.ds(pl.multiple_of(i * n, n), n)

    def cols(i, n=HD):
        return pl.ds(pl.multiple_of(i * n, n), n)

    def piece(slot, p):
        return pl.ds(pl.multiple_of(slot * CH + p * TD, TD), TD)

    barrier = pltpu.get_barrier_semaphore()

    def greet(seq, vis):
        pl.semaphore_signal(barrier, inc=1, device_id=(seq, vis), device_id_type=MESH)

    def to_seq(j):
        return 2 * v + j % 2

    def to_vis(j):
        return 2 * x + j // 2

    def stays(j):
        return jnp.logical_and(to_seq(j) == s, to_vis(j) == v)

    def from_seq(i):
        return i * NX + lax.div(v, 2)

    from_vis = lax.div(s, 2)

    def from_self(i):
        return jnp.logical_and(from_seq(i) == s, from_vis == v)

    for d in range(1, NX):
        greet(z * NX + xpeer(d), v)
        greet(zpeer(d) * NX + x, v)
    for d in range(1, IMAGES):
        greet(s, lax.rem(v + d, IMAGES))

    for i in range(NX):
        @pl.when(jnp.logical_not(from_self(i)))
        def _():
            greet(from_seq(i), from_vis)

    def own_copy(i):
        src, dst = (
            (k_ref.at[:, cols(x)], kbuf.at[piece(2, x), :]),
            (v_ref.at[:, cols(x)], vbuf.at[piece(2, x), :]),
            (q_ref.at[:, cols(x)], qbuf.at[piece(0, x), :]),
            (do_ref.at[:, cols(x)], dobuf.at[piece(0, x), :]),
            (lk_ref.at[0, :, cols(v, WD)], latk.at[v]),
            (lv_ref.at[0, :, cols(v, WD)], latv.at[v]),
            (cq_ref, cqv),
            (do_ref, dov),
        )[i]
        return pltpu.make_async_copy(src, dst, own_sem.at[i])

    for i in range(8):
        own_copy(i).start()

    docs = docs_ref[...].reshape(1, TD)
    row_id = lax.broadcasted_iota(I32, (8, HD), 0)
    counts = jnp.zeros((8, HD), F32)
    for d in range(1, 4):
        c = jnp.sum(jnp.where(docs < d, 1.0, 0.0), axis=1, keepdims=True)
        counts = jnp.where(row_id == d, c, counts)
    cown[...] = counts
    pl.semaphore_wait(barrier, 13 + NX - sum(jnp.where(stays(j), 1, 0) for j in range(NX)))

    ins = (k_ref, v_ref, q_ref, do_ref)
    bufs = (kbuf, vbuf, qbuf, dobuf)
    base = (2, 2, 0, 0)

    def a_copy(arr, d):
        p = xpeer(d)
        return remote(ins[arr].at[:, cols(p)], bufs[arr].at[piece(base[arr], x), :],
                      a_send.at[arr, d - 1], a_recv.at[arr, d - 1], z * NX + p, v)

    def a_wait(arr, d):
        landed(bufs[arr].at[piece(base[arr], xpeer(NX - d)), :], a_recv.at[arr, d - 1])

    def c_copy(step, d):
        if step == 0:
            return remote(cown, cx.at[d - 1], c_send.at[0, d - 1], c_recv.at[0, d - 1],
                          z * NX + xpeer(d), v)
        return remote(crow, cz.at[d - 1], c_send.at[1, d - 1], c_recv.at[1, d - 1],
                      zpeer(d) * NX + x, v)

    def z_copy(arr, dz, i):
        p = xpeer(NX - ORDER[i])
        src = ins[arr].at[:, cols(x)] if i == 0 else bufs[arr].at[piece(2, p), :]
        return remote(src, bufs[arr].at[piece(2 - dz, p), :],
                      z_send.at[arr, dz - 1, i], z_recv.at[arr, dz - 1, i], s + dz * NX, v)

    def f_copy(arr, i):
        p = xpeer(NX - ORDER[i])
        src = ins[arr].at[:, cols(x)] if i == 0 else bufs[arr].at[piece(2, p), :]
        return remote(src, stage.at[arr, i], z_send.at[arr, 1, i], f_recv.at[arr, i], s + 3 * NX, v)

    def f_on(arr, i):
        p = xpeer(NX - ORDER[i])
        return remote(stage.at[arr, i], bufs[arr].at[piece(0, p), :],
                      f_send.at[arr, i], z_recv.at[arr, 1, i], s - NX, v)

    def z_start(arr, i):
        if i < 2:
            @pl.when(z == 0)
            def _():
                f_copy(arr, i).start()

            @pl.when(z == 1)
            def _():
                z_copy(arr, 2, i).start()
        else:
            @pl.when(z <= 1)
            def _():
                z_copy(arr, 2, i).start()

        @pl.when(z <= 2)
        def _():
            z_copy(arr, 1, i).start()

    def f_relay(arr):
        @pl.when(z == 3)
        def _():
            for i in range(2):
                landed(stage.at[arr, i], f_recv.at[arr, i])
                f_on(arr, i).start()

    def z_wait(arr, dz):
        for i in range(NX):
            landed(bufs[arr].at[piece(2 - dz, xpeer(NX - ORDER[i])), :], z_recv.at[arr, dz - 1, i])

    def a_start(arr):
        if arr < 2:
            z_start(arr, 0)
        for d in ORDER[1:]:
            a_copy(arr, d).start()

    def a_finish(arr):
        for i in range(1, NX):
            a_wait(arr, ORDER[i])
            if arr < 2:
                z_start(arr, i)

    @pl.when(core == 0)
    def _():
        for arr in (0, 1, 2):
            a_start(arr)

    @pl.when(core == 1)
    def _():
        for arr in (2, 3):
            a_start(arr)

    for d in ORDER[1:]:
        c_copy(0, d).start()

    lins, lbufs = (lk_ref, lv_ref), (latk, latv)

    def l_copy(arr, d):
        p = lax.rem(v + d, IMAGES)
        return remote(lins[arr].at[0, :, cols(p, WD)], lbufs[arr].at[v],
                      l_send.at[arr, d - 1], l_recv.at[arr, d - 1], s, p)

    for arr in (0, 1):
        for d in range(1, IMAGES):
            l_copy(arr, d).start()

    @pl.when(core == 0)
    def _():
        a_finish(0)
        a_finish(1)
        a_start(3)

    @pl.when(core == 1)
    def _():
        a_finish(2)
        a_finish(3)
        a_start(0)
        a_start(1)
        a_finish(0)
        a_finish(1)

    f_relay(0)

    for d in ORDER[1:]:
        landed(cx.at[d - 1], c_recv.at[0, d - 1])
    crow[...] = cown[...] + cx[0] + cx[1] + cx[2]
    for d in range(1, NX):
        c_copy(1, d).start()
    for i in range(8):
        own_copy(i).wait()
    f_relay(1)

    @pl.when(core == 0)
    def _():
        a_finish(2)

    for d in range(1, NX):
        landed(cz.at[d - 1], c_recv.at[1, d - 1])
    before = crow[...] + cz[0] + cz[1] + cz[2]
    pos = lax.broadcasted_iota(I32, (8, CH), 1)
    start = jnp.zeros((8, CH), I32)
    for d in range(1, 4):
        b = before[d:d + 1, 0:1].astype(I32)
        start = jnp.where(b <= pos + z * CH, b, start)
    starts[...] = start - (z - 2) * CH

    for slot in range(NC):
        maxes[slot] = jnp.full((8, CH), BIG, F32)
        sums[slot] = jnp.zeros((8, CH), F32)
        opart[slot] = jnp.zeros((HD, CH), F32)

    def forward(slot):
        at = slot * CH
        kt[:, at:at + CH] = kbuf[at:at + CH, :].T
        vt[:, at:at + CH] = vbuf[at:at + CH, :].T
        for k0, kn, q0, qn in FWD_TILES[slot]:
            across = slice(q0, q0 + qn)
            raw = dot(kbuf[at + k0:at + k0 + kn, :], qbuf[across, :], NT)
            kpos = lax.broadcasted_iota(I32, (kn, qn), 0) + (at + k0)
            kept = kpos >= starts[0:1, across]
            if slot == 2:
                kept = kept & (kpos <= lax.broadcasted_iota(I32, (kn, qn), 1) + (at + q0))
            raw = jnp.where(kept, raw, BIG)
            sbuf[k0:k0 + kn, across] = raw
            maxes[slot, :, across] = jnp.maximum(maxes[slot, :, across], fold(raw, jnp.max))
        top = jnp.max(maxes[slot], axis=0, keepdims=True)
        maxes[slot] = jnp.broadcast_to(top, (8, CH))
        for k0, kn, q0, qn in FWD_TILES[slot]:
            across = slice(q0, q0 + qn)
            p = jnp.exp2((sbuf[k0:k0 + kn, across] - top[:, across]) * (SCALE * LOG2E))
            pb = p.astype(BF16)
            pbuf[at + k0:at + k0 + kn, across] = pb
            sums[slot, :, across] += fold(p, jnp.sum)
            opart[slot, :, across] += dot(vt[:, at + k0:at + k0 + kn], pb)

    def row_sum(slot):
        dsum[slot] = jnp.broadcast_to(jnp.sum(dot_t[...] * opart[slot], axis=0, keepdims=True), (8, CH))

    dsum[0] = jnp.zeros((8, CH), F32)
    dsum[1] = jnp.zeros((8, CH), F32)
    forward(2)

    @pl.when(core == 0)
    def _():
        a_finish(3)

    dot_t[...] = dobuf[...].astype(F32).T
    row_sum(2)

    for arr in (0, 1):
        for d in range(1, IMAGES):
            landed(lbufs[arr].at[lax.rem(v + IMAGES - d, IMAGES)], l_recv.at[arr, d - 1])
    for i in range(SLOTS):
        lks[i * LAT:(i + 1) * LAT, :] = latk[img_ref[i]]
        lvs[i * LAT:(i + 1) * LAT, :] = latv[img_ref[i]]
    slot_of = lax.broadcasted_iota(I32, (SLOTS * LAT, TD), 0) // LAT
    toks = tok_ref[...].reshape(1, TD)
    seen = slot_of == toks
    any_image = toks < SLOTS
    gate = jnp.tanh(gate_ref[...].reshape(1, WD))
    for h in range(NX):
        sl = slice(h * HD, (h + 1) * HD)
        lkh, lvh, cqh = lks[:, sl], lvs[:, sl], cqv[:, sl]
        raw = dot(lkh, cqh, NT)
        raw = jnp.where(seen, raw * SCALE, BIG)
        w = jnp.where(seen, jnp.exp(raw - jnp.max(raw, axis=0, keepdims=True)), 0.0)
        total = jnp.where(any_image, jnp.sum(w, axis=0, keepdims=True), 1.0)
        probs = w / total
        low = probs.astype(BF16)
        cross[:, sl] = gate[:, sl] * dot(lvh.T, low).T
        back = (gate[:, sl] * dov[:, sl].astype(F32)).astype(BF16)
        gp = dot(lvh, back, NT)
        cdot = jnp.sum(probs * gp, axis=0, keepdims=True)
        ds = (probs * (gp - cdot) * SCALE).astype(BF16)
        cqg_ref[:, sl] = dot(lkh.T, ds).T.astype(cqg_ref.dtype)
        gk[:, sl] = dot(ds, cqh).astype(BF16).astype(F32)
        gv[:, sl] = dot(low, back).astype(BF16).astype(F32)

    for m in range(IMAGES):
        for n, g in enumerate((gk, gv)):
            acc = jnp.zeros((LAT, WD), F32)
            for i in range(SLOTS):
                acc = acc + jnp.where(img_ref[i] == m, 1.0, 0.0) * g[i * LAT:(i + 1) * LAT, :]
            acc = acc.astype(BF16)
            for h in range(2):
                latsend[m // 2, (m % 2) * 2 + h, n] = acc[:, h * 256:(h + 1) * 256]

    def gx_copy(d):
        p = xpeer(d)
        return remote(latsend.at[p], latx.at[d - 1], gx_send.at[d - 1], gx_recv.at[d - 1],
                      z * NX + p, v)

    def gz_copy(j):
        return remote(latz.at[j], latin.at[z], gz_send.at[j], gz_recv.at[z], to_seq(j), to_vis(j))

    for d in ORDER[1:]:
        gx_copy(d).start()

    @pl.when(z >= 1)
    def _():
        z_wait(0, 1)
        z_wait(1, 1)
        forward(1)
        row_sum(1)

    @pl.when(z >= 2)
    def _():
        z_wait(0, 2)
        z_wait(1, 2)
        forward(0)
        row_sum(0)

    top = jnp.maximum(jnp.maximum(maxes[0], maxes[1]), maxes[2])
    total = jnp.zeros((1, CH), F32)
    row_dot = jnp.zeros((8, CH), F32)
    for slot in range(NC):
        factor = jnp.exp2((maxes[slot] - top) * (SCALE * LOG2E))
        maxes[slot] = factor
        total = total + jnp.sum(sums[slot], axis=0, keepdims=True) * factor[0:1]
        row_dot = row_dot + dsum[slot] * factor
    inv = 1.0 / total
    row_dot = row_dot * inv
    for slot in range(NC):
        factor = maxes[slot] * inv
        maxes[slot] = factor
        sums[slot] = factor * row_dot
    dqt[...] = jnp.zeros_like(dqt)

    outs = (obuf, dqb, sum_k, sum_v)
    backs = (o_in, dq_in, dk_in, dv_in)

    def b_copy(arr, d):
        p = xpeer(d)
        return remote(outs[arr].at[rows(p), :], backs[arr].at[:, cols(x)],
                      b_send.at[arr, d - 1], b_recv.at[arr, d - 1], z * NX + p, v)

    def b_wait(arr, d):
        landed(backs[arr].at[:, cols(xpeer(NX - d))], b_recv.at[arr, d - 1])

    def b_own(arr):
        backs[arr][:, cols(x)] = outs[arr][rows(x), :]

    parts, gots = (part_k, part_v), (got_k, got_v)

    def p_copy(arr, dz, p):
        return remote(parts[arr].at[pl.ds((2 - dz) * CH + p * TD, TD), :],
                      gots[arr].at[pl.ds((dz - 1) * CH + p * TD, TD), :],
                      p_send.at[arr, dz - 1, p], p_recv.at[arr, dz - 1, p], s - dz * NX, v)

    def r_copy(arr, p):
        return remote(parts[arr].at[pl.ds(p * TD, TD), :], stage.at[arr, p],
                      p_send.at[arr, 1, p], f_recv.at[arr, p], x, v)

    def r_on(arr, p):
        return remote(stage.at[arr, p], gots[arr].at[pl.ds(CH + p * TD, TD), :],
                      f_send.at[arr, p], p_recv.at[arr, 1, p], NX + x, v)

    def p_start(dz, p):
        for arr in (0, 1):
            if dz == 2 and p < 2:
                @pl.when(z == 3)
                def _():
                    r_copy(arr, p).start()

                @pl.when(z == 2)
                def _():
                    p_copy(arr, dz, p).start()
            else:
                p_copy(arr, dz, p).start()

    def backward(slot):
        at = slot * CH
        sent = 0
        dol[slot] = (dot_t[...] * maxes[slot, 0:1, :]).T.astype(BF16)
        for k0, kn, q0, qn in BWD_TILES[slot]:
            down, across = slice(at + k0, at + k0 + kn), slice(q0, q0 + qn)
            pb = pbuf[down, across]
            grad = dol[slot, across, :]
            dp = dot(vbuf[down, :], grad, NT)
            ds = (pb.astype(F32) * (dp - sums[slot, 0:1, across])).astype(BF16)
            dk = dot(ds, qbuf[across, :]) * SCALE
            dv = dot(pb, grad)
            dqt[:, across] += dot(kt[:, down], ds)
            if slot == 2:
                own_k[k0:k0 + kn, :] = dk
                own_v[k0:k0 + kn, :] = dv
            else:
                part_k[down, :] = dk.astype(BF16)
                part_v[down, :] = dv.astype(BF16)
                while (sent + 1) * TD <= k0 + kn:
                    p_start(2 - slot, sent)
                    sent += 1

    @pl.when(z >= 2)
    def _():
        backward(0)

    for d in ORDER[1:]:
        landed(latx.at[d - 1], gx_recv.at[d - 1])
    for j in range(NX):
        for n in range(2):
            acc = latsend[x, j, n].astype(F32)
            for d in range(3):
                acc = acc + latx[d, j, n].astype(F32)
            latz[j, n] = acc.astype(BF16)

        @pl.when(jnp.logical_not(stays(j)))
        def _():
            gz_copy(j).start()

        @pl.when(stays(j))
        def _():
            latin[z] = latz[j]

    @pl.when(z >= 1)
    def _():
        backward(1)

    out = opart[0] * maxes[0, 0:1, :] + opart[1] * maxes[1, 0:1, :] + opart[2] * maxes[2, 0:1, :]
    obuf[...] = out.T.astype(BF16)
    for d in ORDER[1:]:
        b_copy(0, d).start()
    b_own(0)
    backward(2)
    dqb[...] = (dqt[...] * SCALE).T.astype(BF16)
    for d in ORDER[1:]:
        b_copy(1, d).start()
    b_own(1)

    @pl.when(z == 0)
    def _():
        for p in range(2):
            for arr in (0, 1):
                landed(stage.at[arr, p], f_recv.at[arr, p])
                r_on(arr, p).start()

    def p_wait(arr, dz, p):
        here = gots[arr].at[pl.ds((dz - 1) * CH + p * TD, TD), :]
        landed(here, p_recv.at[arr, dz - 1, p])
        return here

    for p in range(NX):
        sl = slice(p * TD, (p + 1) * TD)
        for arr, (own, out_) in enumerate(((own_k, sum_k), (own_v, sum_v))):
            for dz in (2, 1):
                @pl.when(z + dz < NX)
                def _():
                    here = p_wait(arr, dz, p)
                    own[sl, :] += here[...].astype(F32)
            out_[sl, :] = own[sl, :].astype(BF16)

            @pl.when(x != p)
            def _():
                d = lax.rem(p - x + NX, NX)
                remote(out_.at[sl, :], backs[arr + 2].at[:, cols(x)],
                       b_send.at[arr + 2, d - 1], b_recv.at[arr + 2, d - 1], z * NX + p, v).start()

    for d in ORDER[1:]:
        b_wait(0, d)
    mixed_ref[...] = (o_in[...].astype(F32) + cross[...]).astype(BF16)

    for i in range(NX):
        @pl.when(jnp.logical_not(from_self(i)))
        def _():
            landed(latin.at[i], gz_recv.at[i])

    for n, g in enumerate((lkg_ref, lvg_ref)):
        acc = latin[0, n].astype(F32)
        for i in range(1, NX):
            acc = acc + latin[i, n].astype(F32)
        g[0] = acc
    for d in ORDER[1:]:
        b_wait(1, d)
    qg_ref[...] = dq_in[...]

    for arr, out_ in ((2, kg_ref), (3, vg_ref)):
        b_own(arr)
        for d in ORDER[1:]:
            b_wait(arr, d)
        out_[...] = backs[arr][...]

    for d in range(1, NX):
        for arr in range(4):
            a_copy(arr, d).wait_send()
            b_copy(arr, d).wait_send()
        for step in range(2):
            c_copy(step, d).wait_send()
        gx_copy(d).wait_send()

    for j in range(NX):
        @pl.when(jnp.logical_not(stays(j)))
        def _():
            gz_copy(j).wait_send()

    for arr in (0, 1):
        for d in range(1, IMAGES):
            l_copy(arr, d).wait_send()
        for dz in (1, 2):
            @pl.when(z + dz < NX)
            def _():
                for i in range(NX):
                    z_copy(arr, dz, i).wait_send()

            @pl.when(z >= dz)
            def _():
                for p in range(NX):
                    p_copy(arr, dz, p).wait_send()

        @pl.when(z == 3)
        def _():
            for i in range(2):
                f_on(arr, i).wait_send()

        @pl.when(z == 0)
        def _():
            for p in range(2):
                r_on(arr, p).wait_send()


def widen(mixed_ref, *refs):
    half = len(refs) // 2
    refs[half][...] = mixed_ref[...]
    for src, dst in zip(refs[:half], refs[half + 1:]):
        dst[...] = src[...].astype(F32)


def shards(query, key, value, doc_ids, cross_query, latent_key, latent_value, token_slot,
           slot_image, cross_gate, out_grad):
    vm = pl.BlockSpec(memory_space=pltpu.VMEM)
    sm = pl.BlockSpec(memory_space=pltpu.SMEM)
    hbm = pl.BlockSpec(memory_space=pl.ANY)
    dma = pltpu.SemaphoreType.DMA

    def low(*shape):
        return pltpu.VMEM(shape, BF16)

    def wide(*shape):
        return pltpu.VMEM(shape, F32)

    scratch = [
        low(NC * CH, HD), low(NC * CH, HD), low(CH, HD), low(CH, HD),
        low(NC, CH, HD), low(HD, NC * CH), low(HD, NC * CH),
        wide(CH, CH), low(NC * CH, CH), wide(NC, HD, CH),
        wide(NC, 8, CH), wide(NC, 8, CH), wide(NC, 8, CH), pltpu.VMEM((8, CH), I32),
        wide(HD, CH), wide(HD, CH),
        wide(8, HD), wide(3, 8, HD), wide(8, HD), wide(3, 8, HD),
        low(TD, WD), low(TD, WD), low(2, 2, TD, HD),
        low(IMAGES, LAT, WD), low(IMAGES, LAT, WD),
        low(SLOTS * LAT, WD), low(SLOTS * LAT, WD),
        wide(SLOTS * LAT, WD), wide(SLOTS * LAT, WD), wide(TD, WD),
        low(NX, NX, 2, LAT, 256), low(3, NX, 2, LAT, 256),
        low(NX, 2, LAT, 256), low(NX, 2, LAT, 256),
        low(CH, HD), low(CH, HD), low(2 * CH, HD), low(2 * CH, HD),
        wide(CH, HD), wide(CH, HD), low(2 * CH, HD), low(2 * CH, HD),
        low(CH, HD), low(CH, HD),
        low(TD, WD), low(TD, WD), low(TD, WD), low(TD, WD),
        dma((4, 3)), dma((4, 3)),
        dma((2, 2, 4)), dma((2, 2, 4)),
        dma((2, 3)), dma((2, 3)),
        dma((2, 7)), dma((2, 7)),
        dma((3,)), dma((3,)), dma((4,)), dma((4,)),
        dma((2, 2, 4)), dma((2, 2, 4)),
        dma((4, 3)), dma((4, 3)),
        dma((2, 2)), dma((2, 2)), dma((8,)),
    ]
    full = jax.ShapeDtypeStruct((TD, WD), F32)
    half = jax.ShapeDtypeStruct((TD, WD), BF16)
    lat = jax.ShapeDtypeStruct((1, LAT, 256), F32)
    results = pl.pallas_call(
        kernel,
        out_shape=(half,) * 5 + (lat, lat),
        in_specs=[vm, vm, sm, vm] + [hbm] * 7,
        out_specs=(vm,) * 7,
        scratch_shapes=scratch,
        cost_estimate=pl.CostEstimate(flops=6_500_000_000, bytes_accessed=8_000_000, transcendentals=4_000_000),
        compiler_params=pltpu.CompilerParams(
            collective_id=0, has_side_effects=True, vmem_limit_bytes=58 * 1024 * 1024),
    )(
        doc_ids, token_slot, slot_image, cross_gate,
        query, key, value, cross_query, out_grad, latent_key, latent_value,
    )
    return pl.pallas_call(
        widen,
        out_shape=(half,) + (full,) * 4 + (lat, lat),
        in_specs=[vm] * 7,
        out_specs=(vm,) * 7,
        cost_estimate=pl.CostEstimate(flops=1_000_000, bytes_accessed=5_000_000, transcendentals=0),
    )(*results)


def solution(mesh):
    own = P("seq", "vis")
    lat_in = P("vis", None, None)
    lat_out = P("vis", None, "seq")
    return jax.shard_map(
        shards,
        mesh=mesh,
        in_specs=(own, own, own, P("seq"), own, lat_in, lat_in, P("seq"), P("seq"), P("vis"), own),
        out_specs=(own, own, own, own, own, lat_out, lat_out),
        check_vma=False,
    )
```

```python
import math

import jax
import jax.numpy as jnp
from jax import lax
from jax.experimental import pallas as pl
from jax.experimental.pallas import tpu as pltpu
from jax.sharding import PartitionSpec as P

HD = 128
TD = 320
NX = 4
CH = TD * NX
NC = 3
TILE = 256
NQ = CH // TILE
LAT = 64
SLOTS = 4
IMAGES = 8
WD = 512
SCALE = 1.0 / math.sqrt(HD)
BIG = -1e30
MESH = pl.DeviceIdType.MESH
F32, BF16, I32 = jnp.float32, jnp.bfloat16, jnp.int32

NT = (((1,), (1,)), ((), ()))
NN = (((1,), (0,)), ((), ()))


def dot(a, b, dims=NN):
    return lax.dot_general(a, b, dims, preferred_element_type=F32)


def fold(a, op):
    return op(a.reshape(a.shape[0] // 8, 8, a.shape[1]), axis=0)


LOG2E = 1.4426950408889634

FWD_TILES = (
    tuple((c * TILE, TILE, 0, (c + 1) * TILE) for c in range(NQ)),
    tuple((c * TILE, TILE, 0, CH) for c in range(NQ)),
    tuple((c * TILE, TILE, c * TILE, CH - c * TILE) for c in range(NQ)),
)
BWD_TILES = (FWD_TILES[0], ((0, CH // 2, 0, CH), (CH // 2, CH // 2, 0, CH)), FWD_TILES[2])
ORDER = (0, 1, 3, 2)


def kernel(
    docs_ref, tok_ref, img_ref, gate_ref, q_ref, k_ref, v_ref, cq_ref, do_ref, lk_ref, lv_ref,
    mixed_ref, qg_ref, kg_ref, vg_ref, cqg_ref, lkg_ref, lvg_ref,
    kbuf, vbuf, qbuf, dobuf, dol, kt, vt, sbuf, pbuf, opart, maxes, sums, dsum, starts, dot_t, dqt,
    cown, cx, crow, cz, cqv, dov, stage,
    latk, latv, lks, lvs, gk, gv, cross, latsend, latx, latz, latin,
    obuf, dqb, part_k, part_v, own_k, own_v, got_k, got_v, sum_k, sum_v,
    o_in, dq_in, dk_in, dv_in,
    a_send, a_recv, z_send, z_recv, c_send, c_recv, l_send, l_recv, gx_send, gx_recv, gz_send, gz_recv,
    p_send, p_recv, b_send, b_recv, f_send, f_recv, own_sem, gates,
):
    s = lax.axis_index("seq")
    v = lax.axis_index("vis")
    x = lax.rem(s, NX)
    z = lax.div(s, NX)
    core = lax.rem(v, 2)

    def xpeer(d):
        return lax.rem(x + d, NX)

    def zpeer(d):
        return lax.rem(z + d, NX)

    def remote(src, dst, ssem, rsem, seq, vis):
        return pltpu.make_async_remote_copy(
            src_ref=src, dst_ref=dst, send_sem=ssem, recv_sem=rsem,
            device_id=(seq, vis), device_id_type=MESH,
        )

    def landed(here, rsem):
        remote(here, here, rsem, rsem, s, v).wait_recv()

    def rows(i, n=TD):
        return pl.ds(pl.multiple_of(i * n, n), n)

    def cols(i, n=HD):
        return pl.ds(pl.multiple_of(i * n, n), n)

    def piece(slot, p):
        return pl.ds(pl.multiple_of(slot * CH + p * TD, TD), TD)

    barrier = pltpu.get_barrier_semaphore()

    def greet(seq, vis):
        pl.semaphore_signal(barrier, inc=1, device_id=(seq, vis), device_id_type=MESH)

    def to_seq(j):
        return 2 * v + j % 2

    def to_vis(j):
        return 2 * x + j // 2

    def stays(j):
        return jnp.logical_and(to_seq(j) == s, to_vis(j) == v)

    def from_seq(i):
        return i * NX + lax.div(v, 2)

    from_vis = lax.div(s, 2)

    def from_self(i):
        return jnp.logical_and(from_seq(i) == s, from_vis == v)

    for d in range(1, NX):
        greet(z * NX + xpeer(d), v)
        greet(zpeer(d) * NX + x, v)
    for d in range(1, IMAGES):
        greet(s, lax.rem(v + d, IMAGES))

    for i in range(NX):
        @pl.when(jnp.logical_not(from_self(i)))
        def _():
            greet(from_seq(i), from_vis)

    def own_copy(i):
        src, dst = (
            (k_ref.at[:, cols(x)], kbuf.at[piece(2, x), :]),
            (v_ref.at[:, cols(x)], vbuf.at[piece(2, x), :]),
            (q_ref.at[:, cols(x)], qbuf.at[piece(0, x), :]),
            (do_ref.at[:, cols(x)], dobuf.at[piece(0, x), :]),
            (lk_ref.at[0, :, cols(v, WD)], latk.at[v]),
            (lv_ref.at[0, :, cols(v, WD)], latv.at[v]),
            (cq_ref, cqv),
            (do_ref, dov),
        )[i]
        return pltpu.make_async_copy(src, dst, own_sem.at[i])

    for i in range(8):
        own_copy(i).start()

    docs = docs_ref[...].reshape(1, TD)
    row_id = lax.broadcasted_iota(I32, (8, HD), 0)
    counts = jnp.zeros((8, HD), F32)
    for d in range(1, 4):
        c = jnp.sum(jnp.where(docs < d, 1.0, 0.0), axis=1, keepdims=True)
        counts = jnp.where(row_id == d, c, counts)
    cown[...] = counts
    pl.semaphore_wait(barrier, 13 + NX - sum(jnp.where(stays(j), 1, 0) for j in range(NX)))

    ins = (k_ref, v_ref, q_ref, do_ref)
    bufs = (kbuf, vbuf, qbuf, dobuf)
    base = (2, 2, 0, 0)

    def a_copy(arr, d):
        p = xpeer(d)
        return remote(ins[arr].at[:, cols(p)], bufs[arr].at[piece(base[arr], x), :],
                      a_send.at[arr, d - 1], a_recv.at[arr, d - 1], z * NX + p, v)

    def a_wait(arr, d):
        landed(bufs[arr].at[piece(base[arr], xpeer(NX - d)), :], a_recv.at[arr, d - 1])

    def c_copy(step, d):
        if step == 0:
            return remote(cown, cx.at[d - 1], c_send.at[0, d - 1], c_recv.at[0, d - 1],
                          z * NX + xpeer(d), v)
        return remote(crow, cz.at[d - 1], c_send.at[1, d - 1], c_recv.at[1, d - 1],
                      zpeer(d) * NX + x, v)

    def z_copy(arr, dz, i):
        p = xpeer(NX - ORDER[i])
        src = ins[arr].at[:, cols(x)] if i == 0 else bufs[arr].at[piece(2, p), :]
        return remote(src, bufs[arr].at[piece(2 - dz, p), :],
                      z_send.at[arr, dz - 1, i], z_recv.at[arr, dz - 1, i], s + dz * NX, v)

    def f_copy(arr, i):
        p = xpeer(NX - ORDER[i])
        src = ins[arr].at[:, cols(x)] if i == 0 else bufs[arr].at[piece(2, p), :]
        return remote(src, stage.at[arr, i], z_send.at[arr, 1, i], f_recv.at[arr, i], s + 3 * NX, v)

    def f_on(arr, i):
        p = xpeer(NX - ORDER[i])
        return remote(stage.at[arr, i], bufs[arr].at[piece(0, p), :],
                      f_send.at[arr, i], z_recv.at[arr, 1, i], s - NX, v)

    def z_start(arr, i):
        if i < 2:
            @pl.when(z == 0)
            def _():
                f_copy(arr, i).start()

            @pl.when(z == 1)
            def _():
                z_copy(arr, 2, i).start()
        else:
            @pl.when(z <= 1)
            def _():
                z_copy(arr, 2, i).start()

        @pl.when(z <= 2)
        def _():
            z_copy(arr, 1, i).start()

    def f_relay(arr):
        @pl.when(z == 3)
        def _():
            for i in range(2):
                landed(stage.at[arr, i], f_recv.at[arr, i])
                f_on(arr, i).start()

    def z_sent(arr):
        for dz in (1, 2):
            @pl.when(z + dz < NX)
            def _():
                for i in range(NX):
                    z_copy(arr, dz, i).wait_send()

    def z_wait(arr, dz):
        for i in range(NX):
            landed(bufs[arr].at[piece(2 - dz, xpeer(NX - ORDER[i])), :], z_recv.at[arr, dz - 1, i])

    def a_start(arr):
        for d in ORDER[1:]:
            a_copy(arr, d).start()

    def a_finish(arr):
        for d in ORDER[1:]:
            a_wait(arr, d)

    def open_gate(n):
        pl.semaphore_signal(gates.at[n], inc=1, device_id=(s, v + 1), device_id_type=MESH)

    @pl.when(core == 0)
    def _():
        for arr in (0, 1):
            z_start(arr, 0)
            a_start(arr)

    @pl.when(core == 1)
    def _():
        for arr in (0, 1):
            z_start(arr, 0)

    for d in ORDER[1:]:
        c_copy(0, d).start()

    lins, lbufs = (lk_ref, lv_ref), (latk, latv)

    def l_copy(arr, d):
        p = lax.rem(v + d, IMAGES)
        return remote(lins[arr].at[0, :, cols(p, WD)], lbufs[arr].at[v],
                      l_send.at[arr, d - 1], l_recv.at[arr, d - 1], s, p)

    for arr in (0, 1):
        for d in range(1, IMAGES):
            l_copy(arr, d).start()

    @pl.when(core == 0)
    def _():
        for arr in (0, 1):
            for i in range(1, NX):
                a_wait(arr, ORDER[i])
                z_start(arr, i)
        open_gate(0)
        a_start(2)
        a_start(3)
        f_relay(0)
        f_relay(1)
        z_sent(0)
        open_gate(1)

    @pl.when(core == 1)
    def _():
        pl.semaphore_wait(gates.at[0], 1)
        for arr in (0, 1):
            a_start(arr)
        for arr in (0, 1):
            a_finish(arr)
        a_start(2)
        a_start(3)
        pl.semaphore_wait(gates.at[1], 1)
        for arr in (0, 1):
            for i in range(1, NX):
                z_start(arr, i)

    for d in ORDER[1:]:
        landed(cx.at[d - 1], c_recv.at[0, d - 1])
    crow[...] = cown[...] + cx[0] + cx[1] + cx[2]
    for d in range(1, NX):
        c_copy(1, d).start()
    for i in range(8):
        own_copy(i).wait()
    a_finish(2)
    for d in range(1, NX):
        landed(cz.at[d - 1], c_recv.at[1, d - 1])
    before = crow[...] + cz[0] + cz[1] + cz[2]
    pos = lax.broadcasted_iota(I32, (8, CH), 1)
    start = jnp.zeros((8, CH), I32)
    for d in range(1, 4):
        b = before[d:d + 1, 0:1].astype(I32)
        start = jnp.where(b <= pos + z * CH, b, start)
    starts[...] = start - (z - 2) * CH

    for slot in range(NC):
        maxes[slot] = jnp.full((8, CH), BIG, F32)
        sums[slot] = jnp.zeros((8, CH), F32)
        opart[slot] = jnp.zeros((HD, CH), F32)

    def forward(slot):
        at = slot * CH
        kt[:, at:at + CH] = kbuf[at:at + CH, :].T
        vt[:, at:at + CH] = vbuf[at:at + CH, :].T
        for k0, kn, q0, qn in FWD_TILES[slot]:
            across = slice(q0, q0 + qn)
            raw = dot(kbuf[at + k0:at + k0 + kn, :], qbuf[across, :], NT)
            kpos = lax.broadcasted_iota(I32, (kn, qn), 0) + (at + k0)
            kept = kpos >= starts[0:1, across]
            if slot == 2:
                kept = kept & (kpos <= lax.broadcasted_iota(I32, (kn, qn), 1) + (at + q0))
            raw = jnp.where(kept, raw, BIG)
            sbuf[k0:k0 + kn, across] = raw
            maxes[slot, :, across] = jnp.maximum(maxes[slot, :, across], fold(raw, jnp.max))
        top = jnp.max(maxes[slot], axis=0, keepdims=True)
        maxes[slot] = jnp.broadcast_to(top, (8, CH))
        for k0, kn, q0, qn in FWD_TILES[slot]:
            across = slice(q0, q0 + qn)
            p = jnp.exp2((sbuf[k0:k0 + kn, across] - top[:, across]) * (SCALE * LOG2E))
            pb = p.astype(BF16)
            pbuf[at + k0:at + k0 + kn, across] = pb
            sums[slot, :, across] += fold(p, jnp.sum)
            opart[slot, :, across] += dot(vt[:, at + k0:at + k0 + kn], pb)

    def row_sum(slot):
        dsum[slot] = jnp.broadcast_to(jnp.sum(dot_t[...] * opart[slot], axis=0, keepdims=True), (8, CH))

    dsum[0] = jnp.zeros((8, CH), F32)
    dsum[1] = jnp.zeros((8, CH), F32)
    forward(2)

    @pl.when(core == 1)
    def _():
        f_relay(0)
        f_relay(1)

    a_finish(3)
    dot_t[...] = dobuf[...].astype(F32).T
    row_sum(2)

    for arr in (0, 1):
        for d in range(1, IMAGES):
            landed(lbufs[arr].at[lax.rem(v + IMAGES - d, IMAGES)], l_recv.at[arr, d - 1])
    for i in range(SLOTS):
        lks[i * LAT:(i + 1) * LAT, :] = latk[img_ref[i]]
        lvs[i * LAT:(i + 1) * LAT, :] = latv[img_ref[i]]
    slot_of = lax.broadcasted_iota(I32, (SLOTS * LAT, TD), 0) // LAT
    toks = tok_ref[...].reshape(1, TD)
    seen = slot_of == toks
    any_image = toks < SLOTS
    gate = jnp.tanh(gate_ref[...].reshape(1, WD))
    for h in range(NX):
        sl = slice(h * HD, (h + 1) * HD)
        lkh, lvh, cqh = lks[:, sl], lvs[:, sl], cqv[:, sl]
        raw = dot(lkh, cqh, NT)
        raw = jnp.where(seen, raw * SCALE, BIG)
        w = jnp.where(seen, jnp.exp(raw - jnp.max(raw, axis=0, keepdims=True)), 0.0)
        total = jnp.where(any_image, jnp.sum(w, axis=0, keepdims=True), 1.0)
        probs = w / total
        low = probs.astype(BF16)
        cross[:, sl] = gate[:, sl] * dot(lvh.T, low).T
        back = (gate[:, sl] * dov[:, sl].astype(F32)).astype(BF16)
        gp = dot(lvh, back, NT)
        cdot = jnp.sum(probs * gp, axis=0, keepdims=True)
        ds = (probs * (gp - cdot) * SCALE).astype(BF16)
        cqg_ref[:, sl] = dot(lkh.T, ds).T.astype(cqg_ref.dtype)
        gk[:, sl] = dot(ds, cqh).astype(BF16).astype(F32)
        gv[:, sl] = dot(low, back).astype(BF16).astype(F32)

    for m in range(IMAGES):
        for n, g in enumerate((gk, gv)):
            acc = jnp.zeros((LAT, WD), F32)
            for i in range(SLOTS):
                acc = acc + jnp.where(img_ref[i] == m, 1.0, 0.0) * g[i * LAT:(i + 1) * LAT, :]
            acc = acc.astype(BF16)
            for h in range(2):
                latsend[m // 2, (m % 2) * 2 + h, n] = acc[:, h * 256:(h + 1) * 256]

    def gx_copy(d):
        p = xpeer(d)
        return remote(latsend.at[p], latx.at[d - 1], gx_send.at[d - 1], gx_recv.at[d - 1],
                      z * NX + p, v)

    def gz_copy(j):
        return remote(latz.at[j], latin.at[z], gz_send.at[j], gz_recv.at[z], to_seq(j), to_vis(j))

    for d in ORDER[1:]:
        gx_copy(d).start()

    @pl.when(z >= 1)
    def _():
        z_wait(0, 1)
        z_wait(1, 1)
        forward(1)
        row_sum(1)

    @pl.when(z >= 2)
    def _():
        z_wait(0, 2)
        z_wait(1, 2)
        forward(0)
        row_sum(0)

    top = jnp.maximum(jnp.maximum(maxes[0], maxes[1]), maxes[2])
    total = jnp.zeros((1, CH), F32)
    row_dot = jnp.zeros((8, CH), F32)
    for slot in range(NC):
        factor = jnp.exp2((maxes[slot] - top) * (SCALE * LOG2E))
        maxes[slot] = factor
        total = total + jnp.sum(sums[slot], axis=0, keepdims=True) * factor[0:1]
        row_dot = row_dot + dsum[slot] * factor
    inv = 1.0 / total
    row_dot = row_dot * inv
    for slot in range(NC):
        factor = maxes[slot] * inv
        maxes[slot] = factor
        sums[slot] = factor * row_dot
    dqt[...] = jnp.zeros_like(dqt)

    outs = (obuf, dqb, sum_k, sum_v)
    backs = (o_in, dq_in, dk_in, dv_in)

    def b_copy(arr, d):
        p = xpeer(d)
        return remote(outs[arr].at[rows(p), :], backs[arr].at[:, cols(x)],
                      b_send.at[arr, d - 1], b_recv.at[arr, d - 1], z * NX + p, v)

    def b_wait(arr, d):
        landed(backs[arr].at[:, cols(xpeer(NX - d))], b_recv.at[arr, d - 1])

    def b_own(arr):
        backs[arr][:, cols(x)] = outs[arr][rows(x), :]

    parts, gots = (part_k, part_v), (got_k, got_v)

    def p_copy(arr, dz, p):
        return remote(parts[arr].at[pl.ds((2 - dz) * CH + p * TD, TD), :],
                      gots[arr].at[pl.ds((dz - 1) * CH + p * TD, TD), :],
                      p_send.at[arr, dz - 1, p], p_recv.at[arr, dz - 1, p], s - dz * NX, v)

    def r_copy(arr, p):
        return remote(parts[arr].at[pl.ds(p * TD, TD), :], stage.at[arr, p],
                      p_send.at[arr, 1, p], f_recv.at[arr, p], x, v)

    def r_on(arr, p):
        return remote(stage.at[arr, p], gots[arr].at[pl.ds(CH + p * TD, TD), :],
                      f_send.at[arr, p], p_recv.at[arr, 1, p], NX + x, v)

    def p_start(dz, p):
        for arr in (0, 1):
            if dz == 2 and p < 2:
                @pl.when(z == 3)
                def _():
                    r_copy(arr, p).start()

                @pl.when(z == 2)
                def _():
                    p_copy(arr, dz, p).start()
            else:
                p_copy(arr, dz, p).start()

    def backward(slot):
        at = slot * CH
        sent = 0
        dol[slot] = (dot_t[...] * maxes[slot, 0:1, :]).T.astype(BF16)
        for k0, kn, q0, qn in BWD_TILES[slot]:
            down, across = slice(at + k0, at + k0 + kn), slice(q0, q0 + qn)
            pb = pbuf[down, across]
            grad = dol[slot, across, :]
            dp = dot(vbuf[down, :], grad, NT)
            ds = (pb.astype(F32) * (dp - sums[slot, 0:1, across])).astype(BF16)
            dk = dot(ds, qbuf[across, :]) * SCALE
            dv = dot(pb, grad)
            dqt[:, across] += dot(kt[:, down], ds)
            if slot == 2:
                own_k[k0:k0 + kn, :] = dk
                own_v[k0:k0 + kn, :] = dv
            else:
                part_k[down, :] = dk.astype(BF16)
                part_v[down, :] = dv.astype(BF16)
                while (sent + 1) * TD <= k0 + kn:
                    p_start(2 - slot, sent)
                    sent += 1

    @pl.when(z >= 2)
    def _():
        backward(0)

    for d in ORDER[1:]:
        landed(latx.at[d - 1], gx_recv.at[d - 1])
    for j in range(NX):
        for n in range(2):
            acc = latsend[x, j, n].astype(F32)
            for d in range(3):
                acc = acc + latx[d, j, n].astype(F32)
            latz[j, n] = acc.astype(BF16)

        @pl.when(jnp.logical_not(stays(j)))
        def _():
            gz_copy(j).start()

        @pl.when(stays(j))
        def _():
            latin[z] = latz[j]

    @pl.when(z >= 1)
    def _():
        backward(1)

    out = opart[0] * maxes[0, 0:1, :] + opart[1] * maxes[1, 0:1, :] + opart[2] * maxes[2, 0:1, :]
    obuf[...] = out.T.astype(BF16)
    for d in ORDER[1:]:
        b_copy(0, d).start()
    b_own(0)
    backward(2)
    dqb[...] = (dqt[...] * SCALE).T.astype(BF16)
    for d in ORDER[1:]:
        b_copy(1, d).start()
    b_own(1)

    @pl.when(z == 0)
    def _():
        for p in range(2):
            for arr in (0, 1):
                landed(stage.at[arr, p], f_recv.at[arr, p])
                r_on(arr, p).start()

    def p_wait(arr, dz, p):
        here = gots[arr].at[pl.ds((dz - 1) * CH + p * TD, TD), :]
        landed(here, p_recv.at[arr, dz - 1, p])
        return here

    for p in range(NX):
        sl = slice(p * TD, (p + 1) * TD)
        for arr, (own, out_) in enumerate(((own_k, sum_k), (own_v, sum_v))):
            for dz in (2, 1):
                @pl.when(z + dz < NX)
                def _():
                    here = p_wait(arr, dz, p)
                    own[sl, :] += here[...].astype(F32)
            out_[sl, :] = own[sl, :].astype(BF16)

            @pl.when(x != p)
            def _():
                d = lax.rem(p - x + NX, NX)
                remote(out_.at[sl, :], backs[arr + 2].at[:, cols(x)],
                       b_send.at[arr + 2, d - 1], b_recv.at[arr + 2, d - 1], z * NX + p, v).start()

    for d in ORDER[1:]:
        b_wait(0, d)
    mixed_ref[...] = (o_in[...].astype(F32) + cross[...]).astype(BF16)

    for i in range(NX):
        @pl.when(jnp.logical_not(from_self(i)))
        def _():
            landed(latin.at[i], gz_recv.at[i])

    for n, g in enumerate((lkg_ref, lvg_ref)):
        acc = latin[0, n].astype(F32)
        for i in range(1, NX):
            acc = acc + latin[i, n].astype(F32)
        g[0] = acc
    for d in ORDER[1:]:
        b_wait(1, d)
    qg_ref[...] = dq_in[...]

    for arr, out_ in ((2, kg_ref), (3, vg_ref)):
        b_own(arr)
        for d in ORDER[1:]:
            b_wait(arr, d)
        out_[...] = backs[arr][...]

    for d in range(1, NX):
        for arr in range(4):
            a_copy(arr, d).wait_send()
            b_copy(arr, d).wait_send()
        for step in range(2):
            c_copy(step, d).wait_send()
        gx_copy(d).wait_send()

    for j in range(NX):
        @pl.when(jnp.logical_not(stays(j)))
        def _():
            gz_copy(j).wait_send()

    @pl.when(core == 1)
    def _():
        z_sent(0)

    z_sent(1)
    for arr in (0, 1):
        for d in range(1, IMAGES):
            l_copy(arr, d).wait_send()
        for dz in (1, 2):
            @pl.when(z >= dz)
            def _():
                for p in range(NX):
                    p_copy(arr, dz, p).wait_send()

        @pl.when(z == 3)
        def _():
            for i in range(2):
                f_on(arr, i).wait_send()

        @pl.when(z == 0)
        def _():
            for p in range(2):
                r_on(arr, p).wait_send()


def widen(mixed_ref, *refs):
    half = len(refs) // 2
    refs[half][...] = mixed_ref[...]
    for src, dst in zip(refs[:half], refs[half + 1:]):
        dst[...] = src[...].astype(F32)


def shards(query, key, value, doc_ids, cross_query, latent_key, latent_value, token_slot,
           slot_image, cross_gate, out_grad):
    vm = pl.BlockSpec(memory_space=pltpu.VMEM)
    sm = pl.BlockSpec(memory_space=pltpu.SMEM)
    hbm = pl.BlockSpec(memory_space=pl.ANY)
    dma = pltpu.SemaphoreType.DMA

    def low(*shape):
        return pltpu.VMEM(shape, BF16)

    def wide(*shape):
        return pltpu.VMEM(shape, F32)

    scratch = [
        low(NC * CH, HD), low(NC * CH, HD), low(CH, HD), low(CH, HD),
        low(NC, CH, HD), low(HD, NC * CH), low(HD, NC * CH),
        wide(CH, CH), low(NC * CH, CH), wide(NC, HD, CH),
        wide(NC, 8, CH), wide(NC, 8, CH), wide(NC, 8, CH), pltpu.VMEM((8, CH), I32),
        wide(HD, CH), wide(HD, CH),
        wide(8, HD), wide(3, 8, HD), wide(8, HD), wide(3, 8, HD),
        low(TD, WD), low(TD, WD), low(2, 2, TD, HD),
        low(IMAGES, LAT, WD), low(IMAGES, LAT, WD),
        low(SLOTS * LAT, WD), low(SLOTS * LAT, WD),
        wide(SLOTS * LAT, WD), wide(SLOTS * LAT, WD), wide(TD, WD),
        low(NX, NX, 2, LAT, 256), low(3, NX, 2, LAT, 256),
        low(NX, 2, LAT, 256), low(NX, 2, LAT, 256),
        low(CH, HD), low(CH, HD), low(2 * CH, HD), low(2 * CH, HD),
        wide(CH, HD), wide(CH, HD), low(2 * CH, HD), low(2 * CH, HD),
        low(CH, HD), low(CH, HD),
        low(TD, WD), low(TD, WD), low(TD, WD), low(TD, WD),
        dma((4, 3)), dma((4, 3)),
        dma((2, 2, 4)), dma((2, 2, 4)),
        dma((2, 3)), dma((2, 3)),
        dma((2, 7)), dma((2, 7)),
        dma((3,)), dma((3,)), dma((4,)), dma((4,)),
        dma((2, 2, 4)), dma((2, 2, 4)),
        dma((4, 3)), dma((4, 3)),
        dma((2, 2)), dma((2, 2)), dma((8,)), pltpu.SemaphoreType.REGULAR((2,)),
    ]
    full = jax.ShapeDtypeStruct((TD, WD), F32)
    half = jax.ShapeDtypeStruct((TD, WD), BF16)
    lat = jax.ShapeDtypeStruct((1, LAT, 256), F32)
    results = pl.pallas_call(
        kernel,
        out_shape=(half,) * 5 + (lat, lat),
        in_specs=[vm, vm, sm, vm] + [hbm] * 7,
        out_specs=(vm,) * 7,
        scratch_shapes=scratch,
        cost_estimate=pl.CostEstimate(flops=6_500_000_000, bytes_accessed=8_000_000, transcendentals=4_000_000),
        compiler_params=pltpu.CompilerParams(
            collective_id=0, has_side_effects=True, vmem_limit_bytes=58 * 1024 * 1024),
    )(
        doc_ids, token_slot, slot_image, cross_gate,
        query, key, value, cross_query, out_grad, latent_key, latent_value,
    )
    return pl.pallas_call(
        widen,
        out_shape=(half,) + (full,) * 4 + (lat, lat),
        in_specs=[vm] * 7,
        out_specs=(vm,) * 7,
        cost_estimate=pl.CostEstimate(flops=1_000_000, bytes_accessed=5_000_000, transcendentals=0),
    )(*results)


def solution(mesh):
    own = P("seq", "vis")
    lat_in = P("vis", None, None)
    lat_out = P("vis", None, "seq")
    return jax.shard_map(
        shards,
        mesh=mesh,
        in_specs=(own, own, own, P("seq"), own, lat_in, lat_in, P("seq"), P("seq"), P("vis"), own),
        out_specs=(own, own, own, own, own, lat_out, lat_out),
        check_vma=False,
    )
```

```python
import math

import jax
import jax.numpy as jnp
from jax import lax
from jax.experimental import pallas as pl
from jax.experimental.pallas import tpu as pltpu
from jax.sharding import PartitionSpec as P

HD = 128
TD = 320
NX = 4
CH = TD * NX
NC = 3
TILE = 256
NQ = CH // TILE
LAT = 64
SLOTS = 4
IMAGES = 8
WD = 512
SCALE = 1.0 / math.sqrt(HD)
BIG = -1e30
MESH = pl.DeviceIdType.MESH
F32, BF16, I32 = jnp.float32, jnp.bfloat16, jnp.int32

NT = (((1,), (1,)), ((), ()))
NN = (((1,), (0,)), ((), ()))


def dot(a, b, dims=NN):
    return lax.dot_general(a, b, dims, preferred_element_type=F32)


def fold(a, op):
    return op(a.reshape(a.shape[0] // 8, 8, a.shape[1]), axis=0)


LOG2E = 1.4426950408889634

FWD_TILES = (
    tuple((c * TILE, TILE, 0, (c + 1) * TILE) for c in range(NQ)),
    tuple((c * TILE, TILE, 0, CH) for c in range(NQ)),
    tuple((c * TILE, TILE, c * TILE, CH - c * TILE) for c in range(NQ)),
)
BWD_TILES = (FWD_TILES[0], ((0, CH // 2, 0, CH), (CH // 2, CH // 2, 0, CH)), FWD_TILES[2])
ORDER = (0, 1, 3, 2)


def kernel(
    docs_ref, tok_ref, img_ref, gate_ref, q_ref, k_ref, v_ref, cq_ref, do_ref, lk_ref, lv_ref,
    mixed_ref, qg_ref, kg_ref, vg_ref, cqg_ref, lkg_ref, lvg_ref,
    kbuf, vbuf, qbuf, dobuf, dol, kt, vt, sbuf, pbuf, opart, maxes, sums, dsum, starts, dot_t, dqt,
    cown, cx, crow, cz, cqv, dov, stage,
    latk, latv, lks, lvs, gk, gv, cross, latsend, latx, latz, latin,
    obuf, dqb, part_k, part_v, own_k, own_v, got_k, got_v, sum_k, sum_v,
    o_in, dq_in, dk_in, dv_in, mixed, cqg, lkg, lvg,
    a_send, a_recv, z_send, z_recv, c_send, c_recv, l_send, l_recv, gx_send, gx_recv, gz_send, gz_recv,
    p_send, p_recv, b_send, b_recv, f_send, f_recv, own_sem, out_sem, gates,
):
    s = lax.axis_index("seq")
    v = lax.axis_index("vis")
    x = lax.rem(s, NX)
    z = lax.div(s, NX)
    core = lax.rem(v, 2)

    def xpeer(d):
        return lax.rem(x + d, NX)

    def zpeer(d):
        return lax.rem(z + d, NX)

    def remote(src, dst, ssem, rsem, seq, vis):
        return pltpu.make_async_remote_copy(
            src_ref=src, dst_ref=dst, send_sem=ssem, recv_sem=rsem,
            device_id=(seq, vis), device_id_type=MESH,
        )

    def landed(here, rsem):
        remote(here, here, rsem, rsem, s, v).wait_recv()

    def rows(i, n=TD):
        return pl.ds(pl.multiple_of(i * n, n), n)

    def cols(i, n=HD):
        return pl.ds(pl.multiple_of(i * n, n), n)

    def piece(slot, p):
        return pl.ds(pl.multiple_of(slot * CH + p * TD, TD), TD)

    barrier = pltpu.get_barrier_semaphore()

    def greet(seq, vis):
        pl.semaphore_signal(barrier, inc=1, device_id=(seq, vis), device_id_type=MESH)

    def to_seq(j):
        return 2 * v + j % 2

    def to_vis(j):
        return 2 * x + j // 2

    def stays(j):
        return jnp.logical_and(to_seq(j) == s, to_vis(j) == v)

    def from_seq(i):
        return i * NX + lax.div(v, 2)

    from_vis = lax.div(s, 2)

    def from_self(i):
        return jnp.logical_and(from_seq(i) == s, from_vis == v)

    for d in range(1, NX):
        greet(z * NX + xpeer(d), v)
        greet(zpeer(d) * NX + x, v)
    for d in range(1, IMAGES):
        greet(s, lax.rem(v + d, IMAGES))

    for i in range(NX):
        @pl.when(jnp.logical_not(from_self(i)))
        def _():
            greet(from_seq(i), from_vis)

    def own_copy(i):
        src, dst = (
            (k_ref.at[:, cols(x)], kbuf.at[piece(2, x), :]),
            (v_ref.at[:, cols(x)], vbuf.at[piece(2, x), :]),
            (q_ref.at[:, cols(x)], qbuf.at[piece(0, x), :]),
            (do_ref.at[:, cols(x)], dobuf.at[piece(0, x), :]),
            (lk_ref.at[0, :, cols(v, WD)], latk.at[v]),
            (lv_ref.at[0, :, cols(v, WD)], latv.at[v]),
            (cq_ref, cqv),
            (do_ref, dov),
        )[i]
        return pltpu.make_async_copy(src, dst, own_sem.at[i])

    def out_copy(i):
        src, dst = (
            (mixed, mixed_ref), (dq_in, qg_ref), (dk_in, kg_ref), (dv_in, vg_ref), (cqg, cqg_ref),
            (lkg, lkg_ref.at[0]), (lvg, lvg_ref.at[0]),
        )[i]
        return pltpu.make_async_copy(src, dst, out_sem.at[i])

    for i in range(8):
        own_copy(i).start()

    docs = docs_ref[...].reshape(1, TD)
    row_id = lax.broadcasted_iota(I32, (8, HD), 0)
    counts = jnp.zeros((8, HD), F32)
    for d in range(1, 4):
        c = jnp.sum(jnp.where(docs < d, 1.0, 0.0), axis=1, keepdims=True)
        counts = jnp.where(row_id == d, c, counts)
    cown[...] = counts
    pl.semaphore_wait(barrier, 13 + NX - sum(jnp.where(stays(j), 1, 0) for j in range(NX)))

    ins = (k_ref, v_ref, q_ref, do_ref)
    bufs = (kbuf, vbuf, qbuf, dobuf)
    base = (2, 2, 0, 0)

    def a_copy(arr, d):
        p = xpeer(d)
        return remote(ins[arr].at[:, cols(p)], bufs[arr].at[piece(base[arr], x), :],
                      a_send.at[arr, d - 1], a_recv.at[arr, d - 1], z * NX + p, v)

    def a_wait(arr, d):
        landed(bufs[arr].at[piece(base[arr], xpeer(NX - d)), :], a_recv.at[arr, d - 1])

    def c_copy(step, d):
        if step == 0:
            return remote(cown, cx.at[d - 1], c_send.at[0, d - 1], c_recv.at[0, d - 1],
                          z * NX + xpeer(d), v)
        return remote(crow, cz.at[d - 1], c_send.at[1, d - 1], c_recv.at[1, d - 1],
                      zpeer(d) * NX + x, v)

    def z_copy(arr, dz, i):
        p = xpeer(NX - ORDER[i])
        src = ins[arr].at[:, cols(x)] if i == 0 else bufs[arr].at[piece(2, p), :]
        return remote(src, bufs[arr].at[piece(2 - dz, p), :],
                      z_send.at[arr, dz - 1, i], z_recv.at[arr, dz - 1, i], s + dz * NX, v)

    def f_copy(arr, i):
        p = xpeer(NX - ORDER[i])
        src = ins[arr].at[:, cols(x)] if i == 0 else bufs[arr].at[piece(2, p), :]
        return remote(src, stage.at[arr, i], z_send.at[arr, 1, i], f_recv.at[arr, i], s + 3 * NX, v)

    def f_on(arr, i):
        p = xpeer(NX - ORDER[i])
        return remote(stage.at[arr, i], bufs[arr].at[piece(0, p), :],
                      f_send.at[arr, i], z_recv.at[arr, 1, i], s - NX, v)

    def z_start(arr, i):
        if i < 2:
            @pl.when(z == 0)
            def _():
                f_copy(arr, i).start()

            @pl.when(z == 1)
            def _():
                z_copy(arr, 2, i).start()
        else:
            @pl.when(z <= 1)
            def _():
                z_copy(arr, 2, i).start()

        @pl.when(z <= 2)
        def _():
            z_copy(arr, 1, i).start()

    def f_relay(arr):
        @pl.when(z == 3)
        def _():
            for i in range(2):
                landed(stage.at[arr, i], f_recv.at[arr, i])
                f_on(arr, i).start()

    def z_sent(arr):
        for dz in (1, 2):
            @pl.when(z + dz < NX)
            def _():
                for i in range(NX):
                    z_copy(arr, dz, i).wait_send()

    def z_wait(arr, dz):
        for i in range(NX):
            landed(bufs[arr].at[piece(2 - dz, xpeer(NX - ORDER[i])), :], z_recv.at[arr, dz - 1, i])

    def a_start(arr):
        for d in ORDER[1:]:
            a_copy(arr, d).start()

    def a_finish(arr):
        for d in ORDER[1:]:
            a_wait(arr, d)

    def open_gate(n):
        pl.semaphore_signal(gates.at[n], inc=1, device_id=(s, v + 1), device_id_type=MESH)

    @pl.when(core == 0)
    def _():
        for arr in (0, 1):
            z_start(arr, 0)
            a_start(arr)

    @pl.when(core == 1)
    def _():
        for arr in (0, 1):
            z_start(arr, 0)

    for d in ORDER[1:]:
        c_copy(0, d).start()

    lins, lbufs = (lk_ref, lv_ref), (latk, latv)

    def l_copy(arr, d):
        p = lax.rem(v + d, IMAGES)
        return remote(lins[arr].at[0, :, cols(p, WD)], lbufs[arr].at[v],
                      l_send.at[arr, d - 1], l_recv.at[arr, d - 1], s, p)

    for arr in (0, 1):
        for d in range(1, IMAGES):
            l_copy(arr, d).start()

    @pl.when(core == 0)
    def _():
        for arr in (0, 1):
            for i in range(1, NX):
                a_wait(arr, ORDER[i])
                z_start(arr, i)
        open_gate(0)
        a_start(2)
        a_start(3)
        f_relay(0)
        f_relay(1)
        z_sent(0)
        open_gate(1)

    @pl.when(core == 1)
    def _():
        pl.semaphore_wait(gates.at[0], 1)
        for arr in (0, 1):
            a_start(arr)
        for arr in (0, 1):
            a_finish(arr)
        a_start(2)
        a_start(3)
        pl.semaphore_wait(gates.at[1], 1)
        for arr in (0, 1):
            for i in range(1, NX):
                z_start(arr, i)

    for d in ORDER[1:]:
        landed(cx.at[d - 1], c_recv.at[0, d - 1])
    crow[...] = cown[...] + cx[0] + cx[1] + cx[2]
    for d in range(1, NX):
        c_copy(1, d).start()
    for i in range(8):
        own_copy(i).wait()
    for d in range(1, NX):
        landed(cz.at[d - 1], c_recv.at[1, d - 1])
    before = crow[...] + cz[0] + cz[1] + cz[2]
    pos = lax.broadcasted_iota(I32, (8, CH), 1)
    start = jnp.zeros((8, CH), I32)
    for d in range(1, 4):
        b = before[d:d + 1, 0:1].astype(I32)
        start = jnp.where(b <= pos + z * CH, b, start)
    starts[...] = start - (z - 2) * CH

    for slot in range(NC):
        maxes[slot] = jnp.full((8, CH), BIG, F32)
        sums[slot] = jnp.zeros((8, CH), F32)
        opart[slot] = jnp.zeros((HD, CH), F32)

    def forward(slot):
        at = slot * CH
        kt[:, at:at + CH] = kbuf[at:at + CH, :].T
        vt[:, at:at + CH] = vbuf[at:at + CH, :].T
        for k0, kn, q0, qn in FWD_TILES[slot]:
            across = slice(q0, q0 + qn)
            raw = dot(kbuf[at + k0:at + k0 + kn, :], qbuf[across, :], NT)
            kpos = lax.broadcasted_iota(I32, (kn, qn), 0) + (at + k0)
            kept = kpos >= starts[0:1, across]
            if slot == 2:
                kept = kept & (kpos <= lax.broadcasted_iota(I32, (kn, qn), 1) + (at + q0))
            raw = jnp.where(kept, raw, BIG)
            sbuf[k0:k0 + kn, across] = raw
            maxes[slot, :, across] = jnp.maximum(maxes[slot, :, across], fold(raw, jnp.max))
        top = jnp.max(maxes[slot], axis=0, keepdims=True)
        maxes[slot] = jnp.broadcast_to(top, (8, CH))
        for k0, kn, q0, qn in FWD_TILES[slot]:
            across = slice(q0, q0 + qn)
            p = jnp.exp2((sbuf[k0:k0 + kn, across] - top[:, across]) * (SCALE * LOG2E))
            pb = p.astype(BF16)
            pbuf[at + k0:at + k0 + kn, across] = pb
            sums[slot, :, across] += fold(p, jnp.sum)
            opart[slot, :, across] += dot(vt[:, at + k0:at + k0 + kn], pb)

    for arr in (0, 1):
        for d in range(1, IMAGES):
            landed(lbufs[arr].at[lax.rem(v + IMAGES - d, IMAGES)], l_recv.at[arr, d - 1])
    for i in range(SLOTS):
        lks[i * LAT:(i + 1) * LAT, :] = latk[img_ref[i]]
        lvs[i * LAT:(i + 1) * LAT, :] = latv[img_ref[i]]
    slot_of = lax.broadcasted_iota(I32, (SLOTS * LAT, TD), 0) // LAT
    toks = tok_ref[...].reshape(1, TD)
    seen = slot_of == toks
    any_image = toks < SLOTS
    gate = jnp.tanh(gate_ref[...].reshape(1, WD))
    for h in range(NX):
        sl = slice(h * HD, (h + 1) * HD)
        lkh, lvh, cqh = lks[:, sl], lvs[:, sl], cqv[:, sl]
        raw = dot(lkh, cqh, NT)
        raw = jnp.where(seen, raw * SCALE, BIG)
        w = jnp.where(seen, jnp.exp(raw - jnp.max(raw, axis=0, keepdims=True)), 0.0)
        total = jnp.where(any_image, jnp.sum(w, axis=0, keepdims=True), 1.0)
        probs = w / total
        low = probs.astype(BF16)
        cross[:, sl] = gate[:, sl] * dot(lvh.T, low).T
        back = (gate[:, sl] * dov[:, sl].astype(F32)).astype(BF16)
        gp = dot(lvh, back, NT)
        cdot = jnp.sum(probs * gp, axis=0, keepdims=True)
        ds = (probs * (gp - cdot) * SCALE).astype(BF16)
        cqg[:, sl] = dot(lkh.T, ds).T.astype(BF16)
        gk[:, sl] = dot(ds, cqh).astype(BF16).astype(F32)
        gv[:, sl] = dot(low, back).astype(BF16).astype(F32)

    out_copy(4).start()

    for m in range(IMAGES):
        for n, g in enumerate((gk, gv)):
            acc = jnp.zeros((LAT, WD), F32)
            for i in range(SLOTS):
                acc = acc + jnp.where(img_ref[i] == m, 1.0, 0.0) * g[i * LAT:(i + 1) * LAT, :]
            acc = acc.astype(BF16)
            for h in range(2):
                latsend[m // 2, (m % 2) * 2 + h, n] = acc[:, h * 256:(h + 1) * 256]

    def gx_copy(d):
        p = xpeer(d)
        return remote(latsend.at[p], latx.at[d - 1], gx_send.at[d - 1], gx_recv.at[d - 1],
                      z * NX + p, v)

    def gz_copy(j):
        return remote(latz.at[j], latin.at[z], gz_send.at[j], gz_recv.at[z], to_seq(j), to_vis(j))

    for d in ORDER[1:]:
        gx_copy(d).start()

    def row_sum(slot):
        dsum[slot] = jnp.broadcast_to(jnp.sum(dot_t[...] * opart[slot], axis=0, keepdims=True), (8, CH))

    dsum[0] = jnp.zeros((8, CH), F32)
    dsum[1] = jnp.zeros((8, CH), F32)

    @pl.when(core == 1)
    def _():
        f_relay(0)
        f_relay(1)

    a_finish(2)
    forward(2)
    a_finish(3)
    dot_t[...] = dobuf[...].astype(F32).T
    row_sum(2)

    @pl.when(z >= 1)
    def _():
        z_wait(0, 1)
        z_wait(1, 1)
        forward(1)
        row_sum(1)

    @pl.when(z >= 2)
    def _():
        z_wait(0, 2)
        z_wait(1, 2)
        forward(0)
        row_sum(0)

    top = jnp.maximum(jnp.maximum(maxes[0], maxes[1]), maxes[2])
    total = jnp.zeros((1, CH), F32)
    row_dot = jnp.zeros((8, CH), F32)
    for slot in range(NC):
        factor = jnp.exp2((maxes[slot] - top) * (SCALE * LOG2E))
        maxes[slot] = factor
        total = total + jnp.sum(sums[slot], axis=0, keepdims=True) * factor[0:1]
        row_dot = row_dot + dsum[slot] * factor
    inv = 1.0 / total
    row_dot = row_dot * inv
    for slot in range(NC):
        factor = maxes[slot] * inv
        maxes[slot] = factor
        sums[slot] = factor * row_dot
    dqt[...] = jnp.zeros_like(dqt)

    outs = (obuf, dqb, sum_k, sum_v)
    backs = (o_in, dq_in, dk_in, dv_in)

    def b_copy(arr, d):
        p = xpeer(d)
        return remote(outs[arr].at[rows(p), :], backs[arr].at[:, cols(x)],
                      b_send.at[arr, d - 1], b_recv.at[arr, d - 1], z * NX + p, v)

    def b_wait(arr, d):
        landed(backs[arr].at[:, cols(xpeer(NX - d))], b_recv.at[arr, d - 1])

    def b_own(arr):
        backs[arr][:, cols(x)] = outs[arr][rows(x), :]

    parts, gots = (part_k, part_v), (got_k, got_v)

    def p_copy(arr, dz, p):
        return remote(parts[arr].at[pl.ds((2 - dz) * CH + p * TD, TD), :],
                      gots[arr].at[pl.ds((dz - 1) * CH + p * TD, TD), :],
                      p_send.at[arr, dz - 1, p], p_recv.at[arr, dz - 1, p], s - dz * NX, v)

    def r_copy(arr, p):
        return remote(parts[arr].at[pl.ds(p * TD, TD), :], stage.at[arr, p],
                      p_send.at[arr, 1, p], f_recv.at[arr, p], x, v)

    def r_on(arr, p):
        return remote(stage.at[arr, p], gots[arr].at[pl.ds(CH + p * TD, TD), :],
                      f_send.at[arr, p], p_recv.at[arr, 1, p], NX + x, v)

    def p_start(dz, p):
        for arr in (0, 1):
            if dz == 2 and p < 2:
                @pl.when(z == 3)
                def _():
                    r_copy(arr, p).start()

                @pl.when(z == 2)
                def _():
                    p_copy(arr, dz, p).start()
            else:
                p_copy(arr, dz, p).start()

    def backward(slot):
        at = slot * CH
        sent = 0
        dol[slot] = (dot_t[...] * maxes[slot, 0:1, :]).T.astype(BF16)
        for k0, kn, q0, qn in BWD_TILES[slot]:
            down, across = slice(at + k0, at + k0 + kn), slice(q0, q0 + qn)
            pb = pbuf[down, across]
            grad = dol[slot, across, :]
            dp = dot(vbuf[down, :], grad, NT)
            ds = (pb.astype(F32) * (dp - sums[slot, 0:1, across])).astype(BF16)
            dk = dot(ds, qbuf[across, :]) * SCALE
            dv = dot(pb, grad)
            dqt[:, across] += dot(kt[:, down], ds)
            if slot == 2:
                own_k[k0:k0 + kn, :] = dk
                own_v[k0:k0 + kn, :] = dv
            else:
                part_k[down, :] = dk.astype(BF16)
                part_v[down, :] = dv.astype(BF16)
                while (sent + 1) * TD <= k0 + kn:
                    p_start(2 - slot, sent)
                    sent += 1

    @pl.when(z >= 2)
    def _():
        backward(0)

    for d in ORDER[1:]:
        landed(latx.at[d - 1], gx_recv.at[d - 1])
    for j in range(NX):
        for n in range(2):
            acc = latsend[x, j, n].astype(F32)
            for d in range(3):
                acc = acc + latx[d, j, n].astype(F32)
            latz[j, n] = acc.astype(BF16)

        @pl.when(jnp.logical_not(stays(j)))
        def _():
            gz_copy(j).start()

        @pl.when(stays(j))
        def _():
            latin[z] = latz[j]

    @pl.when(z >= 1)
    def _():
        backward(1)

    out = opart[0] * maxes[0, 0:1, :] + opart[1] * maxes[1, 0:1, :] + opart[2] * maxes[2, 0:1, :]
    obuf[...] = out.T.astype(BF16)
    for d in ORDER[1:]:
        b_copy(0, d).start()
    b_own(0)
    backward(2)
    dqb[...] = (dqt[...] * SCALE).T.astype(BF16)
    for d in ORDER[1:]:
        b_copy(1, d).start()
    b_own(1)

    @pl.when(z == 0)
    def _():
        for p in range(2):
            for arr in (0, 1):
                landed(stage.at[arr, p], f_recv.at[arr, p])
                r_on(arr, p).start()

    def p_wait(arr, dz, p):
        here = gots[arr].at[pl.ds((dz - 1) * CH + p * TD, TD), :]
        landed(here, p_recv.at[arr, dz - 1, p])
        return here

    for p in range(NX):
        sl = slice(p * TD, (p + 1) * TD)
        for arr, (own, out_) in enumerate(((own_k, sum_k), (own_v, sum_v))):
            for dz in (2, 1):
                @pl.when(z + dz < NX)
                def _():
                    here = p_wait(arr, dz, p)
                    own[sl, :] += here[...].astype(F32)
            out_[sl, :] = own[sl, :].astype(BF16)

            @pl.when(x != p)
            def _():
                d = lax.rem(p - x + NX, NX)
                remote(out_.at[sl, :], backs[arr + 2].at[:, cols(x)],
                       b_send.at[arr + 2, d - 1], b_recv.at[arr + 2, d - 1], z * NX + p, v).start()

    for d in ORDER[1:]:
        b_wait(0, d)
    mixed[...] = (o_in[...].astype(F32) + cross[...]).astype(BF16)
    out_copy(0).start()

    for i in range(NX):
        @pl.when(jnp.logical_not(from_self(i)))
        def _():
            landed(latin.at[i], gz_recv.at[i])

    for n, g in enumerate((lkg, lvg)):
        acc = latin[0, n].astype(F32)
        for i in range(1, NX):
            acc = acc + latin[i, n].astype(F32)
        g[...] = acc
        out_copy(5 + n).start()
    for d in ORDER[1:]:
        b_wait(1, d)
    out_copy(1).start()

    for arr in (2, 3):
        b_own(arr)
        for d in ORDER[1:]:
            b_wait(arr, d)
        out_copy(arr).start()

    for i in range(7):
        out_copy(i).wait()
    for d in range(1, NX):
        for arr in range(4):
            a_copy(arr, d).wait_send()
            b_copy(arr, d).wait_send()
        for step in range(2):
            c_copy(step, d).wait_send()
        gx_copy(d).wait_send()

    for j in range(NX):
        @pl.when(jnp.logical_not(stays(j)))
        def _():
            gz_copy(j).wait_send()

    @pl.when(core == 1)
    def _():
        z_sent(0)

    z_sent(1)
    for arr in (0, 1):
        for d in range(1, IMAGES):
            l_copy(arr, d).wait_send()
        for dz in (1, 2):
            @pl.when(z >= dz)
            def _():
                for p in range(NX):
                    p_copy(arr, dz, p).wait_send()

        @pl.when(z == 3)
        def _():
            for i in range(2):
                f_on(arr, i).wait_send()

        @pl.when(z == 0)
        def _():
            for p in range(2):
                r_on(arr, p).wait_send()


def widen(*refs):
    ins, outs, (narrow, full, lat, in_sem, out_sem) = refs[:7], refs[7:14], refs[14:]

    def fetch(i):
        dst = narrow.at[i] if i < 5 else lat.at[i - 5]
        return pltpu.make_async_copy(ins[i], dst, in_sem.at[i])

    def keep(i):
        src = narrow.at[0] if i == 0 else full.at[i - 1] if i < 5 else lat.at[i - 5]
        return pltpu.make_async_copy(src, outs[i], out_sem.at[i])

    for i in range(7):
        fetch(i).start()
    for i in range(7):
        fetch(i).wait()
        if 1 <= i <= 4:
            full[i - 1] = narrow[i].astype(F32)
        keep(i).start()
    for i in range(7):
        keep(i).wait()


def shards(query, key, value, doc_ids, cross_query, latent_key, latent_value, token_slot,
           slot_image, cross_gate, out_grad):
    vm = pl.BlockSpec(memory_space=pltpu.VMEM)
    sm = pl.BlockSpec(memory_space=pltpu.SMEM)
    hbm = pl.BlockSpec(memory_space=pl.ANY)
    dma = pltpu.SemaphoreType.DMA

    def low(*shape):
        return pltpu.VMEM(shape, BF16)

    def wide(*shape):
        return pltpu.VMEM(shape, F32)

    scratch = [
        low(NC * CH, HD), low(NC * CH, HD), low(CH, HD), low(CH, HD),
        low(NC, CH, HD), low(HD, NC * CH), low(HD, NC * CH),
        wide(CH, CH), low(NC * CH, CH), wide(NC, HD, CH),
        wide(NC, 8, CH), wide(NC, 8, CH), wide(NC, 8, CH), pltpu.VMEM((8, CH), I32),
        wide(HD, CH), wide(HD, CH),
        wide(8, HD), wide(3, 8, HD), wide(8, HD), wide(3, 8, HD),
        low(TD, WD), low(TD, WD), low(2, 2, TD, HD),
        low(IMAGES, LAT, WD), low(IMAGES, LAT, WD),
        low(SLOTS * LAT, WD), low(SLOTS * LAT, WD),
        wide(SLOTS * LAT, WD), wide(SLOTS * LAT, WD), wide(TD, WD),
        low(NX, NX, 2, LAT, 256), low(3, NX, 2, LAT, 256),
        low(NX, 2, LAT, 256), low(NX, 2, LAT, 256),
        low(CH, HD), low(CH, HD), low(2 * CH, HD), low(2 * CH, HD),
        wide(CH, HD), wide(CH, HD), low(2 * CH, HD), low(2 * CH, HD),
        low(CH, HD), low(CH, HD),
        low(TD, WD), low(TD, WD), low(TD, WD), low(TD, WD),
        low(TD, WD), low(TD, WD), wide(LAT, 256), wide(LAT, 256),
        dma((4, 3)), dma((4, 3)),
        dma((2, 2, 4)), dma((2, 2, 4)),
        dma((2, 3)), dma((2, 3)),
        dma((2, 7)), dma((2, 7)),
        dma((3,)), dma((3,)), dma((4,)), dma((4,)),
        dma((2, 2, 4)), dma((2, 2, 4)),
        dma((4, 3)), dma((4, 3)),
        dma((2, 2)), dma((2, 2)), dma((8,)), dma((7,)), pltpu.SemaphoreType.REGULAR((2,)),
    ]
    full = jax.ShapeDtypeStruct((TD, WD), F32)
    half = jax.ShapeDtypeStruct((TD, WD), BF16)
    lat = jax.ShapeDtypeStruct((1, LAT, 256), F32)
    results = pl.pallas_call(
        kernel,
        out_shape=(half,) * 5 + (lat, lat),
        in_specs=[vm, vm, sm, vm] + [hbm] * 7,
        out_specs=(hbm,) * 7,
        scratch_shapes=scratch,
        cost_estimate=pl.CostEstimate(flops=6_500_000_000, bytes_accessed=8_000_000, transcendentals=4_000_000),
        compiler_params=pltpu.CompilerParams(
            collective_id=0, has_side_effects=True, vmem_limit_bytes=58 * 1024 * 1024),
    )(
        doc_ids, token_slot, slot_image, cross_gate,
        query, key, value, cross_query, out_grad, latent_key, latent_value,
    )
    return pl.pallas_call(
        widen,
        out_shape=(half,) + (full,) * 4 + (lat, lat),
        in_specs=[hbm] * 7,
        out_specs=(hbm,) * 7,
        scratch_shapes=[low(5, TD, WD), wide(4, TD, WD), wide(2, 1, LAT, 256), dma((7,)), dma((7,))],
        cost_estimate=pl.CostEstimate(flops=1_000_000, bytes_accessed=5_000_000, transcendentals=0),
    )(*results)


def solution(mesh):
    own = P("seq", "vis")
    lat_in = P("vis", None, None)
    lat_out = P("vis", None, "seq")
    return jax.shard_map(
        shards,
        mesh=mesh,
        in_specs=(own, own, own, P("seq"), own, lat_in, lat_in, P("seq"), P("seq"), P("vis"), own),
        out_specs=(own, own, own, own, own, lat_out, lat_out),
        check_vma=False,
    )
```

```python
import math

import jax
import jax.numpy as jnp
from jax import lax
from jax.experimental import pallas as pl
from jax.experimental.pallas import tpu as pltpu
from jax.sharding import PartitionSpec as P

HD = 128
TD = 320
NX = 4
CH = TD * NX
NC = 3
TILE = 256
NQ = CH // TILE
LAT = 64
SLOTS = 4
IMAGES = 8
WD = 512
SCALE = 1.0 / math.sqrt(HD)
BIG = -1e30
MESH = pl.DeviceIdType.MESH
F32, BF16, I32 = jnp.float32, jnp.bfloat16, jnp.int32

NT = (((1,), (1,)), ((), ()))
NN = (((1,), (0,)), ((), ()))


def dot(a, b, dims=NN):
    return lax.dot_general(a, b, dims, preferred_element_type=F32)


def fold(a, op):
    return op(a.reshape(a.shape[0] // 8, 8, a.shape[1]), axis=0)


LOG2E = 1.4426950408889634

FWD_TILES = (
    tuple((c * TILE, TILE, 0, (c + 1) * TILE) for c in range(NQ)),
    tuple((c * TILE, TILE, 0, CH) for c in range(NQ)),
    tuple((c * TILE, TILE, c * TILE, CH - c * TILE) for c in range(NQ)),
)
BWD_TILES = (FWD_TILES[0], ((0, CH // 2, 0, CH), (CH // 2, CH // 2, 0, CH)), FWD_TILES[2])
ORDER = (0, 1, 3, 2)


def kernel(
    docs_ref, tok_ref, img_ref, gate_ref, q_ref, k_ref, v_ref, cq_ref, do_ref, lk_ref, lv_ref,
    mixed_ref, qg_ref, kg_ref, vg_ref, cqg_ref, lkg_ref, lvg_ref,
    kbuf, vbuf, qbuf, dobuf, dol, kt, vt, sbuf, pbuf, opart, maxes, sums, dsum, starts, dot_t, dqt,
    cown, cx, crow, cz, cqv, dov, stage,
    latk, latv, lks, lvs, gk, gv, cross, latsend, latx, latz, latin,
    obuf, dqb, part_k, part_v, own_k, own_v, got_k, got_v, sum_k, sum_v,
    o_in, dq_in, dk_in, dv_in, mixed, cqg, lkg, lvg,
    a_send, a_recv, z_send, z_recv, c_send, c_recv, l_send, l_recv, gx_send, gx_recv, gz_send, gz_recv,
    p_send, p_recv, b_send, b_recv, f_send, f_recv, own_sem, out_sem, gates,
):
    s = lax.axis_index("seq")
    v = lax.axis_index("vis")
    x = lax.rem(s, NX)
    z = lax.div(s, NX)
    core = lax.rem(v, 2)

    def xpeer(d):
        return lax.rem(x + d, NX)

    def zpeer(d):
        return lax.rem(z + d, NX)

    def remote(src, dst, ssem, rsem, seq, vis):
        return pltpu.make_async_remote_copy(
            src_ref=src, dst_ref=dst, send_sem=ssem, recv_sem=rsem,
            device_id=(seq, vis), device_id_type=MESH,
        )

    def landed(here, rsem):
        remote(here, here, rsem, rsem, s, v).wait_recv()

    def rows(i, n=TD):
        return pl.ds(pl.multiple_of(i * n, n), n)

    def cols(i, n=HD):
        return pl.ds(pl.multiple_of(i * n, n), n)

    def piece(slot, p):
        return pl.ds(pl.multiple_of(slot * CH + p * TD, TD), TD)

    barrier = pltpu.get_barrier_semaphore()

    def greet(seq, vis):
        pl.semaphore_signal(barrier, inc=1, device_id=(seq, vis), device_id_type=MESH)

    def to_seq(j):
        return 2 * v + j % 2

    def to_vis(j):
        return 2 * x + j // 2

    def stays(j):
        return jnp.logical_and(to_seq(j) == s, to_vis(j) == v)

    def from_seq(i):
        return i * NX + lax.div(v, 2)

    from_vis = lax.div(s, 2)

    def from_self(i):
        return jnp.logical_and(from_seq(i) == s, from_vis == v)

    for d in range(1, NX):
        greet(z * NX + xpeer(d), v)
        greet(zpeer(d) * NX + x, v)
    for d in range(1, IMAGES):
        greet(s, lax.rem(v + d, IMAGES))

    for i in range(NX):
        @pl.when(jnp.logical_not(from_self(i)))
        def _():
            greet(from_seq(i), from_vis)

    def own_copy(i):
        src, dst = (
            (k_ref.at[:, cols(x)], kbuf.at[piece(2, x), :]),
            (v_ref.at[:, cols(x)], vbuf.at[piece(2, x), :]),
            (q_ref.at[:, cols(x)], qbuf.at[piece(0, x), :]),
            (do_ref.at[:, cols(x)], dobuf.at[piece(0, x), :]),
            (lk_ref.at[0, :, cols(v, WD)], latk.at[v]),
            (lv_ref.at[0, :, cols(v, WD)], latv.at[v]),
            (cq_ref, cqv),
            (do_ref, dov),
        )[i]
        return pltpu.make_async_copy(src, dst, own_sem.at[i])

    def out_copy(i):
        src, dst = (
            (mixed, mixed_ref), (dq_in, qg_ref), (dk_in, kg_ref), (dv_in, vg_ref), (cqg, cqg_ref),
            (lkg, lkg_ref.at[0]), (lvg, lvg_ref.at[0]),
        )[i]
        return pltpu.make_async_copy(src, dst, out_sem.at[i])

    for i in range(8):
        own_copy(i).start()

    docs = docs_ref[...].reshape(1, TD)
    row_id = lax.broadcasted_iota(I32, (8, HD), 0)
    counts = jnp.zeros((8, HD), F32)
    for d in range(1, 4):
        c = jnp.sum(jnp.where(docs < d, 1.0, 0.0), axis=1, keepdims=True)
        counts = jnp.where(row_id == d, c, counts)
    cown[...] = counts
    pl.semaphore_wait(barrier, 13 + NX - sum(jnp.where(stays(j), 1, 0) for j in range(NX)))

    ins = (k_ref, v_ref, q_ref, do_ref)
    bufs = (kbuf, vbuf, qbuf, dobuf)
    base = (2, 2, 0, 0)

    def a_copy(arr, d):
        p = xpeer(d)
        return remote(ins[arr].at[:, cols(p)], bufs[arr].at[piece(base[arr], x), :],
                      a_send.at[arr, d - 1], a_recv.at[arr, d - 1], z * NX + p, v)

    def a_wait(arr, d):
        landed(bufs[arr].at[piece(base[arr], xpeer(NX - d)), :], a_recv.at[arr, d - 1])

    def c_copy(step, d):
        if step == 0:
            return remote(cown, cx.at[d - 1], c_send.at[0, d - 1], c_recv.at[0, d - 1],
                          z * NX + xpeer(d), v)
        return remote(crow, cz.at[d - 1], c_send.at[1, d - 1], c_recv.at[1, d - 1],
                      zpeer(d) * NX + x, v)

    def z_copy(arr, dz, i):
        p = xpeer(NX - ORDER[i])
        src = ins[arr].at[:, cols(x)] if i == 0 else bufs[arr].at[piece(2, p), :]
        return remote(src, bufs[arr].at[piece(2 - dz, p), :],
                      z_send.at[arr, dz - 1, i], z_recv.at[arr, dz - 1, i], s + dz * NX, v)

    def f_copy(arr, i):
        p = xpeer(NX - ORDER[i])
        src = ins[arr].at[:, cols(x)] if i == 0 else bufs[arr].at[piece(2, p), :]
        return remote(src, stage.at[arr, i], z_send.at[arr, 1, i], f_recv.at[arr, i], s + 3 * NX, v)

    def f_on(arr, i):
        p = xpeer(NX - ORDER[i])
        return remote(stage.at[arr, i], bufs[arr].at[piece(0, p), :],
                      f_send.at[arr, i], z_recv.at[arr, 1, i], s - NX, v)

    def z_start(arr, i):
        if i < 2:
            @pl.when(z == 0)
            def _():
                f_copy(arr, i).start()

            @pl.when(z == 1)
            def _():
                z_copy(arr, 2, i).start()
        else:
            @pl.when(z <= 1)
            def _():
                z_copy(arr, 2, i).start()

        @pl.when(z <= 2)
        def _():
            z_copy(arr, 1, i).start()

    def f_relay(arr):
        @pl.when(z == 3)
        def _():
            for i in range(2):
                landed(stage.at[arr, i], f_recv.at[arr, i])
                f_on(arr, i).start()

    def z_sent(arr):
        for dz in (1, 2):
            @pl.when(z + dz < NX)
            def _():
                for i in range(NX):
                    z_copy(arr, dz, i).wait_send()

    def z_wait(arr, dz):
        for i in range(NX):
            landed(bufs[arr].at[piece(2 - dz, xpeer(NX - ORDER[i])), :], z_recv.at[arr, dz - 1, i])

    def a_start(arr):
        for d in ORDER[1:]:
            a_copy(arr, d).start()

    def a_finish(arr):
        for d in ORDER[1:]:
            a_wait(arr, d)

    def open_gate(n):
        pl.semaphore_signal(gates.at[n], inc=1, device_id=(s, v + 1), device_id_type=MESH)

    @pl.when(core == 0)
    def _():
        for arr in (0, 1):
            z_start(arr, 0)
            a_start(arr)

    @pl.when(core == 1)
    def _():
        for arr in (0, 1):
            z_start(arr, 0)

    for d in ORDER[1:]:
        c_copy(0, d).start()

    lins, lbufs = (lk_ref, lv_ref), (latk, latv)

    def l_copy(arr, d):
        p = lax.rem(v + d, IMAGES)
        return remote(lins[arr].at[0, :, cols(p, WD)], lbufs[arr].at[v],
                      l_send.at[arr, d - 1], l_recv.at[arr, d - 1], s, p)

    for arr in (0, 1):
        for d in range(1, IMAGES):
            l_copy(arr, d).start()

    @pl.when(core == 0)
    def _():
        for arr in (0, 1):
            for i in range(1, NX):
                a_wait(arr, ORDER[i])
                z_start(arr, i)
        open_gate(0)
        a_start(2)
        a_start(3)
        f_relay(0)
        f_relay(1)
        z_sent(0)
        open_gate(1)

    @pl.when(core == 1)
    def _():
        pl.semaphore_wait(gates.at[0], 1)
        for arr in (0, 1):
            a_start(arr)
        for arr in (0, 1):
            a_finish(arr)
        a_start(2)
        a_start(3)
        pl.semaphore_wait(gates.at[1], 1)
        for arr in (0, 1):
            for i in range(1, NX):
                z_start(arr, i)

    for d in ORDER[1:]:
        landed(cx.at[d - 1], c_recv.at[0, d - 1])
    crow[...] = cown[...] + cx[0] + cx[1] + cx[2]
    for d in range(1, NX):
        c_copy(1, d).start()
    for i in range(8):
        own_copy(i).wait()
    for d in range(1, NX):
        landed(cz.at[d - 1], c_recv.at[1, d - 1])
    before = crow[...] + cz[0] + cz[1] + cz[2]
    pos = lax.broadcasted_iota(I32, (8, CH), 1)
    start = jnp.zeros((8, CH), I32)
    for d in range(1, 4):
        b = before[d:d + 1, 0:1].astype(I32)
        start = jnp.where(b <= pos + z * CH, b, start)
    starts[...] = start - (z - 2) * CH

    for slot in range(NC):
        maxes[slot] = jnp.full((8, CH), BIG, F32)
        sums[slot] = jnp.zeros((8, CH), F32)
        opart[slot] = jnp.zeros((HD, CH), F32)

    def forward(slot):
        at = slot * CH
        kt[:, at:at + CH] = kbuf[at:at + CH, :].T
        vt[:, at:at + CH] = vbuf[at:at + CH, :].T
        for k0, kn, q0, qn in FWD_TILES[slot]:
            across = slice(q0, q0 + qn)
            raw = dot(kbuf[at + k0:at + k0 + kn, :], qbuf[across, :], NT)
            kpos = lax.broadcasted_iota(I32, (kn, qn), 0) + (at + k0)
            kept = kpos >= starts[0:1, across]
            if slot == 2:
                kept = kept & (kpos <= lax.broadcasted_iota(I32, (kn, qn), 1) + (at + q0))
            raw = jnp.where(kept, raw, BIG)
            sbuf[k0:k0 + kn, across] = raw
            maxes[slot, :, across] = jnp.maximum(maxes[slot, :, across], fold(raw, jnp.max))
        top = jnp.max(maxes[slot], axis=0, keepdims=True)
        maxes[slot] = jnp.broadcast_to(top, (8, CH))
        for k0, kn, q0, qn in FWD_TILES[slot]:
            across = slice(q0, q0 + qn)
            p = jnp.exp2((sbuf[k0:k0 + kn, across] - top[:, across]) * (SCALE * LOG2E))
            pb = p.astype(BF16)
            pbuf[at + k0:at + k0 + kn, across] = pb
            sums[slot, :, across] += fold(p, jnp.sum)
            opart[slot, :, across] += dot(vt[:, at + k0:at + k0 + kn], pb)

    for arr in (0, 1):
        for d in range(1, IMAGES):
            landed(lbufs[arr].at[lax.rem(v + IMAGES - d, IMAGES)], l_recv.at[arr, d - 1])
    for i in range(SLOTS):
        lks[i * LAT:(i + 1) * LAT, :] = latk[img_ref[i]]
        lvs[i * LAT:(i + 1) * LAT, :] = latv[img_ref[i]]
    slot_of = lax.broadcasted_iota(I32, (SLOTS * LAT, TD), 0) // LAT
    toks = tok_ref[...].reshape(1, TD)
    seen = slot_of == toks
    any_image = toks < SLOTS
    gate = jnp.tanh(gate_ref[...].reshape(1, WD))
    for h in range(NX):
        sl = slice(h * HD, (h + 1) * HD)
        lkh, lvh, cqh = lks[:, sl], lvs[:, sl], cqv[:, sl]
        raw = dot(lkh, cqh, NT)
        raw = jnp.where(seen, raw * SCALE, BIG)
        w = jnp.where(seen, jnp.exp(raw - jnp.max(raw, axis=0, keepdims=True)), 0.0)
        total = jnp.where(any_image, jnp.sum(w, axis=0, keepdims=True), 1.0)
        probs = w / total
        low = probs.astype(BF16)
        cross[:, sl] = gate[:, sl] * dot(lvh.T, low).T
        back = (gate[:, sl] * dov[:, sl].astype(F32)).astype(BF16)
        gp = dot(lvh, back, NT)
        cdot = jnp.sum(probs * gp, axis=0, keepdims=True)
        ds = (probs * (gp - cdot) * SCALE).astype(BF16)
        cqg[:, sl] = dot(lkh.T, ds).T.astype(BF16)
        gk[:, sl] = dot(ds, cqh).astype(BF16).astype(F32)
        gv[:, sl] = dot(low, back).astype(BF16).astype(F32)

    out_copy(4).start()

    for m in range(IMAGES):
        for n, g in enumerate((gk, gv)):
            acc = jnp.zeros((LAT, WD), F32)
            for i in range(SLOTS):
                acc = acc + jnp.where(img_ref[i] == m, 1.0, 0.0) * g[i * LAT:(i + 1) * LAT, :]
            acc = acc.astype(BF16)
            for h in range(2):
                latsend[m // 2, (m % 2) * 2 + h, n] = acc[:, h * 256:(h + 1) * 256]

    def gx_copy(d):
        p = xpeer(d)
        return remote(latsend.at[p], latx.at[d - 1], gx_send.at[d - 1], gx_recv.at[d - 1],
                      z * NX + p, v)

    def gz_copy(j):
        return remote(latz.at[j], latin.at[z], gz_send.at[j], gz_recv.at[z], to_seq(j), to_vis(j))

    for d in ORDER[1:]:
        gx_copy(d).start()

    def row_sum(slot):
        dsum[slot] = jnp.broadcast_to(jnp.sum(dot_t[...] * opart[slot], axis=0, keepdims=True), (8, CH))

    dsum[0] = jnp.zeros((8, CH), F32)
    dsum[1] = jnp.zeros((8, CH), F32)

    @pl.when(core == 1)
    def _():
        f_relay(0)
        f_relay(1)

    a_finish(2)
    forward(2)
    a_finish(3)
    dot_t[...] = dobuf[...].astype(F32).T
    row_sum(2)

    @pl.when(z >= 1)
    def _():
        z_wait(0, 1)
        z_wait(1, 1)
        forward(1)
        row_sum(1)

    @pl.when(z >= 2)
    def _():
        z_wait(0, 2)
        z_wait(1, 2)
        forward(0)
        row_sum(0)

    top = jnp.maximum(jnp.maximum(maxes[0], maxes[1]), maxes[2])
    total = jnp.zeros((1, CH), F32)
    row_dot = jnp.zeros((8, CH), F32)
    for slot in range(NC):
        factor = jnp.exp2((maxes[slot] - top) * (SCALE * LOG2E))
        maxes[slot] = factor
        total = total + jnp.sum(sums[slot], axis=0, keepdims=True) * factor[0:1]
        row_dot = row_dot + dsum[slot] * factor
    inv = 1.0 / total
    row_dot = row_dot * inv
    for slot in range(NC):
        factor = maxes[slot] * inv
        maxes[slot] = factor
        sums[slot] = factor * row_dot
    dqt[...] = jnp.zeros_like(dqt)

    outs = (obuf, dqb, sum_k, sum_v)
    backs = (o_in, dq_in, dk_in, dv_in)

    def b_copy(arr, d):
        p = xpeer(d)
        return remote(outs[arr].at[rows(p), :], backs[arr].at[:, cols(x)],
                      b_send.at[arr, d - 1], b_recv.at[arr, d - 1], z * NX + p, v)

    def b_wait(arr, d):
        landed(backs[arr].at[:, cols(xpeer(NX - d))], b_recv.at[arr, d - 1])

    def b_own(arr):
        backs[arr][:, cols(x)] = outs[arr][rows(x), :]

    parts, gots = (part_k, part_v), (got_k, got_v)

    def p_copy(arr, dz, p):
        return remote(parts[arr].at[piece(2 - dz, p), :],
                      gots[arr].at[piece(dz - 1, p), :],
                      p_send.at[arr, dz - 1, p], p_recv.at[arr, dz - 1, p], s - dz * NX, v)

    def r_copy(arr, p):
        return remote(parts[arr].at[pl.ds(p * TD, TD), :], stage.at[arr, p],
                      p_send.at[arr, 1, p], f_recv.at[arr, p], x, v)

    def r_on(arr, p):
        return remote(stage.at[arr, p], gots[arr].at[pl.ds(CH + p * TD, TD), :],
                      f_send.at[arr, p], p_recv.at[arr, 1, p], NX + x, v)

    def p_start(dz, p):
        for arr in (0, 1):
            if dz == 2 and p < 2:
                @pl.when(z == 3)
                def _():
                    r_copy(arr, p).start()

                @pl.when(z == 2)
                def _():
                    p_copy(arr, dz, p).start()
            else:
                p_copy(arr, dz, p).start()

    def turn(j):
        return (x, x + 1 - 2 * lax.rem(x, 2), lax.rem(x + 2, NX), NX - 1 - x)[j]

    def backward(slot):
        at = slot * CH
        sent = 0
        dol[slot] = (dot_t[...] * maxes[slot, 0:1, :]).T.astype(BF16)
        for k0, kn, q0, qn in BWD_TILES[slot]:
            down, across = slice(at + k0, at + k0 + kn), slice(q0, q0 + qn)
            if slot == 1:
                first = lax.rem(lax.div(x, 2) + k0 // kn, 2)
                down = pl.ds(pl.multiple_of(at + first * kn, 128), kn)
            pb = pbuf[down, across]
            grad = dol[slot, across, :]
            dp = dot(vbuf[down, :], grad, NT)
            ds = (pb.astype(F32) * (dp - sums[slot, 0:1, across])).astype(BF16)
            dk = dot(ds, qbuf[across, :]) * SCALE
            dv = dot(pb, grad)
            dqt[:, across] += dot(kt[:, down], ds)
            if slot == 2:
                own_k[k0:k0 + kn, :] = dk
                own_v[k0:k0 + kn, :] = dv
            else:
                part_k[down, :] = dk.astype(BF16)
                part_v[down, :] = dv.astype(BF16)
                while (sent + 1) * TD <= k0 + kn:
                    p_start(2 - slot, turn(sent) if slot == 1 else sent)
                    sent += 1

    @pl.when(z >= 2)
    def _():
        backward(0)

    for d in ORDER[1:]:
        landed(latx.at[d - 1], gx_recv.at[d - 1])
    for j in range(NX):
        for n in range(2):
            acc = latsend[x, j, n].astype(F32)
            for d in range(3):
                acc = acc + latx[d, j, n].astype(F32)
            latz[j, n] = acc.astype(BF16)

        @pl.when(jnp.logical_not(stays(j)))
        def _():
            gz_copy(j).start()

        @pl.when(stays(j))
        def _():
            latin[z] = latz[j]

    @pl.when(z >= 1)
    def _():
        backward(1)

    out = opart[0] * maxes[0, 0:1, :] + opart[1] * maxes[1, 0:1, :] + opart[2] * maxes[2, 0:1, :]
    obuf[...] = out.T.astype(BF16)
    for d in ORDER[1:]:
        b_copy(0, d).start()
    b_own(0)
    backward(2)
    dqb[...] = (dqt[...] * SCALE).T.astype(BF16)
    for d in ORDER[1:]:
        b_copy(1, d).start()
    b_own(1)

    @pl.when(z == 0)
    def _():
        for p in range(2):
            for arr in (0, 1):
                landed(stage.at[arr, p], f_recv.at[arr, p])
                r_on(arr, p).start()

    def p_wait(arr, dz, p):
        here = gots[arr].at[piece(dz - 1, p), :]
        landed(here, p_recv.at[arr, dz - 1, p])
        return here

    for j in range(NX):
        p = turn(j)
        sl = rows(p)
        for arr, (own, out_) in enumerate(((own_k, sum_k), (own_v, sum_v))):
            for dz in (2, 1):
                @pl.when(z + dz < NX)
                def _():
                    here = p_wait(arr, dz, p)
                    own[sl, :] += here[...].astype(F32)
            out_[sl, :] = own[sl, :].astype(BF16)
            if j:
                d = lax.rem(p - x + NX, NX)
                remote(out_.at[sl, :], backs[arr + 2].at[:, cols(x)],
                       b_send.at[arr + 2, d - 1], b_recv.at[arr + 2, d - 1], z * NX + p, v).start()

    for d in ORDER[1:]:
        b_wait(0, d)
    mixed[...] = (o_in[...].astype(F32) + cross[...]).astype(BF16)
    out_copy(0).start()

    for i in range(NX):
        @pl.when(jnp.logical_not(from_self(i)))
        def _():
            landed(latin.at[i], gz_recv.at[i])

    for n, g in enumerate((lkg, lvg)):
        acc = latin[0, n].astype(F32)
        for i in range(1, NX):
            acc = acc + latin[i, n].astype(F32)
        g[...] = acc
        out_copy(5 + n).start()
    for d in ORDER[1:]:
        b_wait(1, d)
    out_copy(1).start()

    for arr in (2, 3):
        b_own(arr)
        for d in ORDER[1:]:
            b_wait(arr, d)
        out_copy(arr).start()

    for i in range(7):
        out_copy(i).wait()
    for d in range(1, NX):
        for arr in range(4):
            a_copy(arr, d).wait_send()
            b_copy(arr, d).wait_send()
        for step in range(2):
            c_copy(step, d).wait_send()
        gx_copy(d).wait_send()

    for j in range(NX):
        @pl.when(jnp.logical_not(stays(j)))
        def _():
            gz_copy(j).wait_send()

    @pl.when(core == 1)
    def _():
        z_sent(0)

    z_sent(1)
    for arr in (0, 1):
        for d in range(1, IMAGES):
            l_copy(arr, d).wait_send()
        for dz in (1, 2):
            @pl.when(z >= dz)
            def _():
                for p in range(NX):
                    p_copy(arr, dz, p).wait_send()

        @pl.when(z == 3)
        def _():
            for i in range(2):
                f_on(arr, i).wait_send()

        @pl.when(z == 0)
        def _():
            for p in range(2):
                r_on(arr, p).wait_send()


def widen(*refs):
    ins, outs, (narrow, full, lat, in_sem, out_sem) = refs[:7], refs[7:14], refs[14:]

    def fetch(i):
        dst = narrow.at[i] if i < 5 else lat.at[i - 5]
        return pltpu.make_async_copy(ins[i], dst, in_sem.at[i])

    def keep(i):
        src = narrow.at[0] if i == 0 else full.at[i - 1] if i < 5 else lat.at[i - 5]
        return pltpu.make_async_copy(src, outs[i], out_sem.at[i])

    for i in range(7):
        fetch(i).start()
    for i in range(7):
        fetch(i).wait()
        if 1 <= i <= 4:
            full[i - 1] = narrow[i].astype(F32)
        keep(i).start()
    for i in range(7):
        keep(i).wait()


def shards(query, key, value, doc_ids, cross_query, latent_key, latent_value, token_slot,
           slot_image, cross_gate, out_grad):
    vm = pl.BlockSpec(memory_space=pltpu.VMEM)
    sm = pl.BlockSpec(memory_space=pltpu.SMEM)
    hbm = pl.BlockSpec(memory_space=pl.ANY)
    dma = pltpu.SemaphoreType.DMA

    def low(*shape):
        return pltpu.VMEM(shape, BF16)

    def wide(*shape):
        return pltpu.VMEM(shape, F32)

    scratch = [
        low(NC * CH, HD), low(NC * CH, HD), low(CH, HD), low(CH, HD),
        low(NC, CH, HD), low(HD, NC * CH), low(HD, NC * CH),
        wide(CH, CH), low(NC * CH, CH), wide(NC, HD, CH),
        wide(NC, 8, CH), wide(NC, 8, CH), wide(NC, 8, CH), pltpu.VMEM((8, CH), I32),
        wide(HD, CH), wide(HD, CH),
        wide(8, HD), wide(3, 8, HD), wide(8, HD), wide(3, 8, HD),
        low(TD, WD), low(TD, WD), low(2, 2, TD, HD),
        low(IMAGES, LAT, WD), low(IMAGES, LAT, WD),
        low(SLOTS * LAT, WD), low(SLOTS * LAT, WD),
        wide(SLOTS * LAT, WD), wide(SLOTS * LAT, WD), wide(TD, WD),
        low(NX, NX, 2, LAT, 256), low(3, NX, 2, LAT, 256),
        low(NX, 2, LAT, 256), low(NX, 2, LAT, 256),
        low(CH, HD), low(CH, HD), low(2 * CH, HD), low(2 * CH, HD),
        wide(CH, HD), wide(CH, HD), low(2 * CH, HD), low(2 * CH, HD),
        low(CH, HD), low(CH, HD),
        low(TD, WD), low(TD, WD), low(TD, WD), low(TD, WD),
        low(TD, WD), low(TD, WD), wide(LAT, 256), wide(LAT, 256),
        dma((4, 3)), dma((4, 3)),
        dma((2, 2, 4)), dma((2, 2, 4)),
        dma((2, 3)), dma((2, 3)),
        dma((2, 7)), dma((2, 7)),
        dma((3,)), dma((3,)), dma((4,)), dma((4,)),
        dma((2, 2, 4)), dma((2, 2, 4)),
        dma((4, 3)), dma((4, 3)),
        dma((2, 2)), dma((2, 2)), dma((8,)), dma((7,)), pltpu.SemaphoreType.REGULAR((2,)),
    ]
    full = jax.ShapeDtypeStruct((TD, WD), F32)
    half = jax.ShapeDtypeStruct((TD, WD), BF16)
    lat = jax.ShapeDtypeStruct((1, LAT, 256), F32)
    results = pl.pallas_call(
        kernel,
        out_shape=(half,) * 5 + (lat, lat),
        in_specs=[vm, vm, sm, vm] + [hbm] * 7,
        out_specs=(hbm,) * 7,
        scratch_shapes=scratch,
        cost_estimate=pl.CostEstimate(flops=6_500_000_000, bytes_accessed=8_000_000, transcendentals=4_000_000),
        compiler_params=pltpu.CompilerParams(
            collective_id=0, has_side_effects=True, vmem_limit_bytes=58 * 1024 * 1024),
    )(
        doc_ids, token_slot, slot_image, cross_gate,
        query, key, value, cross_query, out_grad, latent_key, latent_value,
    )
    return pl.pallas_call(
        widen,
        out_shape=(half,) + (full,) * 4 + (lat, lat),
        in_specs=[hbm] * 7,
        out_specs=(hbm,) * 7,
        scratch_shapes=[low(5, TD, WD), wide(4, TD, WD), wide(2, 1, LAT, 256), dma((7,)), dma((7,))],
        cost_estimate=pl.CostEstimate(flops=1_000_000, bytes_accessed=5_000_000, transcendentals=0),
    )(*results)


def solution(mesh):
    own = P("seq", "vis")
    lat_in = P("vis", None, None)
    lat_out = P("vis", None, "seq")
    return jax.shard_map(
        shards,
        mesh=mesh,
        in_specs=(own, own, own, P("seq"), own, lat_in, lat_in, P("seq"), P("seq"), P("vis"), own),
        out_specs=(own, own, own, own, own, lat_out, lat_out),
        check_vma=False,
    )
```

```python
import math

import jax
import jax.numpy as jnp
from jax import lax
from jax.experimental import pallas as pl
from jax.experimental.pallas import tpu as pltpu
from jax.sharding import PartitionSpec as P

HD = 128
TD = 320
NX = 4
CH = TD * NX
NC = 3
TILE = 256
NQ = CH // TILE
LAT = 64
SLOTS = 4
IMAGES = 8
WD = 512
SCALE = 1.0 / math.sqrt(HD)
BIG = -1e30
MESH = pl.DeviceIdType.MESH
F32, BF16, I32 = jnp.float32, jnp.bfloat16, jnp.int32

NT = (((1,), (1,)), ((), ()))
NN = (((1,), (0,)), ((), ()))


def dot(a, b, dims=NN):
    return lax.dot_general(a, b, dims, preferred_element_type=F32)


def fold(a, op):
    return op(a.reshape(a.shape[0] // 8, 8, a.shape[1]), axis=0)


LOG2E = 1.4426950408889634

FWD_TILES = (
    tuple((c * TILE, TILE, 0, (c + 1) * TILE) for c in range(NQ)),
    tuple((c * TILE, TILE, 0, CH) for c in range(NQ)),
    tuple((c * TILE, TILE, c * TILE, CH - c * TILE) for c in range(NQ)),
)
BWD_TILES = (FWD_TILES[0], ((0, CH // 2, 0, CH), (CH // 2, CH // 2, 0, CH)), FWD_TILES[2])
ORDER = (0, 1, 3, 2)


def kernel(
    docs_ref, tok_ref, img_ref, gate_ref, q_ref, k_ref, v_ref, cq_ref, do_ref, lk_ref, lv_ref,
    mixed_ref, qg_ref, kg_ref, vg_ref, cqg_ref, lkg_ref, lvg_ref,
    kbuf, vbuf, qbuf, dobuf, dol, kt, vt, sbuf, pbuf, opart, maxes, sums, dsum, starts, dot_t, dqt,
    cown, cx, crow, cz, cqv, dov, stage,
    latk, latv, lks, lvs, gk, gv, cross, latsend, latx, latz, latin,
    obuf, dqb, part_k, part_v, own_k, own_v, got_k, got_v, sum_k, sum_v,
    o_in, dq_in, dk_in, dv_in, mixed, cqg, lkg, lvg,
    a_send, a_recv, z_send, z_recv, c_send, c_recv, l_send, l_recv, gx_send, gx_recv, gz_send, gz_recv,
    p_send, p_recv, b_send, b_recv, f_send, f_recv, own_sem, out_sem, gates,
):
    s = lax.axis_index("seq")
    v = lax.axis_index("vis")
    x = lax.rem(s, NX)
    z = lax.div(s, NX)
    core = lax.rem(v, 2)

    def xpeer(d):
        return lax.rem(x + d, NX)

    def zpeer(d):
        return lax.rem(z + d, NX)

    def remote(src, dst, ssem, rsem, seq, vis):
        return pltpu.make_async_remote_copy(
            src_ref=src, dst_ref=dst, send_sem=ssem, recv_sem=rsem,
            device_id=(seq, vis), device_id_type=MESH,
        )

    def landed(here, rsem):
        remote(here, here, rsem, rsem, s, v).wait_recv()

    def rows(i, n=TD):
        return pl.ds(pl.multiple_of(i * n, n), n)

    def cols(i, n=HD):
        return pl.ds(pl.multiple_of(i * n, n), n)

    def piece(slot, p):
        return pl.ds(pl.multiple_of(slot * CH + p * TD, TD), TD)

    barrier = pltpu.get_barrier_semaphore()

    def greet(seq, vis):
        pl.semaphore_signal(barrier, inc=1, device_id=(seq, vis), device_id_type=MESH)

    def to_seq(j):
        return 2 * v + j % 2

    def to_vis(j):
        return 2 * x + j // 2

    def stays(j):
        return jnp.logical_and(to_seq(j) == s, to_vis(j) == v)

    def from_seq(i):
        return i * NX + lax.div(v, 2)

    from_vis = lax.div(s, 2)

    def from_self(i):
        return jnp.logical_and(from_seq(i) == s, from_vis == v)

    for d in range(1, NX):
        greet(z * NX + xpeer(d), v)
        greet(zpeer(d) * NX + x, v)
    for d in range(1, IMAGES):
        greet(s, lax.rem(v + d, IMAGES))

    for i in range(NX):
        @pl.when(jnp.logical_not(from_self(i)))
        def _():
            greet(from_seq(i), from_vis)

    def own_copy(i):
        src, dst = (
            (k_ref.at[:, cols(x)], kbuf.at[piece(2, x), :]),
            (v_ref.at[:, cols(x)], vbuf.at[piece(2, x), :]),
            (q_ref.at[:, cols(x)], qbuf.at[piece(0, x), :]),
            (do_ref.at[:, cols(x)], dobuf.at[piece(0, x), :]),
            (lk_ref.at[0, :, cols(v, WD)], latk.at[v]),
            (lv_ref.at[0, :, cols(v, WD)], latv.at[v]),
            (cq_ref, cqv),
            (do_ref, dov),
        )[i]
        return pltpu.make_async_copy(src, dst, own_sem.at[i])

    def out_copy(i):
        src, dst = (
            (mixed, mixed_ref), (dq_in, qg_ref), (dk_in, kg_ref), (dv_in, vg_ref), (cqg, cqg_ref),
            (lkg, lkg_ref.at[0]), (lvg, lvg_ref.at[0]),
        )[i]
        return pltpu.make_async_copy(src, dst, out_sem.at[i])

    for i in range(8):
        own_copy(i).start()

    docs = docs_ref[...].reshape(1, TD)
    row_id = lax.broadcasted_iota(I32, (8, HD), 0)
    counts = jnp.zeros((8, HD), F32)
    for d in range(1, 4):
        c = jnp.sum(jnp.where(docs < d, 1.0, 0.0), axis=1, keepdims=True)
        counts = jnp.where(row_id == d, c, counts)
    cown[...] = counts
    pl.semaphore_wait(barrier, 13 + NX - sum(jnp.where(stays(j), 1, 0) for j in range(NX)))

    ins = (k_ref, v_ref, q_ref, do_ref)
    bufs = (kbuf, vbuf, qbuf, dobuf)
    base = (2, 2, 0, 0)

    def a_copy(arr, d):
        p = xpeer(d)
        return remote(ins[arr].at[:, cols(p)], bufs[arr].at[piece(base[arr], x), :],
                      a_send.at[arr, d - 1], a_recv.at[arr, d - 1], z * NX + p, v)

    def a_wait(arr, d):
        landed(bufs[arr].at[piece(base[arr], xpeer(NX - d)), :], a_recv.at[arr, d - 1])

    def c_copy(step, d):
        if step == 0:
            return remote(cown, cx.at[d - 1], c_send.at[0, d - 1], c_recv.at[0, d - 1],
                          z * NX + xpeer(d), v)
        return remote(crow, cz.at[d - 1], c_send.at[1, d - 1], c_recv.at[1, d - 1],
                      zpeer(d) * NX + x, v)

    def z_copy(arr, dz, i):
        p = xpeer(NX - ORDER[i])
        src = ins[arr].at[:, cols(x)] if i == 0 else bufs[arr].at[piece(2, p), :]
        return remote(src, bufs[arr].at[piece(2 - dz, p), :],
                      z_send.at[arr, dz - 1, i], z_recv.at[arr, dz - 1, i], s + dz * NX, v)

    def f_copy(arr, i):
        p = xpeer(NX - ORDER[i])
        src = ins[arr].at[:, cols(x)] if i == 0 else bufs[arr].at[piece(2, p), :]
        return remote(src, stage.at[arr, i], z_send.at[arr, 1, i], f_recv.at[arr, i], s + 3 * NX, v)

    def f_on(arr, i):
        p = xpeer(NX - ORDER[i])
        return remote(stage.at[arr, i], bufs[arr].at[piece(0, p), :],
                      f_send.at[arr, i], z_recv.at[arr, 1, i], s - NX, v)

    def z_start(arr, i):
        @pl.when(z <= 2)
        def _():
            z_copy(arr, 1, i).start()

        if i < 2:
            @pl.when(z == 0)
            def _():
                f_copy(arr, i).start()

            @pl.when(z == 1)
            def _():
                z_copy(arr, 2, i).start()
        else:
            @pl.when(z <= 1)
            def _():
                z_copy(arr, 2, i).start()

    def f_relay(arr):
        @pl.when(z == 3)
        def _():
            for i in range(2):
                landed(stage.at[arr, i], f_recv.at[arr, i])
                f_on(arr, i).start()

    def z_sent(arr):
        for dz in (1, 2):
            @pl.when(z + dz < NX)
            def _():
                for i in range(NX):
                    z_copy(arr, dz, i).wait_send()

    def z_wait(arr, dz):
        for i in range(NX):
            landed(bufs[arr].at[piece(2 - dz, xpeer(NX - ORDER[i])), :], z_recv.at[arr, dz - 1, i])

    def a_start(arr):
        for d in ORDER[1:]:
            a_copy(arr, d).start()

    def a_finish(arr):
        for d in ORDER[1:]:
            a_wait(arr, d)

    def open_gate(n):
        pl.semaphore_signal(gates.at[n], inc=1, device_id=(s, v + 1), device_id_type=MESH)

    @pl.when(core == 0)
    def _():
        for arr in (0, 1):
            z_start(arr, 0)
            a_start(arr)

    @pl.when(core == 1)
    def _():
        for arr in (0, 1):
            z_start(arr, 0)

    for d in ORDER[1:]:
        c_copy(0, d).start()

    lins, lbufs = (lk_ref, lv_ref), (latk, latv)

    def l_copy(arr, d):
        p = lax.rem(v + d, IMAGES)
        return remote(lins[arr].at[0, :, cols(p, WD)], lbufs[arr].at[v],
                      l_send.at[arr, d - 1], l_recv.at[arr, d - 1], s, p)

    for arr in (0, 1):
        for d in range(1, IMAGES):
            l_copy(arr, d).start()

    @pl.when(core == 0)
    def _():
        for arr in (0, 1):
            for i in range(1, NX):
                a_wait(arr, ORDER[i])
                z_start(arr, i)
        open_gate(0)
        open_gate(1)
        a_start(2)
        a_start(3)
        f_relay(0)
        f_relay(1)
        z_sent(0)

    @pl.when(core == 1)
    def _():
        pl.semaphore_wait(gates.at[0], 1)
        for arr in (0, 1):
            a_start(arr)
        for arr in (0, 1):
            a_finish(arr)
        a_start(2)
        a_start(3)
        pl.semaphore_wait(gates.at[1], 1)
        for arr in (0, 1):
            for i in range(1, NX):
                z_start(arr, i)

    for d in ORDER[1:]:
        landed(cx.at[d - 1], c_recv.at[0, d - 1])
    crow[...] = cown[...] + cx[0] + cx[1] + cx[2]
    for d in range(1, NX):
        c_copy(1, d).start()
    for i in range(8):
        own_copy(i).wait()
    for d in range(1, NX):
        landed(cz.at[d - 1], c_recv.at[1, d - 1])
    before = crow[...] + cz[0] + cz[1] + cz[2]
    pos = lax.broadcasted_iota(I32, (8, CH), 1)
    start = jnp.zeros((8, CH), I32)
    for d in range(1, 4):
        b = before[d:d + 1, 0:1].astype(I32)
        start = jnp.where(b <= pos + z * CH, b, start)
    starts[...] = start - (z - 2) * CH

    for slot in range(NC):
        maxes[slot] = jnp.full((8, CH), BIG, F32)
        sums[slot] = jnp.zeros((8, CH), F32)
        opart[slot] = jnp.zeros((HD, CH), F32)

    def forward(slot):
        at = slot * CH
        kt[:, at:at + CH] = kbuf[at:at + CH, :].T
        vt[:, at:at + CH] = vbuf[at:at + CH, :].T
        for k0, kn, q0, qn in FWD_TILES[slot]:
            across = slice(q0, q0 + qn)
            raw = dot(kbuf[at + k0:at + k0 + kn, :], qbuf[across, :], NT)
            kpos = lax.broadcasted_iota(I32, (kn, qn), 0) + (at + k0)
            kept = kpos >= starts[0:1, across]
            if slot == 2:
                kept = kept & (kpos <= lax.broadcasted_iota(I32, (kn, qn), 1) + (at + q0))
            raw = jnp.where(kept, raw, BIG)
            sbuf[k0:k0 + kn, across] = raw
            maxes[slot, :, across] = jnp.maximum(maxes[slot, :, across], fold(raw, jnp.max))
        top = jnp.max(maxes[slot], axis=0, keepdims=True)
        maxes[slot] = jnp.broadcast_to(top, (8, CH))
        for k0, kn, q0, qn in FWD_TILES[slot]:
            across = slice(q0, q0 + qn)
            p = jnp.exp2((sbuf[k0:k0 + kn, across] - top[:, across]) * (SCALE * LOG2E))
            pb = p.astype(BF16)
            pbuf[at + k0:at + k0 + kn, across] = pb
            sums[slot, :, across] += fold(p, jnp.sum)
            opart[slot, :, across] += dot(vt[:, at + k0:at + k0 + kn], pb)

    for arr in (0, 1):
        for d in range(1, IMAGES):
            landed(lbufs[arr].at[lax.rem(v + IMAGES - d, IMAGES)], l_recv.at[arr, d - 1])
    for i in range(SLOTS):
        lks[i * LAT:(i + 1) * LAT, :] = latk[img_ref[i]]
        lvs[i * LAT:(i + 1) * LAT, :] = latv[img_ref[i]]
    slot_of = lax.broadcasted_iota(I32, (SLOTS * LAT, TD), 0) // LAT
    toks = tok_ref[...].reshape(1, TD)
    seen = slot_of == toks
    any_image = toks < SLOTS
    gate = jnp.tanh(gate_ref[...].reshape(1, WD))
    for h in range(NX):
        sl = slice(h * HD, (h + 1) * HD)
        lkh, lvh, cqh = lks[:, sl], lvs[:, sl], cqv[:, sl]
        raw = dot(lkh, cqh, NT)
        raw = jnp.where(seen, raw * SCALE, BIG)
        w = jnp.where(seen, jnp.exp(raw - jnp.max(raw, axis=0, keepdims=True)), 0.0)
        total = jnp.where(any_image, jnp.sum(w, axis=0, keepdims=True), 1.0)
        probs = w / total
        low = probs.astype(BF16)
        cross[:, sl] = gate[:, sl] * dot(lvh.T, low).T
        back = (gate[:, sl] * dov[:, sl].astype(F32)).astype(BF16)
        gp = dot(lvh, back, NT)
        cdot = jnp.sum(probs * gp, axis=0, keepdims=True)
        ds = (probs * (gp - cdot) * SCALE).astype(BF16)
        cqg[:, sl] = dot(lkh.T, ds).T.astype(BF16)
        gk[:, sl] = dot(ds, cqh).astype(BF16).astype(F32)
        gv[:, sl] = dot(low, back).astype(BF16).astype(F32)

    out_copy(4).start()

    for m in range(IMAGES):
        for n, g in enumerate((gk, gv)):
            acc = jnp.zeros((LAT, WD), F32)
            for i in range(SLOTS):
                acc = acc + jnp.where(img_ref[i] == m, 1.0, 0.0) * g[i * LAT:(i + 1) * LAT, :]
            acc = acc.astype(BF16)
            for h in range(2):
                latsend[m // 2, (m % 2) * 2 + h, n] = acc[:, h * 256:(h + 1) * 256]

    def gx_copy(d):
        p = xpeer(d)
        return remote(latsend.at[p], latx.at[d - 1], gx_send.at[d - 1], gx_recv.at[d - 1],
                      z * NX + p, v)

    def gz_copy(j):
        return remote(latz.at[j], latin.at[z], gz_send.at[j], gz_recv.at[z], to_seq(j), to_vis(j))

    for d in ORDER[1:]:
        gx_copy(d).start()

    def row_sum(slot):
        dsum[slot] = jnp.broadcast_to(jnp.sum(dot_t[...] * opart[slot], axis=0, keepdims=True), (8, CH))

    dsum[0] = jnp.zeros((8, CH), F32)
    dsum[1] = jnp.zeros((8, CH), F32)

    @pl.when(core == 1)
    def _():
        f_relay(0)
        f_relay(1)

    a_finish(2)
    forward(2)
    a_finish(3)
    dot_t[...] = dobuf[...].astype(F32).T
    row_sum(2)

    @pl.when(z >= 1)
    def _():
        z_wait(0, 1)
        z_wait(1, 1)
        forward(1)
        row_sum(1)

    @pl.when(z >= 2)
    def _():
        z_wait(0, 2)
        z_wait(1, 2)
        forward(0)
        row_sum(0)

    top = jnp.maximum(jnp.maximum(maxes[0], maxes[1]), maxes[2])
    total = jnp.zeros((1, CH), F32)
    row_dot = jnp.zeros((8, CH), F32)
    for slot in range(NC):
        factor = jnp.exp2((maxes[slot] - top) * (SCALE * LOG2E))
        maxes[slot] = factor
        total = total + jnp.sum(sums[slot], axis=0, keepdims=True) * factor[0:1]
        row_dot = row_dot + dsum[slot] * factor
    inv = 1.0 / total
    row_dot = row_dot * inv
    for slot in range(NC):
        factor = maxes[slot] * inv
        maxes[slot] = factor
        sums[slot] = factor * row_dot
    dqt[...] = jnp.zeros_like(dqt)

    outs = (obuf, dqb, sum_k, sum_v)
    backs = (o_in, dq_in, dk_in, dv_in)

    def b_copy(arr, d):
        p = xpeer(d)
        return remote(outs[arr].at[rows(p), :], backs[arr].at[:, cols(x)],
                      b_send.at[arr, d - 1], b_recv.at[arr, d - 1], z * NX + p, v)

    def b_wait(arr, d):
        landed(backs[arr].at[:, cols(xpeer(NX - d))], b_recv.at[arr, d - 1])

    def b_own(arr):
        backs[arr][:, cols(x)] = outs[arr][rows(x), :]

    parts, gots = (part_k, part_v), (got_k, got_v)

    def p_copy(arr, dz, p):
        return remote(parts[arr].at[pl.ds((2 - dz) * CH + p * TD, TD), :],
                      gots[arr].at[pl.ds((dz - 1) * CH + p * TD, TD), :],
                      p_send.at[arr, dz - 1, p], p_recv.at[arr, dz - 1, p], s - dz * NX, v)

    def r_copy(arr, p):
        return remote(parts[arr].at[pl.ds(p * TD, TD), :], stage.at[arr, p],
                      p_send.at[arr, 1, p], f_recv.at[arr, p], x, v)

    def r_on(arr, p):
        return remote(stage.at[arr, p], gots[arr].at[pl.ds(CH + p * TD, TD), :],
                      f_send.at[arr, p], p_recv.at[arr, 1, p], NX + x, v)

    def p_start(dz, p):
        for arr in (0, 1):
            if dz == 2 and p < 2:
                @pl.when(z == 3)
                def _():
                    r_copy(arr, p).start()

                @pl.when(z == 2)
                def _():
                    p_copy(arr, dz, p).start()
            else:
                p_copy(arr, dz, p).start()

    def backward(slot):
        at = slot * CH
        sent = 0
        dol[slot] = (dot_t[...] * maxes[slot, 0:1, :]).T.astype(BF16)
        for k0, kn, q0, qn in BWD_TILES[slot]:
            down, across = slice(at + k0, at + k0 + kn), slice(q0, q0 + qn)
            pb = pbuf[down, across]
            grad = dol[slot, across, :]
            dp = dot(vbuf[down, :], grad, NT)
            ds = (pb.astype(F32) * (dp - sums[slot, 0:1, across])).astype(BF16)
            dk = dot(ds, qbuf[across, :]) * SCALE
            dv = dot(pb, grad)
            dqt[:, across] += dot(kt[:, down], ds)
            if slot == 2:
                own_k[k0:k0 + kn, :] = dk
                own_v[k0:k0 + kn, :] = dv
            else:
                part_k[down, :] = dk.astype(BF16)
                part_v[down, :] = dv.astype(BF16)
                while (sent + 1) * TD <= k0 + kn:
                    p_start(2 - slot, sent)
                    sent += 1

    @pl.when(z >= 2)
    def _():
        backward(0)

    for d in ORDER[1:]:
        landed(latx.at[d - 1], gx_recv.at[d - 1])
    for j in range(NX):
        for n in range(2):
            acc = latsend[x, j, n].astype(F32)
            for d in range(3):
                acc = acc + latx[d, j, n].astype(F32)
            latz[j, n] = acc.astype(BF16)

        @pl.when(jnp.logical_not(stays(j)))
        def _():
            gz_copy(j).start()

        @pl.when(stays(j))
        def _():
            latin[z] = latz[j]

    @pl.when(z >= 1)
    def _():
        backward(1)

    out = opart[0] * maxes[0, 0:1, :] + opart[1] * maxes[1, 0:1, :] + opart[2] * maxes[2, 0:1, :]
    obuf[...] = out.T.astype(BF16)
    for d in ORDER[1:]:
        b_copy(0, d).start()
    b_own(0)
    backward(2)
    dqb[...] = (dqt[...] * SCALE).T.astype(BF16)
    for d in ORDER[1:]:
        b_copy(1, d).start()
    b_own(1)

    @pl.when(z == 0)
    def _():
        for p in range(2):
            for arr in (0, 1):
                landed(stage.at[arr, p], f_recv.at[arr, p])
                r_on(arr, p).start()

    def p_wait(arr, dz, p):
        here = gots[arr].at[pl.ds((dz - 1) * CH + p * TD, TD), :]
        landed(here, p_recv.at[arr, dz - 1, p])
        return here

    for p in range(NX):
        sl = slice(p * TD, (p + 1) * TD)
        for arr, (own, out_) in enumerate(((own_k, sum_k), (own_v, sum_v))):
            for dz in (2, 1):
                @pl.when(z + dz < NX)
                def _():
                    here = p_wait(arr, dz, p)
                    own[sl, :] += here[...].astype(F32)
            out_[sl, :] = own[sl, :].astype(BF16)

            @pl.when(x != p)
            def _():
                d = lax.rem(p - x + NX, NX)
                remote(out_.at[sl, :], backs[arr + 2].at[:, cols(x)],
                       b_send.at[arr + 2, d - 1], b_recv.at[arr + 2, d - 1], z * NX + p, v).start()

    for d in ORDER[1:]:
        b_wait(0, d)
    mixed[...] = (o_in[...].astype(F32) + cross[...]).astype(BF16)
    out_copy(0).start()

    for i in range(NX):
        @pl.when(jnp.logical_not(from_self(i)))
        def _():
            landed(latin.at[i], gz_recv.at[i])

    for n, g in enumerate((lkg, lvg)):
        acc = latin[0, n].astype(F32)
        for i in range(1, NX):
            acc = acc + latin[i, n].astype(F32)
        g[...] = acc
        out_copy(5 + n).start()
    for d in ORDER[1:]:
        b_wait(1, d)
    out_copy(1).start()

    for arr in (2, 3):
        b_own(arr)
        for d in ORDER[1:]:
            b_wait(arr, d)
        out_copy(arr).start()

    for i in range(7):
        out_copy(i).wait()
    for d in range(1, NX):
        for arr in range(4):
            a_copy(arr, d).wait_send()
            b_copy(arr, d).wait_send()
        for step in range(2):
            c_copy(step, d).wait_send()
        gx_copy(d).wait_send()

    for j in range(NX):
        @pl.when(jnp.logical_not(stays(j)))
        def _():
            gz_copy(j).wait_send()

    @pl.when(core == 1)
    def _():
        z_sent(0)

    z_sent(1)
    for arr in (0, 1):
        for d in range(1, IMAGES):
            l_copy(arr, d).wait_send()
        for dz in (1, 2):
            @pl.when(z >= dz)
            def _():
                for p in range(NX):
                    p_copy(arr, dz, p).wait_send()

        @pl.when(z == 3)
        def _():
            for i in range(2):
                f_on(arr, i).wait_send()

        @pl.when(z == 0)
        def _():
            for p in range(2):
                r_on(arr, p).wait_send()


def widen(*refs):
    ins, outs, (narrow, full, lat, in_sem, out_sem) = refs[:7], refs[7:14], refs[14:]

    def fetch(i):
        dst = narrow.at[i] if i < 5 else lat.at[i - 5]
        return pltpu.make_async_copy(ins[i], dst, in_sem.at[i])

    def keep(i):
        src = narrow.at[0] if i == 0 else full.at[i - 1] if i < 5 else lat.at[i - 5]
        return pltpu.make_async_copy(src, outs[i], out_sem.at[i])

    for i in range(7):
        fetch(i).start()
    for i in range(7):
        fetch(i).wait()
        if 1 <= i <= 4:
            full[i - 1] = narrow[i].astype(F32)
        keep(i).start()
    for i in range(7):
        keep(i).wait()


def shards(query, key, value, doc_ids, cross_query, latent_key, latent_value, token_slot,
           slot_image, cross_gate, out_grad):
    vm = pl.BlockSpec(memory_space=pltpu.VMEM)
    sm = pl.BlockSpec(memory_space=pltpu.SMEM)
    hbm = pl.BlockSpec(memory_space=pl.ANY)
    dma = pltpu.SemaphoreType.DMA

    def low(*shape):
        return pltpu.VMEM(shape, BF16)

    def wide(*shape):
        return pltpu.VMEM(shape, F32)

    scratch = [
        low(NC * CH, HD), low(NC * CH, HD), low(CH, HD), low(CH, HD),
        low(NC, CH, HD), low(HD, NC * CH), low(HD, NC * CH),
        wide(CH, CH), low(NC * CH, CH), wide(NC, HD, CH),
        wide(NC, 8, CH), wide(NC, 8, CH), wide(NC, 8, CH), pltpu.VMEM((8, CH), I32),
        wide(HD, CH), wide(HD, CH),
        wide(8, HD), wide(3, 8, HD), wide(8, HD), wide(3, 8, HD),
        low(TD, WD), low(TD, WD), low(2, 2, TD, HD),
        low(IMAGES, LAT, WD), low(IMAGES, LAT, WD),
        low(SLOTS * LAT, WD), low(SLOTS * LAT, WD),
        wide(SLOTS * LAT, WD), wide(SLOTS * LAT, WD), wide(TD, WD),
        low(NX, NX, 2, LAT, 256), low(3, NX, 2, LAT, 256),
        low(NX, 2, LAT, 256), low(NX, 2, LAT, 256),
        low(CH, HD), low(CH, HD), low(2 * CH, HD), low(2 * CH, HD),
        wide(CH, HD), wide(CH, HD), low(2 * CH, HD), low(2 * CH, HD),
        low(CH, HD), low(CH, HD),
        low(TD, WD), low(TD, WD), low(TD, WD), low(TD, WD),
        low(TD, WD), low(TD, WD), wide(LAT, 256), wide(LAT, 256),
        dma((4, 3)), dma((4, 3)),
        dma((2, 2, 4)), dma((2, 2, 4)),
        dma((2, 3)), dma((2, 3)),
        dma((2, 7)), dma((2, 7)),
        dma((3,)), dma((3,)), dma((4,)), dma((4,)),
        dma((2, 2, 4)), dma((2, 2, 4)),
        dma((4, 3)), dma((4, 3)),
        dma((2, 2)), dma((2, 2)), dma((8,)), dma((7,)), pltpu.SemaphoreType.REGULAR((2,)),
    ]
    full = jax.ShapeDtypeStruct((TD, WD), F32)
    half = jax.ShapeDtypeStruct((TD, WD), BF16)
    lat = jax.ShapeDtypeStruct((1, LAT, 256), F32)
    results = pl.pallas_call(
        kernel,
        out_shape=(half,) * 5 + (lat, lat),
        in_specs=[vm, vm, sm, vm] + [hbm] * 7,
        out_specs=(hbm,) * 7,
        scratch_shapes=scratch,
        cost_estimate=pl.CostEstimate(flops=6_500_000_000, bytes_accessed=8_000_000, transcendentals=4_000_000),
        compiler_params=pltpu.CompilerParams(
            collective_id=0, has_side_effects=True, vmem_limit_bytes=58 * 1024 * 1024),
    )(
        doc_ids, token_slot, slot_image, cross_gate,
        query, key, value, cross_query, out_grad, latent_key, latent_value,
    )
    return pl.pallas_call(
        widen,
        out_shape=(half,) + (full,) * 4 + (lat, lat),
        in_specs=[hbm] * 7,
        out_specs=(hbm,) * 7,
        scratch_shapes=[low(5, TD, WD), wide(4, TD, WD), wide(2, 1, LAT, 256), dma((7,)), dma((7,))],
        cost_estimate=pl.CostEstimate(flops=1_000_000, bytes_accessed=5_000_000, transcendentals=0),
    )(*results)


def solution(mesh):
    own = P("seq", "vis")
    lat_in = P("vis", None, None)
    lat_out = P("vis", None, "seq")
    return jax.shard_map(
        shards,
        mesh=mesh,
        in_specs=(own, own, own, P("seq"), own, lat_in, lat_in, P("seq"), P("seq"), P("vis"), own),
        out_specs=(own, own, own, own, own, lat_out, lat_out),
        check_vma=False,
    )
```
